128 devices in a mesh: growth: 4 (over x), lateral: 32 (over z, y, core).
Axes of the slice: x: 4, y: 4, z: 4, core: 2. Of those that a mesh axis runs over, the one named last changes fastest.
Arguments:
- phase_now: float32 [128, 1024, 128], P('growth', 'lateral'), may hold values from -1 to 1
- phase_old: float32 [128, 1024, 128], P('growth', 'lateral'), may hold values from -1 to 1
- solute: float32 [128, 1024, 128], P('growth', 'lateral'), may hold values from 0.5 to 1.5
- iface_blocks: int32 [4, 32, 6], P('growth', 'lateral'), may hold values from 0 to 7, as said below
- iface_count: int32 [4, 32], P('growth', 'lateral'), may hold values from 1 to 6, as said below
Outputs:
- solute_next: float32 [128, 1024, 128], P('growth', 'lateral')
The draws below stay inside these ranges and needn't reach their ends.
Inputs may be any that keep to these rules, and one draw needn't show every extreme that they name: `iface_blocks`: in each row of a device's list all 6 ids differ; the first iface_count of them name its interface blocks. `iface_count`: the devices at lateral indices 2j and 2j+1 with the same growth index hold at most 8 interface blocks together; in every growth row one such pair holds exactly 8, one device of it 6.
All inputs are finite; a program needn't handle non-finite values.
Results may differ from the reference program's by a relative error of at most 0.00013.
Values sent between devices are 32-bit elements; how exact they have to be, the bound alone decides.
A program may use at most 64 MiB of HBM per device.

```python
import jax
import jax.numpy as jnp
from jax import lax

CX = 32
NY = 128
BZ = 4
NBLK = 8
SLOTS = 6
NZ = 128
NX = 1024
N_GROWTH = 4
N_LATERAL = 32


def draw_iface_count(key, part):
    key = jax.random.fold_in(key, 7)
    key_a, key_b, key_c, key_d = jax.random.split(key, 4)
    pair_count = N_LATERAL // 2
    first_side = jax.random.randint(key_a, (N_GROWTH, pair_count), NBLK // 4, SLOTS + 1)
    spare_room = NBLK - first_side
    second_side = jax.random.randint(key_b, (N_GROWTH, pair_count), 0, 1 << 20) % spare_room + 1
    chosen = jax.random.randint(key_c, (N_GROWTH, 1), 0, pair_count)
    column = jnp.arange(pair_count)[None, :]
    first_side = jnp.where(column == chosen, SLOTS, first_side)
    second_side = jnp.where(column == chosen, NBLK - SLOTS, second_side)
    flipped = jax.random.randint(key_d, (N_GROWTH, pair_count), 0, 2)
    even_side = jnp.where(flipped == 1, second_side, first_side)
    odd_side = jnp.where(flipped == 1, first_side, second_side)
    return jnp.stack([even_side, odd_side], axis=-1).reshape(N_GROWTH, N_LATERAL).astype(jnp.int32)


def draw_iface_blocks(key, part):
    key = jax.random.fold_in(key, 5)
    scores = jax.random.randint(key, (N_GROWTH, N_LATERAL, NBLK), 0, 1 << 20) * NBLK + jnp.arange(NBLK)[None, None, :]
    ordering = jnp.argsort(scores, axis=-1)
    return ordering[..., :SLOTS].astype(jnp.int32)


def level_of(rng, extent, cuts, low, high):
    def one(position, blocks):
        steps = jax.random.uniform(jax.random.fold_in(jax.random.fold_in(rng, 6), position), (blocks,), jnp.float32, low / len(cuts), high / len(cuts))
        return jnp.repeat(jnp.exp(steps), extent[position] // blocks).reshape((-1,) + (1,) * (len(extent) - position - 1))

    factor_of = one(*cuts[0])
    for cut in cuts[1:]:
        factor_of = factor_of * one(*cut)
    return factor_of


def setup_inputs(seed: int = 0) -> dict:
    arg_keys = jax.random.split(jax.random.key(seed), 6)
    phase_now = jnp.clip(jax.random.uniform(arg_keys[0], (NZ, NX, NY), jnp.float32, -1.0, 1.0) * level_of(arg_keys[0], (NZ, NX, NY), ((0, 4), (1, 32)), -0.4, 0.0), -1.0, 1.0)
    phase_old = jnp.clip(jax.random.uniform(arg_keys[1], (NZ, NX, NY), jnp.float32, -1.0, 1.0) * level_of(arg_keys[1], (NZ, NX, NY), ((0, 4), (1, 32)), -0.4, 0.0), -1.0, 1.0)
    solute = jnp.clip(0.5 + 1.0 * jax.random.uniform(arg_keys[2], (NZ, NX, NY), jnp.float32) ** level_of(arg_keys[2], (NZ, NX, NY), ((0, 4), (1, 32)), -0.2, 0.2), 0.5, 1.5)
    iface_blocks = draw_iface_blocks(jax.random.fold_in(arg_keys[5], 71), 0)
    iface_count = draw_iface_count(jax.random.fold_in(arg_keys[5], 71), 0)
    return dict(phase_now=phase_now, phase_old=phase_old, solute=solute, iface_blocks=iface_blocks, iface_count=iface_count)


DIFF_LIQ = 1.0
DIFF_SOL = 0.1
LATERAL_RATE = 0.1
VERTICAL_RATE = 400.0
TRAPPING = 0.5
PARTITION = 0.3
ANISOTROPY = 0.3
REGULAR = 0.25

def diffusivity(phase_values):
    return DIFF_LIQ * (1.0 - phase_values) * 0.5 + DIFF_SOL * (1.0 + phase_values) * 0.5

def interface_flux(grad_x, grad_y, grad_z, change, solute):
    norm_sq = grad_x * grad_x + grad_y * grad_y + grad_z * grad_z + REGULAR
    quartic = grad_x * grad_x * grad_x * grad_x + grad_y * grad_y * grad_y * grad_y + grad_z * grad_z * grad_z * grad_z
    anisotropic = 1.0 + ANISOTROPY * (4.0 * quartic / (norm_sq * norm_sq) - 3.0)
    strength = TRAPPING * (1.0 + (1.0 - PARTITION) * solute) * change * anisotropic / jnp.sqrt(norm_sq)
    return (strength * grad_x, strength * grad_y, strength * grad_z)

def reference(phase_now, phase_old, solute, iface_blocks, iface_count):
    phase_pad = jnp.pad(phase_now, 1)
    solute_pad = jnp.pad(solute, 1)
    diff_pad = diffusivity(phase_pad)
    centre = diff_pad[1:-1, 1:-1, 1:-1]
    lateral = (centre + diff_pad[1:-1, 2:, 1:-1]) * 0.5 * (solute_pad[1:-1, 2:, 1:-1] - solute)
    lateral = lateral + (centre + diff_pad[1:-1, :-2, 1:-1]) * 0.5 * (solute_pad[1:-1, :-2, 1:-1] - solute)
    lateral = lateral + (centre + diff_pad[1:-1, 1:-1, 2:]) * 0.5 * (solute_pad[1:-1, 1:-1, 2:] - solute)
    lateral = lateral + (centre + diff_pad[1:-1, 1:-1, :-2]) * 0.5 * (solute_pad[1:-1, 1:-1, :-2] - solute)
    lateral = LATERAL_RATE * lateral
    grad_x = (phase_pad[1:-1, 2:, 1:-1] - phase_pad[1:-1, :-2, 1:-1]) * 0.5
    grad_y = (phase_pad[1:-1, 1:-1, 2:] - phase_pad[1:-1, 1:-1, :-2]) * 0.5
    grad_z = (phase_pad[2:, 1:-1, 1:-1] - phase_pad[:-2, 1:-1, 1:-1]) * 0.5
    flux_x, flux_y, flux_z = interface_flux(grad_x, grad_y, grad_z, phase_now - phase_old, solute)
    slot_index = jnp.arange(SLOTS, dtype=jnp.int32)
    live_mask = slot_index[None, None, :] < iface_count[:, :, None]
    matches = (iface_blocks[:, :, :, None] == jnp.arange(NBLK, dtype=jnp.int32)[None, None, None, :]) & live_mask[:, :, :, None]
    block_mask = jnp.any(matches, axis=2).astype(jnp.float32)
    block_mask = jnp.transpose(block_mask, (0, 2, 1)).reshape(N_GROWTH * NBLK, 1, N_LATERAL, 1, 1)
    cell_shape = (N_GROWTH * NBLK, BZ, N_LATERAL, CX, NY)
    flux_x = (flux_x.reshape(cell_shape) * block_mask).reshape(phase_now.shape)
    flux_y = (flux_y.reshape(cell_shape) * block_mask).reshape(phase_now.shape)
    flux_z = (flux_z.reshape(cell_shape) * block_mask).reshape(phase_now.shape)
    pad_x = jnp.pad(flux_x, 1)
    pad_y = jnp.pad(flux_y, 1)
    pad_z = jnp.pad(flux_z, 1)
    source = (pad_x[1:-1, 2:, 1:-1] - pad_x[1:-1, :-2, 1:-1] + (pad_y[1:-1, 1:-1, 2:] - pad_y[1:-1, 1:-1, :-2]) + (pad_z[2:, 1:-1, 1:-1] - pad_z[:-2, 1:-1, 1:-1])) * 0.5
    rhs = solute + lateral + source
    lower_face = VERTICAL_RATE * (centre + diff_pad[:-2, 1:-1, 1:-1]) * 0.5
    upper_face = VERTICAL_RATE * (centre + diff_pad[2:, 1:-1, 1:-1]) * 0.5
    diagonal = 1.0 + lower_face + upper_face
    row_index = jnp.arange(phase_now.shape[0], dtype=jnp.int32)[:, None, None]
    below_coef = jnp.where(row_index == 0, 0.0, -lower_face)
    above_coef = jnp.where(row_index == phase_now.shape[0] - 1, 0.0, -upper_face)
    result = lax.linalg.tridiagonal_solve(jnp.transpose(below_coef, (1, 2, 0)), jnp.transpose(diagonal, (1, 2, 0)), jnp.transpose(above_coef, (1, 2, 0)), jnp.transpose(rhs, (1, 2, 0))[..., None])[..., 0]
    return jnp.transpose(result, (2, 0, 1))
```

```python
import jax
import jax.numpy as jnp
from jax import lax
from jax.experimental import pallas as pl
from jax.experimental.pallas import tpu as pltpu
from jax.sharding import PartitionSpec as P

BZ = 4
MESH = pl.DeviceIdType.MESH
NG = 4
NL = 32
CZ = 32
CX = 32
NY = 128
PAD = 8
ROW = CX + 2 * PAD
F32 = jnp.float32


def flux_factor(gx, gy, gz, pre):
    x2 = gx * gx
    y2 = gy * gy
    z2 = gz * gz
    inv = lax.rsqrt(x2 + y2 + z2 + 1.0)
    inv2 = inv * inv
    quartic = x2 * x2 + y2 * y2 + z2 * z2
    return pre * inv * (0.1 + 1.2 * quartic * (inv2 * inv2))


def next_y(a, last):
    return jnp.where(last, 0.0, pltpu.roll(a, NY - 1, 1))


def prev_y(a, first):
    return jnp.where(first, 0.0, pltpu.roll(a, 1, 1))


def kernel(
    phase, old, solute, blocks, count, out,
    ph, so, po, s0, fx, fz, rh, ee, wf, pf, vb, dd, pp, qq, col,
    xs, xr, zs, zr, cs, cr, sts, str_, pvs, pvr, blk, cnt,
    in_sem, x_ss, x_rs, z_ss, z_rs, c_ss, c_rs, st_ss, st_rs, pv_ss, pv_rs,
):
    g = lax.axis_index("growth")
    l = lax.axis_index("lateral")
    has_lo, has_hi = g > 0, g < NG - 1
    has_xl, has_xr = l > 0, l < NL - 1
    g_lo, g_hi = jnp.maximum(g - 1, 0), jnp.minimum(g + 1, NG - 1)
    l_lo, l_hi = jnp.maximum(l - 1, 0), jnp.minimum(l + 1, NL - 1)
    others = [lax.rem(g + d, NG) for d in range(1, NG)]

    barrier = pltpu.get_barrier_semaphore()

    def greet(cond, dev):
        @pl.when(cond)
        def _():
            pl.semaphore_signal(barrier, inc=1, device_id=dev, device_id_type=MESH)

    diag = [
        (has_lo & has_xl, (g_lo, l_lo)),
        (has_lo & has_xr, (g_lo, l_hi)),
        (has_hi & has_xl, (g_hi, l_lo)),
        (has_hi & has_xr, (g_hi, l_hi)),
    ]
    greet(has_xl, (g, l_lo))
    greet(has_xr, (g, l_hi))
    for cond, dev in diag:
        greet(cond, dev)
    for o in others:
        pl.semaphore_signal(barrier, inc=1, device_id=(o, l), device_id_type=MESH)

    ins = [
        pltpu.make_async_copy(phase, ph.at[pl.ds(1, CZ), pl.ds(PAD, CX), :], in_sem.at[0]),
        pltpu.make_async_copy(old, po, in_sem.at[1]),
        pltpu.make_async_copy(solute, so.at[:, pl.ds(PAD, CX), :], in_sem.at[2]),
        pltpu.make_async_copy(blocks, blk, in_sem.at[3]),
        pltpu.make_async_copy(count, cnt, in_sem.at[4]),
    ]
    for c in ins:
        c.start()

    lane = lax.broadcasted_iota(jnp.int32, (CX, NY), 1)
    first, last = lane == 0, lane == NY - 1
    zero = jnp.zeros((CX, NY), F32)

    def face(a, b):
        return 220.0 - 90.0 * (a + b)

    def phz(z, off=0):
        return ph[z + 1, pl.ds(PAD + off, CX), :]

    def soz(z, off=0):
        return so[z, pl.ds(PAD + off, CX), :]

    ins[0].wait()
    bottom = jnp.where(g == 0, face(phz(0), 0.0), zero) + 1.0
    top = jnp.where(g == NG - 1, face(phz(CZ - 1), 0.0), zero) + 1.0
    ee[0] = bottom
    pf[0] = zero + 1.0

    def up(i, carry):
        e, prod = carry
        u = face(phz(i), phz(i + 1))
        w = u / (u + e)
        e = 1.0 + w * e
        prod = prod * w
        wf[i] = w
        ee[i + 1] = e
        pf[i + 1] = prod
        return e, prod

    e_top, prod_top = lax.fori_loop(0, CZ - 1, up, (bottom, zero + 1.0))

    def finish(i, e, prod):
        d = 1.0 / (ee[i] + e - 1.0)
        dd[i] = d
        pp[i] = pf[i] * d
        qq[i] = prod * d

    def down(j, carry):
        i = CZ - 1 - j
        e, prod = carry
        finish(i, e, prod)
        u = face(phz(i), phz(i - 1))
        v = u / (u + e)
        vb[i] = v
        return 1.0 + v * e, prod * v

    e_bot, prod_bot = lax.fori_loop(0, CZ - 1, down, (top, zero + 1.0))
    finish(0, e_bot, prod_bot)

    for c in ins[1:]:
        c.wait()

    def prefactor(k, _):
        hit = jnp.int32(0)
        for s in range(6):
            hit = hit | jnp.where((blk[0, 0, s] == k) & (s < cnt[0, 0]), 1, 0)
        mask = hit.astype(F32) * 0.25
        for r in range(BZ):
            z = k * BZ + r
            s0[z] = (1.0 + 0.7 * soz(z)) * (phz(z) - po[z]) * mask
        return 0

    lax.fori_loop(0, CZ // BZ, prefactor, 0)

    for side, x in ((0, 0), (1, CX - 1)):
        inner = 1 if x == 0 else CX - 2
        xs[side, 0] = ph[1:CZ + 1, PAD + x, :]
        xs[side, 1] = ph[1:CZ + 1, PAD + inner, :]
        xs[side, 2] = so[:, PAD + x, :]
        xs[side, 3] = s0[:, x, :]
    for side, z in ((0, 0), (1, CZ - 1)):
        zs[side, 0] = phz(z)
        zs[side, 1] = phz(1 if z == 0 else CZ - 2)
        zs[side, 2] = s0[z]
        zs[side, 3] = pp[0] if z == 0 else qq[CZ - 1]
        cs[2 * side] = phz(z)[0:8]
        cs[2 * side + 1] = phz(z)[CX - 8:CX]

    pl.semaphore_wait(
        barrier,
        NG - 1
        + has_xl.astype(jnp.int32) * (1 + has_lo.astype(jnp.int32) + has_hi.astype(jnp.int32))
        + has_xr.astype(jnp.int32) * (1 + has_lo.astype(jnp.int32) + has_hi.astype(jnp.int32)),
    )

    def remote(src, dst, ss, rs, dev):
        return pltpu.make_async_remote_copy(
            src_ref=src, dst_ref=dst, send_sem=ss, recv_sem=rs, device_id=dev, device_id_type=MESH
        )

    x_out = [
        (has_xl, remote(xs.at[0], xr.at[1], x_ss.at[0], x_rs.at[1], (g, l_lo))),
        (has_xr, remote(xs.at[1], xr.at[0], x_ss.at[1], x_rs.at[0], (g, l_hi))),
    ]
    z_out = [
        (has_lo, remote(zs.at[0], zr.at[1], z_ss.at[0], z_rs.at[1], (g_lo, l))),
        (has_hi, remote(zs.at[1], zr.at[0], z_ss.at[1], z_rs.at[0], (g_hi, l))),
    ]
    c_out = [
        (cond, remote(cs.at[i], cr.at[3 - i], c_ss.at[i], c_rs.at[3 - i], dev))
        for i, (cond, dev) in enumerate(diag)
    ]
    for cond, cp in x_out + c_out + z_out:
        pl.when(cond)(cp.start)

    x_in = [
        (has_xl, remote(xs.at[1], xr.at[0], x_ss.at[1], x_rs.at[0], (g, l_lo))),
        (has_xr, remote(xs.at[0], xr.at[1], x_ss.at[0], x_rs.at[1], (g, l_hi))),
    ]
    z_in = [
        (has_lo, remote(zs.at[1], zr.at[0], z_ss.at[1], z_rs.at[0], (g_lo, l))),
        (has_hi, remote(zs.at[0], zr.at[1], z_ss.at[0], z_rs.at[1], (g_hi, l))),
    ]
    c_in = [
        (cond, remote(cs.at[3 - i], cr.at[i], c_ss.at[3 - i], c_rs.at[i], dev))
        for i, (cond, dev) in enumerate(diag)
    ]

    for side, here in ((0, has_xl), (1, has_xr)):
        @pl.when(jnp.logical_not(here))
        def _():
            xr[side] = jnp.zeros((4, CZ, NY), F32)
    for side, here in ((0, has_lo), (1, has_hi)):
        @pl.when(jnp.logical_not(here))
        def _():
            zr[side] = jnp.zeros((4, CX, NY), F32)
    for i, (cond, _) in enumerate(diag):
        @pl.when(jnp.logical_not(cond))
        def _():
            cr[i] = jnp.zeros((8, NY), F32)

    for cond, cp in z_in:
        pl.when(cond)(cp.wait_recv)
    sts[0] = 1.0 / face(phz(CZ - 1), zr[1, 0]) + qq[CZ - 1] + zr[1, 3]
    sts[1] = pp[CZ - 1]
    str_[g] = sts[...]

    st_out = [remote(sts, str_.at[g], st_ss.at[d], st_rs.at[g], (o, l)) for d, o in enumerate(others)]
    for cp in st_out:
        cp.start()

    for cond, cp in x_in + c_in:
        pl.when(cond)(cp.wait_recv)

    ph[0, pl.ds(PAD, CX), :] = zr[0, 0]
    ph[CZ + 1, pl.ds(PAD, CX), :] = zr[1, 0]
    for side, x in ((0, -1), (1, CX)):
        ph[1:CZ + 1, PAD + x, :] = xr[side, 0]
        so[:, PAD + x, :] = xr[side, 2]
        row_lo = cr[side][7:8] if side == 0 else cr[side][0:1]
        row_hi = cr[2 + side][7:8] if side == 0 else cr[2 + side][0:1]
        ph[0, PAD + x:PAD + x + 1, :] = row_lo
        ph[CZ + 1, PAD + x:PAD + x + 1, :] = row_hi
        col[side, 7:8, :] = row_lo
        col[side, 8:40, :] = xr[side, 0]
        col[side, 40:41, :] = row_hi

    def ydiff(a):
        return next_y(a, last) - prev_y(a, first)

    for side, x in ((0, -1), (1, CX)):
        here = xr[side, 0]
        if side == 0:
            gx = ph[1:CZ + 1, PAD, :] - xr[side, 1]
        else:
            gx = xr[side, 1] - ph[1:CZ + 1, PAD + CX - 1, :]
        gz = col[side, 9:41, :] - col[side, 7:39, :]
        fx[:, PAD + x, :] = flux_factor(gx, ydiff(here), gz, xr[side, 3]) * gx
    for side, z in ((0, -1), (1, CZ)):
        here = zr[side, 0]
        gz = phz(0) - zr[side, 1] if side == 0 else zr[side, 1] - phz(CZ - 1)
        gx = phz(z, 1) - phz(z, -1)
        fz[z + 1] = flux_factor(gx, ydiff(here), gz, zr[side, 2]) * gz

    def coupling(a, b):
        return 0.055 - 0.0225 * (a + b)

    def cells(k, _):
        for r in range(BZ):
            z = k * BZ + r
            here = phz(z)
            right, left = phz(z, 1), phz(z, -1)
            yn, yp = next_y(here, last), prev_y(here, first)
            gx = right - left
            gy = yn - yp
            gz = phz(z + 1) - phz(z - 1)
            factor = flux_factor(gx, gy, gz, s0[z])
            fx[z, pl.ds(PAD, CX), :] = factor * gx
            fz[z + 1] = factor * gz
            flux_y = factor * gy
            s = soz(z)
            side = coupling(here, right) * (soz(z, 1) - s) + coupling(here, left) * (soz(z, -1) - s)
            side = side + coupling(here, yn) * (next_y(s, last) - s)
            side = side + coupling(here, yp) * (prev_y(s, first) - s)
            rh[z] = s + side + ydiff(flux_y)
        return 0

    lax.fori_loop(0, CZ // BZ, cells, 0)

    def rhs(k, _):
        for r in range(BZ):
            z = k * BZ + r
            rh[z] = (
                rh[z]
                + (fx[z, pl.ds(PAD + 1, CX), :] - fx[z, pl.ds(PAD - 1, CX), :])
                + (fz[z + 2] - fz[z])
            )
        return 0

    lax.fori_loop(0, CZ // BZ, rhs, 0)

    ee[0] = rh[0]

    def sweep_up(i, f):
        f = rh[i] + wf[i - 1] * f
        ee[i] = f
        return f

    f_top = lax.fori_loop(1, CZ, sweep_up, rh[0])

    def sweep_down(j, b):
        i = CZ - 1 - j
        r = rh[i]
        b = b + r
        ee[i] = (ee[i] + b - r) * dd[i]
        return b * vb[i]

    b_bot = lax.fori_loop(0, CZ - 1, sweep_down, zero) + rh[0]
    ee[0] = b_bot * dd[0]

    pvs[0] = ee[0]
    pvs[1] = ee[CZ - 1]
    pvr[g] = pvs[...]
    pv_out = [remote(pvs, pvr.at[g], pv_ss.at[d], pv_rs.at[g], (o, l)) for d, o in enumerate(others)]
    for cp in pv_out:
        cp.start()

    def arrive(src, dst, ss, rs):
        for o in others:
            remote(src, dst.at[o], ss.at[0], rs.at[o], (o, l)).wait_recv()

    arrive(sts, str_, st_ss, st_rs)
    m0 = 1.0 / str_[0, 0]
    t1, t2 = str_[1, 1], str_[2, 1]
    k1 = t1 * m0
    m1 = 1.0 / (str_[1, 0] - t1 * k1)
    k2 = t2 * m1
    m2 = 1.0 / (str_[2, 0] - t2 * k2)
    arrive(pvs, pvr, pv_ss, pv_rs)
    b0 = pvr[0, 1] - pvr[1, 0]
    b1 = pvr[1, 1] - pvr[2, 0] + k1 * b0
    b2 = pvr[2, 1] - pvr[3, 0] + k2 * b1
    q2 = b2 * m2
    q1 = b1 * m1 + k2 * q2
    q0 = b0 * m0 + k1 * q1
    below = jnp.where(g == 1, q0, jnp.where(g == 2, q1, jnp.where(g == 3, q2, 0.0)))
    above = jnp.where(g == 0, q0, jnp.where(g == 1, q1, jnp.where(g == 2, q2, 0.0)))

    def close(k, _):
        for r in range(BZ):
            z = k * BZ + r
            out[z] = ee[z] + pp[z] * below - qq[z] * above
        return 0

    lax.fori_loop(0, CZ // BZ, close, 0)

    for cond, cp in x_out + z_out + c_out:
        pl.when(cond)(cp.wait_send)
    for cp in st_out + pv_out:
        cp.wait_send()


def step(phase, old, solute, blocks, count):
    slab = pltpu.VMEM((CZ, CX, NY), F32)
    dma = pltpu.SemaphoreType.DMA
    return pl.pallas_call(
        kernel,
        out_shape=jax.ShapeDtypeStruct((CZ, CX, NY), F32),
        in_specs=[pl.BlockSpec(memory_space=pl.ANY)] * 5,
        out_specs=pl.BlockSpec(memory_space=pltpu.VMEM),
        scratch_shapes=[
            pltpu.VMEM((CZ + 2, ROW, NY), F32),
            pltpu.VMEM((CZ, ROW, NY), F32),
            slab,
            slab,
            pltpu.VMEM((CZ, ROW, NY), F32),
            pltpu.VMEM((CZ + 2, CX, NY), F32),
            slab, slab, slab, slab, slab, slab, slab, slab,
            pltpu.VMEM((2, ROW, NY), F32),
            pltpu.VMEM((2, 4, CZ, NY), F32),
            pltpu.VMEM((2, 4, CZ, NY), F32),
            pltpu.VMEM((2, 4, CX, NY), F32),
            pltpu.VMEM((2, 4, CX, NY), F32),
            pltpu.VMEM((4, 8, NY), F32),
            pltpu.VMEM((4, 8, NY), F32),
            pltpu.VMEM((2, CX, NY), F32),
            pltpu.VMEM((NG, 2, CX, NY), F32),
            pltpu.VMEM((2, CX, NY), F32),
            pltpu.VMEM((NG, 2, CX, NY), F32),
            pltpu.SMEM((1, 1, 6), jnp.int32),
            pltpu.SMEM((1, 1), jnp.int32),
            dma((5,)),
            dma((2,)), dma((2,)),
            dma((2,)), dma((2,)),
            dma((4,)), dma((4,)),
            dma((3,)), dma((NG,)),
            dma((3,)), dma((NG,)),
        ],
        compiler_params=pltpu.CompilerParams(
            collective_id=0, has_side_effects=True, vmem_limit_bytes=32 * 1024 * 1024
        ),
    )(phase, old, solute, blocks, count)


def solution(mesh):
    spec = P("growth", "lateral", None)
    return jax.shard_map(
        step,
        mesh=mesh,
        in_specs=(spec, spec, spec, spec, P("growth", "lateral")),
        out_specs=spec,
        check_vma=False,
    )
```

```python
import jax
import jax.numpy as jnp
from jax import lax
from jax.experimental import pallas as pl
from jax.experimental.pallas import tpu as pltpu
from jax.sharding import PartitionSpec as P

BZ = 4
MESH = pl.DeviceIdType.MESH
NG = 4
NL = 32
CZ = 32
CX = 32
NY = 128
PAD = 8
ROW = CX + 2 * PAD
F32 = jnp.float32


def flux_factor(gx, gy, gz, pre):
    x2 = gx * gx
    y2 = gy * gy
    z2 = gz * gz
    inv = lax.rsqrt(x2 + y2 + z2 + 1.0)
    inv2 = inv * inv
    quartic = x2 * x2 + y2 * y2 + z2 * z2
    return pre * inv * (0.1 + 1.2 * quartic * (inv2 * inv2))


def next_y(a, last):
    return jnp.where(last, 0.0, pltpu.roll(a, NY - 1, 1))


def prev_y(a, first):
    return jnp.where(first, 0.0, pltpu.roll(a, 1, 1))


def kernel(
    phase, old, solute, blocks, count, out,
    ph, so, po, s0, fx, fz, rh, ee, bb, wf, pf, vb, qf, dd, pp, qq, ea, eb,
    cin, cnx, cout, cs0, cgy, cgz, cfa, cfz, cpq,
    xs, xr, zs, zr, cs, cr, gs, gr, pvs, pvr, es, er, blk, cnt,
    in_sem, x_ss, x_rs, z_ss, z_rs, c_ss, c_rs, g_ss, g_rs, pv_ss, pv_rs, e_ss, e_rs,
):
    g = lax.axis_index("growth")
    l = lax.axis_index("lateral")
    has_lo, has_hi = g > 0, g < NG - 1
    has_xl, has_xr = l > 0, l < NL - 1
    g_lo, g_hi = jnp.maximum(g - 1, 0), jnp.minimum(g + 1, NG - 1)
    l_lo, l_hi = jnp.maximum(l - 1, 0), jnp.minimum(l + 1, NL - 1)
    others = [lax.rem(g + d, NG) for d in range(1, NG)]

    barrier = pltpu.get_barrier_semaphore()

    def greet(cond, dev):
        @pl.when(cond)
        def _():
            pl.semaphore_signal(barrier, inc=1, device_id=dev, device_id_type=MESH)

    diag = [
        (has_lo & has_xl, (g_lo, l_lo)),
        (has_lo & has_xr, (g_lo, l_hi)),
        (has_hi & has_xl, (g_hi, l_lo)),
        (has_hi & has_xr, (g_hi, l_hi)),
    ]
    greet(has_xl, (g, l_lo))
    greet(has_xr, (g, l_hi))
    for cond, dev in diag:
        greet(cond, dev)
    for o in others:
        pl.semaphore_signal(barrier, inc=1, device_id=(o, l), device_id_type=MESH)

    ins = [
        pltpu.make_async_copy(phase, ph.at[pl.ds(1, CZ), pl.ds(PAD, CX), :], in_sem.at[0]),
        pltpu.make_async_copy(old, po, in_sem.at[1]),
        pltpu.make_async_copy(solute, so.at[:, pl.ds(PAD, CX), :], in_sem.at[2]),
        pltpu.make_async_copy(blocks, blk, in_sem.at[3]),
        pltpu.make_async_copy(count, cnt, in_sem.at[4]),
    ]
    for c in ins:
        c.start()

    lane = lax.broadcasted_iota(jnp.int32, (CX, NY), 1)
    row = lax.broadcasted_iota(jnp.int32, (CX, NY), 0)
    first, last = lane == 0, lane == NY - 1
    inner = (row > 0) & (row < CX - 1)
    zero = jnp.zeros((CX, NY), F32)
    one = zero + 1.0
    EXT = 40
    lane_e = lax.broadcasted_iota(jnp.int32, (EXT, NY), 1)
    first_e, last_e = lane_e == 0, lane_e == NY - 1

    def face(a, b):
        return 220.0 - 90.0 * (a + b)

    def coupling(a, b):
        return 0.055 - 0.0225 * (a + b)

    def ydiff(a):
        return next_y(a, last) - prev_y(a, first)

    def phz(z, off=0):
        return ph[z + 1, pl.ds(PAD + off, CX), :]

    def soz(z, off=0):
        return so[z, pl.ds(PAD + off, CX), :]

    for side, x in ((0, -1), (1, CX)):
        ph[0:CZ, PAD + x, :] = zero
        ph[CZ:CZ + 2, PAD + x, :] = zero[0:2]
        fx[:, PAD + x, :] = zero
        for buf in (cin, cnx, cout, cs0):
            buf[side, 0:8] = zero[0:8]
            buf[side, 40:56] = zero[0:16]
        @pl.when(jnp.logical_not((has_xl, has_xr)[side]))
        def _():
            xr[side] = jnp.zeros((4, CZ, NY), F32)
        @pl.when(jnp.logical_not((has_lo, has_hi)[side]))
        def _():
            zr[side] = jnp.zeros((3, CX, NY), F32)
    for i, (cond, _) in enumerate(diag):
        @pl.when(jnp.logical_not(cond))
        def _():
            cr[i] = jnp.zeros((8, NY), F32)

    for c in ins:
        c.wait()

    def prefactor(k, _):
        hit = jnp.int32(0)
        for s in range(6):
            hit = hit | jnp.where((blk[0, 0, s] == k) & (s < cnt[0, 0]), 1, 0)
        mask = hit.astype(F32) * 0.25
        for r in range(BZ):
            z = k * BZ + r
            s0[z] = (1.0 + 0.7 * soz(z)) * (phz(z) - po[z]) * mask
        return 0

    lax.fori_loop(0, CZ // BZ, prefactor, 0)

    for side, x in ((0, 0), (1, CX - 1)):
        near = 1 if x == 0 else CX - 2
        xs[side, 0] = ph[1:CZ + 1, PAD + x, :]
        xs[side, 1] = ph[1:CZ + 1, PAD + near, :]
        edge = so[:, PAD + x, :]
        xs[side, 2] = edge
        so[:, PAD + (-1 if side == 0 else CX), :] = edge
        xs[side, 3] = s0[:, x, :]
    for side, z in ((0, 0), (1, CZ - 1)):
        zs[side, 0] = phz(z)
        zs[side, 1] = phz(1 if z == 0 else CZ - 2)
        zs[side, 2] = s0[z]
        cs[2 * side] = phz(z)[0:8]
        cs[2 * side + 1] = phz(z)[CX - 8:CX]

    bottom = jnp.where(g == 0, face(phz(0), 0.0), zero) + 1.0
    top = jnp.where(g == NG - 1, face(phz(CZ - 1), 0.0), zero) + 1.0
    ea[0] = bottom
    pf[0] = one
    eb[CZ - 1] = top
    qf[CZ - 1] = one

    def eliminate(i, carry):
        e, prod, ebar, qprod = carry
        j = CZ - 1 - i
        u = face(phz(i), phz(i + 1))
        v = face(phz(j), phz(j - 1))
        w = u / (u + e)
        y = v / (v + ebar)
        e = 1.0 + w * e
        ebar = 1.0 + y * ebar
        prod = prod * w
        qprod = qprod * y
        wf[i] = w
        vb[j] = y
        ea[i + 1] = e
        eb[j - 1] = ebar
        pf[i + 1] = prod
        qf[j - 1] = qprod
        return e, prod, ebar, qprod

    def eliminate3(k, carry):
        for r in range(3):
            carry = eliminate(1 + 3 * k + r, carry)
        return carry

    lax.fori_loop(0, 10, eliminate3, eliminate(0, (bottom, one, top, one)))

    def finish(k, _):
        for r in range(BZ):
            i = k * BZ + r
            d = 1.0 / (ea[i] + eb[i] - 1.0)
            dd[i] = d
            pp[i] = pf[i] * d
            qq[i] = qf[i] * d
        return 0

    lax.fori_loop(0, CZ // BZ, finish, 0)
    gs[0] = pp[0]
    gs[1] = qq[CZ - 1]
    gs[2] = pp[CZ - 1]
    gs[3] = phz(0)
    gs[4] = phz(CZ - 1)
    gr[g] = gs[...]

    both = has_lo.astype(jnp.int32) + has_hi.astype(jnp.int32) + 1
    pl.semaphore_wait(
        barrier, NG - 1 + (has_xl.astype(jnp.int32) + has_xr.astype(jnp.int32)) * both
    )

    def remote(src, dst, ss, rs, dev):
        return pltpu.make_async_remote_copy(
            src_ref=src, dst_ref=dst, send_sem=ss, recv_sem=rs, device_id=dev, device_id_type=MESH
        )

    x_out = [
        (has_xl, remote(xs.at[0], xr.at[1], x_ss.at[0], x_rs.at[1], (g, l_lo))),
        (has_xr, remote(xs.at[1], xr.at[0], x_ss.at[1], x_rs.at[0], (g, l_hi))),
    ]
    z_out = [
        (has_lo, remote(zs.at[0], zr.at[1], z_ss.at[0], z_rs.at[1], (g_lo, l))),
        (has_hi, remote(zs.at[1], zr.at[0], z_ss.at[1], z_rs.at[0], (g_hi, l))),
    ]
    c_out = [
        (cond, remote(cs.at[i], cr.at[3 - i], c_ss.at[i], c_rs.at[3 - i], dev))
        for i, (cond, dev) in enumerate(diag)
    ]
    for cond, cp in x_out + z_out + c_out:
        pl.when(cond)(cp.start)
    x_in = [
        (has_xl, remote(xs.at[1], xr.at[0], x_ss.at[1], x_rs.at[0], (g, l_lo))),
        (has_xr, remote(xs.at[0], xr.at[1], x_ss.at[0], x_rs.at[1], (g, l_hi))),
    ]
    z_in = [
        (has_lo, remote(zs.at[1], zr.at[0], z_ss.at[1], z_rs.at[0], (g_lo, l))),
        (has_hi, remote(zs.at[0], zr.at[1], z_ss.at[0], z_rs.at[1], (g_hi, l))),
    ]
    c_in = [
        (cond, remote(cs.at[3 - i], cr.at[i], c_ss.at[3 - i], c_rs.at[i], dev))
        for i, (cond, dev) in enumerate(diag)
    ]

    def spread(src, dst, ss, rs):
        cps = [remote(src, dst.at[g], ss.at[d], rs.at[g], (o, l)) for d, o in enumerate(others)]
        for cp in cps:
            cp.start()
        return cps

    def arrive(src, dst, ss, rs):
        for o in others:
            remote(src, dst.at[o], ss.at[0], rs.at[o], (o, l)).wait_recv()

    def plane(z):
        here = phz(z)
        right, left = phz(z, 1), phz(z, -1)
        yn, yp = next_y(here, last), prev_y(here, first)
        gx = right - left
        gy = yn - yp
        gz = phz(z + 1) - phz(z - 1)
        factor = flux_factor(gx, gy, gz, jnp.where(inner, s0[z], 0.0))
        fx[z, pl.ds(PAD, CX), :] = factor * gx
        fz[z + 1] = factor * gz
        flux_y = factor * gy
        s = soz(z)
        side = coupling(here, right) * (soz(z, 1) - s) + coupling(here, left) * (soz(z, -1) - s)
        side = side + coupling(here, yn) * (next_y(s, last) - s)
        side = side + coupling(here, yp) * (prev_y(s, first) - s)
        rh[z] = s + side + ydiff(flux_y)

    def gather_rhs(z, sums):
        r = (
            rh[z]
            + (fx[z, pl.ds(PAD + 1, CX), :] - fx[z, pl.ds(PAD - 1, CX), :])
            + (fz[z + 2] - fz[z])
        )
        rh[z] = r
        return sums[0] + pp[z] * r, sums[1] + qq[z] * r

    def planes(k, _):
        for r in range(3):
            plane(1 + 3 * k + r)
        return 0

    lax.fori_loop(0, 10, planes, 0)

    g_out = spread(gs, gr, g_ss, g_rs)

    def rows(k, sums):
        for r in range(BZ):
            sums = gather_rhs(2 + BZ * k + r, sums)
        return sums

    sums = lax.fori_loop(0, 7, rows, (zero, zero))

    for side, x in ((0, 0), (1, CX - 1)):
        near = 1 if x == 0 else CX - 2
        cin[side, 8:40] = xs[side, 0]
        cnx[side, 8:40] = xs[side, 1]
        cs0[side, 8:40] = xs[side, 3]
        cpq[side, 0] = pp[:, x, :]
        cpq[side, 1] = qq[:, x, :]
        cpq[side, 2] = pp[:, near, :]
        cpq[side, 3] = qq[:, near, :]

    for cond, cp in z_in:
        pl.when(cond)(cp.wait_recv)
    ph[0, pl.ds(PAD, CX), :] = zr[0, 0]
    ph[CZ + 1, pl.ds(PAD, CX), :] = zr[1, 0]
    for side, z in ((0, -1), (1, CZ)):
        gz = phz(0) - zr[side, 1] if side == 0 else zr[side, 1] - phz(CZ - 1)
        gx = phz(z, 1) - phz(z, -1)
        factor = flux_factor(gx, ydiff(zr[side, 0]), gz, jnp.where(inner, zr[side, 2], 0.0))
        fz[z + 1] = factor * gz
    plane(0)
    plane(CZ - 1)
    for z in (0, 1, CZ - 2, CZ - 1):
        sums = gather_rhs(z, sums)
    pvs[0] = sums[0]
    pvs[1] = sums[1]
    pvr[g] = pvs[...]
    pv_out = spread(pvs, pvr, pv_ss, pv_rs)

    for side, x in ((0, 0), (1, CX - 1)):
        near = 1 if x == 0 else CX - 2
        for buf, which, xx in ((cin, 0, x), (cnx, 0, near), (cs0, 2, x)):
            buf[side, 7:8] = zr[0, which, xx:xx + 1, :]
            buf[side, 40:41] = zr[1, which, xx:xx + 1, :]
        cin[side, 6:7] = zr[0, 1, x:x + 1, :]
        cin[side, 41:42] = zr[1, 1, x:x + 1, :]
        a = cin[side, 7:47]
        cgy[side] = next_y(a, last_e) - prev_y(a, first_e)
        cgz[side] = cin[side, 8:48] - cin[side, 6:46]

    for cond, cp in x_in + c_in:
        pl.when(cond)(cp.wait_recv)
    sub = lax.broadcasted_iota(jnp.int32, (8, NY), 0)
    tile_p = jnp.zeros((8, NY), F32)
    tile_q = jnp.zeros((8, NY), F32)
    for side, x in ((0, 0), (1, CX - 1)):
        near = 1 if x == 0 else CX - 2
        pick = slice(7, 8) if side == 0 else slice(0, 1)
        outer = xr[side, 0]
        cout[side, 7:8] = cr[side, pick]
        cout[side, 8:40] = outer
        cout[side, 40:41] = cr[2 + side, pick]
        gin = cnx[side, 7:47] - cout[side, 7:47]
        factor = flux_factor(gin, cgy[side], cgz[side], cs0[side, 7:47])
        cfa[side] = factor
        cfz[side] = factor * cgz[side]
        g_out2 = xs[side, 0] - xr[side, 1]
        f_out = flux_factor(
            g_out2, ydiff(outer), cout[side, 9:41] - cout[side, 7:39], xr[side, 3]
        ) * g_out2
        own = cfa[side, 1:33]
        d_near = -own * (xs[side, 1] - outer)
        d_edge = (
            coupling(xs[side, 0], outer) * (xr[side, 2] - xs[side, 2])
            - f_out
            + ydiff(own * cgy[side, 1:33])
            + (cfz[side, 2:34] - cfz[side, 0:32])
        )
        at, at_near = (0, 1) if side == 0 else (7, 6)
        for d, where, k in ((d_edge, at, 0), (d_near, at_near, 2)):
            tile_p = jnp.where(sub == where, jnp.sum(cpq[side, k] * d, axis=0, keepdims=True), tile_p)
            tile_q = jnp.where(sub == where, jnp.sum(cpq[side, k + 1] * d, axis=0, keepdims=True), tile_q)
        cfa[side, 0:32] = d_edge
        cfz[side, 0:32] = d_near
    es[0] = tile_p
    es[1] = tile_q
    er[g] = es[...]
    e_out = spread(es, er, e_ss, e_rs)
    for side, x in ((0, 0), (1, CX - 1)):
        near = 1 if x == 0 else CX - 2
        rh[:, x, :] = rh[:, x, :] + cfa[side, 0:32]
        rh[:, near, :] = rh[:, near, :] + cfz[side, 0:32]

    ee[0] = rh[0]
    bb[CZ - 1] = rh[CZ - 1]

    def sweep(i, carry):
        f, b = carry
        j = CZ - 1 - i
        f = rh[i] + wf[i - 1] * f
        b = rh[j] + vb[j + 1] * b
        ee[i] = f
        bb[j] = b
        return f, b

    def sweep3(k, carry):
        for r in range(3):
            carry = sweep(2 + 3 * k + r, carry)
        return carry

    lax.fori_loop(0, 10, sweep3, sweep(1, (rh[0], rh[CZ - 1])))

    def local(k, _):
        for r in range(BZ):
            z = k * BZ + r
            ee[z] = (ee[z] + bb[z] - rh[z]) * dd[z]
        return 0

    lax.fori_loop(0, CZ // BZ, local, 0)

    arrive(gs, gr, g_ss, g_rs)

    def self_term(k):
        return 1.0 / face(gr[k, 4], gr[k + 1, 3]) + gr[k, 1] + gr[k + 1, 0]

    m0 = 1.0 / self_term(0)
    t1, t2 = gr[1, 2], gr[2, 2]
    k1 = t1 * m0
    m1 = 1.0 / (self_term(1) - t1 * k1)
    k2 = t2 * m1
    m2 = 1.0 / (self_term(2) - t2 * k2)
    arrive(pvs, pvr, pv_ss, pv_rs)
    jump = [pvr[k, 1] - pvr[k + 1, 0] for k in range(NG - 1)]
    arrive(es, er, e_ss, e_rs)
    for k in range(NG - 1):
        tile = er[k, 1] - er[k + 1, 0]
        full = jnp.concatenate([tile, jnp.zeros((CX - 16, NY), F32), tile], axis=0)
        jump[k] = jump[k] + jnp.where((row < 2) | (row >= CX - 2), full, 0.0)
    b0 = jump[0]
    b1 = jump[1] + k1 * b0
    b2 = jump[2] + k2 * b1
    q2 = b2 * m2
    q1 = b1 * m1 + k2 * q2
    q0 = b0 * m0 + k1 * q1
    below = jnp.where(g == 1, q0, jnp.where(g == 2, q1, jnp.where(g == 3, q2, 0.0)))
    above = jnp.where(g == 0, q0, jnp.where(g == 1, q1, jnp.where(g == 2, q2, 0.0)))

    def close(k, _):
        for r in range(BZ):
            z = k * BZ + r
            out[z] = ee[z] + pp[z] * below - qq[z] * above
        return 0

    lax.fori_loop(0, CZ // BZ, close, 0)

    for cond, cp in x_out + z_out + c_out:
        pl.when(cond)(cp.wait_send)
    for cp in g_out + pv_out + e_out:
        cp.wait_send()


def step(phase, old, solute, blocks, count):
    def buf(*shape):
        return pltpu.VMEM(shape + (NY,), F32)

    slab = buf(CZ, CX)
    dma = pltpu.SemaphoreType.DMA
    return pl.pallas_call(
        kernel,
        out_shape=pltpu.VMEM((CZ, CX, NY), F32),
        in_specs=[pl.BlockSpec(memory_space=pl.ANY)] * 5,
        out_specs=pl.BlockSpec(memory_space=pltpu.VMEM),
        scratch_shapes=[
            buf(CZ + 2, ROW), buf(CZ, ROW), slab, slab, buf(CZ, ROW), buf(CZ + 2, CX),
            slab, slab, slab, slab, slab, slab, slab, slab, slab, slab, slab, slab,
            buf(2, 56), buf(2, 56), buf(2, 56), buf(2, 56),
            buf(2, 40), buf(2, 40), buf(2, 40), buf(2, 40), buf(2, 4, CZ),
            buf(2, 4, CZ), buf(2, 4, CZ),
            buf(2, 3, CX), buf(2, 3, CX),
            buf(4, 8), buf(4, 8),
            buf(5, CX), buf(NG, 5, CX),
            buf(2, CX), buf(NG, 2, CX),
            buf(2, 8), buf(NG, 2, 8),
            pltpu.SMEM((1, 1, 6), jnp.int32),
            pltpu.SMEM((1, 1), jnp.int32),
            dma((5,)),
            dma((2,)), dma((2,)),
            dma((2,)), dma((2,)),
            dma((4,)), dma((4,)),
            dma((3,)), dma((NG,)),
            dma((3,)), dma((NG,)),
            dma((3,)), dma((NG,)),
        ],
        compiler_params=pltpu.CompilerParams(
            collective_id=0, has_side_effects=True, vmem_limit_bytes=66000000
        ),
    )(phase, old, solute, blocks, count)


def solution(mesh):
    spec = P("growth", "lateral", None)
    return jax.shard_map(
        step,
        mesh=mesh,
        in_specs=(spec, spec, spec, spec, P("growth", "lateral")),
        out_specs=spec,
        check_vma=False,
    )
```

```python
import jax
import jax.numpy as jnp
from jax import lax
from jax.experimental import pallas as pl
from jax.experimental.pallas import tpu as pltpu
from jax.sharding import PartitionSpec as P

BZ = 4
MESH = pl.DeviceIdType.MESH
NG = 4
NL = 32
CZ = 32
CX = 32
NY = 128
PAD = 8
ROW = CX + 2 * PAD
F32 = jnp.float32


def flux_factor(gx, gy, gz, pre):
    x2 = gx * gx
    y2 = gy * gy
    z2 = gz * gz
    inv = lax.rsqrt(x2 + y2 + z2 + 1.0)
    inv2 = inv * inv
    quartic = x2 * x2 + y2 * y2 + z2 * z2
    return pre * inv * (0.1 + 1.2 * quartic * (inv2 * inv2))


def next_y(a, last):
    return jnp.where(last, 0.0, pltpu.roll(a, NY - 1, 1))


def prev_y(a, first):
    return jnp.where(first, 0.0, pltpu.roll(a, 1, 1))


def kernel(
    phase, old, solute, blocks, count, out,
    ph, so, po, s0, fx, fz, rh, ee, bb, wf, pf, vb, qf, dd, pp, qq, ea, eb,
    cin, cnx, cout, cs0, cgy, cgz, cfa, cfz, cpq,
    xs, xr, zs, zr, cs, cr, ts, tr, pvs, pvr, es, er, blk, cnt,
    in_sem, x_ss, x_rs, z_ss, z_rs, c_ss, c_rs, t_ss, t_rs, pv_ss, pv_rs, e_ss, e_rs, met,
):
    g = lax.axis_index("growth")
    l = lax.axis_index("lateral")
    has_lo, has_hi = g > 0, g < NG - 1
    has_xl, has_xr = l > 0, l < NL - 1
    g_lo, g_hi = jnp.maximum(g - 1, 0), jnp.minimum(g + 1, NG - 1)
    l_lo, l_hi = jnp.maximum(l - 1, 0), jnp.minimum(l + 1, NL - 1)
    others = [lax.rem(g + d, NG) for d in (2, 1, 3)]

    barrier = pltpu.get_barrier_semaphore()

    def greet(cond, dev):
        @pl.when(cond)
        def _():
            pl.semaphore_signal(barrier, inc=1, device_id=dev, device_id_type=MESH)

    diag = [
        (has_lo & has_xl, (g_lo, l_lo)),
        (has_lo & has_xr, (g_lo, l_hi)),
        (has_hi & has_xl, (g_hi, l_lo)),
        (has_hi & has_xr, (g_hi, l_hi)),
    ]
    ends = jnp.logical_not(has_lo & has_hi)
    greet(has_lo, (g_lo, l))
    greet(has_hi, (g_hi, l))
    greet(has_xl, (g, l_lo))
    greet(has_xr, (g, l_hi))
    greet(ends, (NG - 1 - g, l))

    ins = [
        pltpu.make_async_copy(phase, ph.at[pl.ds(1, CZ), pl.ds(PAD, CX), :], in_sem.at[0]),
        pltpu.make_async_copy(old, po, in_sem.at[1]),
        pltpu.make_async_copy(solute, so.at[:, pl.ds(PAD, CX), :], in_sem.at[2]),
        pltpu.make_async_copy(blocks, blk, in_sem.at[3]),
        pltpu.make_async_copy(count, cnt, in_sem.at[4]),
    ]
    for c in ins:
        c.start()

    lane = lax.broadcasted_iota(jnp.int32, (CX, NY), 1)
    row = lax.broadcasted_iota(jnp.int32, (CX, NY), 0)
    first, last = lane == 0, lane == NY - 1
    inner = (row > 0) & (row < CX - 1)
    zero = jnp.zeros((CX, NY), F32)
    one = zero + 1.0
    EXT = 40
    lane_e = lax.broadcasted_iota(jnp.int32, (EXT, NY), 1)
    first_e, last_e = lane_e == 0, lane_e == NY - 1

    def face(a, b):
        return 220.0 - 90.0 * (a + b)

    def coupling(a, b):
        return 0.055 - 0.0225 * (a + b)

    def ydiff(a):
        return next_y(a, last) - prev_y(a, first)

    def phz(z, off=0):
        return ph[z + 1, pl.ds(PAD + off, CX), :]

    def soz(z, off=0):
        return so[z, pl.ds(PAD + off, CX), :]

    for c in ins:
        c.wait()

    live = [jnp.where(s < cnt[0, 0], blk[0, 0, s], -1) for s in range(6)]

    def masked(k):
        hit = k == live[0]
        for b in live[1:]:
            hit = hit | (k == b)
        return jnp.where(hit, 0.25, 0.0)

    column_mask = masked(row // BZ)
    for side, x in ((0, 0), (1, CX - 1)):
        near = 1 if x == 0 else CX - 2
        here, s = ph[1:CZ + 1, PAD + x, :], so[:, PAD + x, :]
        xs[side, 0] = here
        xs[side, 1] = ph[1:CZ + 1, PAD + near, :]
        xs[side, 2] = s
        xs[side, 3] = (1.0 + 0.7 * s) * (here - po[:, x, :]) * column_mask
    for side, z in ((0, 0), (1, CZ - 1)):
        zs[side, 0] = phz(z)
        zs[side, 1] = phz(1 if z == 0 else CZ - 2)
        zs[side, 2] = (1.0 + 0.7 * soz(z)) * (phz(z) - po[z]) * masked(jnp.int32(z // BZ))
        cs[2 * side] = phz(z)[0:8]
        cs[2 * side + 1] = phz(z)[CX - 8:CX]

    def many(*conds):
        return sum(c.astype(jnp.int32) for c in conds)

    pl.semaphore_wait(barrier, many(has_lo, has_hi, has_xl, has_xr, ends))

    def remote(src, dst, ss, rs, dev):
        return pltpu.make_async_remote_copy(
            src_ref=src, dst_ref=dst, send_sem=ss, recv_sem=rs, device_id=dev, device_id_type=MESH
        )

    x_out = [
        (has_xl, remote(xs.at[0], xr.at[1], x_ss.at[0], x_rs.at[1], (g, l_lo))),
        (has_xr, remote(xs.at[1], xr.at[0], x_ss.at[1], x_rs.at[0], (g, l_hi))),
    ]
    z_out = [
        (has_lo, remote(zs.at[0, 0:3], zr.at[1, 0:3], z_ss.at[0], z_rs.at[1], (g_lo, l))),
        (has_hi, remote(zs.at[1, 0:3], zr.at[0, 0:3], z_ss.at[1], z_rs.at[0], (g_hi, l))),
    ]
    w_out = [
        (has_lo, remote(zs.at[0, 3], zr.at[1, 3], z_ss.at[2], z_rs.at[3], (g_lo, l))),
        (has_hi, remote(zs.at[1, 3], zr.at[0, 3], z_ss.at[3], z_rs.at[2], (g_hi, l))),
    ]
    w_in = [
        (has_lo, remote(zs.at[1, 3], zr.at[0, 3], z_ss.at[3], z_rs.at[2], (g_lo, l))),
        (has_hi, remote(zs.at[0, 3], zr.at[1, 3], z_ss.at[2], z_rs.at[3], (g_hi, l))),
    ]
    c_out = [
        (cond, remote(cs.at[i], cr.at[3 - i], c_ss.at[i], c_rs.at[3 - i], dev))
        for i, (cond, dev) in enumerate(diag)
    ]
    for cond, cp in z_out + x_out:
        pl.when(cond)(cp.start)
    for i, (cond, o) in enumerate(((has_lo, g_lo), (has_hi, g_hi))):
        @pl.when(cond)
        def _():
            pl.semaphore_signal(met, inc=1, device_id=(o, l), device_id_type=MESH)
    x_in = [
        (has_xl, remote(xs.at[1], xr.at[0], x_ss.at[1], x_rs.at[0], (g, l_lo))),
        (has_xr, remote(xs.at[0], xr.at[1], x_ss.at[0], x_rs.at[1], (g, l_hi))),
    ]
    z_in = [
        (has_lo, remote(zs.at[1, 0:3], zr.at[0, 0:3], z_ss.at[1], z_rs.at[0], (g_lo, l))),
        (has_hi, remote(zs.at[0, 0:3], zr.at[1, 0:3], z_ss.at[0], z_rs.at[1], (g_hi, l))),
    ]
    c_in = [
        (cond, remote(cs.at[3 - i], cr.at[i], c_ss.at[3 - i], c_rs.at[i], dev))
        for i, (cond, dev) in enumerate(diag)
    ]

    middle = has_lo & has_hi
    up = g >= NG // 2
    half = up.astype(jnp.int32)
    inner_dev, outer_dev = 1 + half, 3 * half
    far_inner, far_outer = 2 - half, 3 - 3 * half
    t_out, pv_out = [], []
    for d, o in enumerate(others):
        to_end = middle & (o == outer_dev)
        to_far = middle & (o != outer_dev)
        for cond, at in ((to_end, pl.ds(0, 2)), (to_far, pl.ds(1, 2))):
            t_out.append((cond, remote(ts.at[at], tr.at[g, at], t_ss.at[d], t_rs.at[g], (o, l))))
        for cond, at in ((to_end, pl.ds(0, 2)), (jnp.logical_not(to_end), pl.ds(2, 1))):
            pv_out.append((cond, remote(pvs.at[at], pvr.at[g, at], pv_ss.at[d], pv_rs.at[g], (o, l))))
    t_in, pv_in = [], []
    for k in range(NG):
        from_inner = jnp.logical_not(middle) & (inner_dev == k)
        if k in (1, 2):
            from_far = far_inner == k
            for cond, at in ((from_inner, pl.ds(0, 2)), (from_far, pl.ds(1, 2))):
                t_in.append((cond, remote(ts.at[at], tr.at[k, at], t_ss.at[0], t_rs.at[k], (k, l))))
        from_other = (g != k) & jnp.logical_not(from_inner)
        for cond, at in ((from_inner, pl.ds(0, 2)), (from_other, pl.ds(2, 1))):
            pv_in.append((cond, remote(pvs.at[at], pvr.at[k, at], pv_ss.at[0], pv_rs.at[k], (k, l))))
    e_out = [
        (None, remote(es, er.at[g], e_ss.at[d], e_rs.at[g], (o, l))) for d, o in enumerate(others)
    ]

    bottom = jnp.where(g == 0, face(phz(0), 0.0), zero) + 1.0
    top = jnp.where(g == NG - 1, face(phz(CZ - 1), 0.0), zero) + 1.0
    ea[0] = bottom
    pf[0] = one
    eb[CZ - 1] = top
    qf[CZ - 1] = one

    def eliminate(i, carry):
        e, prod, ebar, qprod = carry
        j = CZ - 1 - i
        u = face(phz(i), phz(i + 1))
        v = face(phz(j), phz(j - 1))
        w = u / (u + e)
        y = v / (v + ebar)
        e = 1.0 + w * e
        ebar = 1.0 + y * ebar
        prod = prod * w
        qprod = qprod * y
        wf[i] = w
        vb[j] = y
        ea[i + 1] = e
        eb[j - 1] = ebar
        pf[i + 1] = prod
        qf[j - 1] = qprod
        return e, prod, ebar, qprod

    def eliminate3(k, carry):
        for r in range(3):
            carry = eliminate(1 + 3 * k + r, carry)
        return carry

    lax.fori_loop(0, 10, eliminate3, eliminate(0, (bottom, one, top, one)))

    def finish(k, _):
        for r in range(BZ):
            i = k * BZ + r
            d = 1.0 / (ea[i] + eb[i] - 1.0)
            dd[i] = d
            pp[i] = pf[i] * d
            qq[i] = qf[i] * d
        return 0

    lax.fori_loop(0, CZ // BZ, finish, 0)
    zs[0, 3] = pp[0]
    zs[1, 3] = qq[CZ - 1]
    ts[1] = pp[CZ - 1]
    pl.semaphore_wait(met, many(has_lo, has_hi))
    for cond, cp in c_out + w_out:
        pl.when(cond)(cp.start)


    for side, x in ((0, -1), (1, CX)):
        ph[0:CZ, PAD + x, :] = zero
        ph[CZ:CZ + 2, PAD + x, :] = zero[0:2]
        fx[:, PAD + x, :] = zero
        so[:, PAD + x, :] = xs[side, 2]
        for buf in (cin, cnx, cout, cs0):
            buf[side, 0:8] = zero[0:8]
            buf[side, 40:56] = zero[0:16]
        @pl.when(jnp.logical_not((has_xl, has_xr)[side]))
        def _():
            xr[side] = jnp.zeros((4, CZ, NY), F32)
        @pl.when(jnp.logical_not((has_lo, has_hi)[side]))
        def _():
            zr[side] = jnp.zeros((4, CX, NY), F32)
    for i, (cond, _) in enumerate(diag):
        @pl.when(jnp.logical_not(cond))
        def _():
            cr[i] = jnp.zeros((8, NY), F32)

    def prefactor(k, _):
        mask = masked(k)
        for r in range(BZ):
            z = k * BZ + r
            s0[z] = (1.0 + 0.7 * soz(z)) * (phz(z) - po[z]) * mask
        return 0

    lax.fori_loop(0, CZ // BZ, prefactor, 0)

    def plane(z):
        here = phz(z)
        right, left = phz(z, 1), phz(z, -1)
        yn, yp = next_y(here, last), prev_y(here, first)
        gx = right - left
        gy = yn - yp
        gz = phz(z + 1) - phz(z - 1)
        factor = flux_factor(gx, gy, gz, jnp.where(inner, s0[z], 0.0))
        fx[z, pl.ds(PAD, CX), :] = factor * gx
        fz[z + 1] = factor * gz
        flux_y = factor * gy
        s = soz(z)
        side = coupling(here, right) * (soz(z, 1) - s) + coupling(here, left) * (soz(z, -1) - s)
        step_y = coupling(here, yn) * (next_y(s, last) - s)
        back = jnp.where(first, coupling(here, 0.0) * s, pltpu.roll(step_y + flux_y, 1, 1))
        rh[z] = s + side + (step_y + next_y(flux_y, last) - back)

    def gather_rhs(z, sums):
        r = (
            rh[z]
            + (fx[z, pl.ds(PAD + 1, CX), :] - fx[z, pl.ds(PAD - 1, CX), :])
            + (fz[z + 2] - fz[z])
        )
        rh[z] = r
        return sums[0] + pp[z] * r, sums[1] + qq[z] * r

    def planes(k, _):
        for r in range(6):
            plane(1 + 6 * k + r)
        return 0

    lax.fori_loop(0, 5, planes, 0)

    def rows(k, sums):
        for r in range(BZ):
            sums = gather_rhs(2 + BZ * k + r, sums)
        return sums

    sums = lax.fori_loop(0, 7, rows, (zero, zero))

    for side, x in ((0, 0), (1, CX - 1)):
        near = 1 if x == 0 else CX - 2
        cin[side, 8:40] = xs[side, 0]
        cnx[side, 8:40] = xs[side, 1]
        cs0[side, 8:40] = xs[side, 3]
        cpq[side, 0] = pp[:, x, :]
        cpq[side, 1] = qq[:, x, :]
        cpq[side, 2] = pp[:, near, :]
        cpq[side, 3] = qq[:, near, :]

    for cond, cp in z_in:
        pl.when(cond)(cp.wait_recv)
    for cond, cp in w_in:
        pl.when(cond)(cp.wait_recv)
    self_hi = 1.0 / face(phz(CZ - 1), zr[1, 0]) + qq[CZ - 1] + zr[1, 3]
    self_lo = 1.0 / face(phz(0), zr[0, 0]) + pp[0] + zr[0, 3]
    even = lax.rem(g, 2) == 0
    self_out = jnp.where(even, self_hi, self_lo)
    ts[0] = jnp.where(even, self_lo, self_hi)
    ts[2] = self_out
    tr[g] = ts[...]
    for cond, cp in t_out:
        pl.when(cond)(cp.start)
    own_k = ts[1] / self_out
    ph[0, pl.ds(PAD, CX), :] = zr[0, 0]
    ph[CZ + 1, pl.ds(PAD, CX), :] = zr[1, 0]
    for side, z in ((0, -1), (1, CZ)):
        gz = phz(0) - zr[side, 1] if side == 0 else zr[side, 1] - phz(CZ - 1)
        gx = phz(z, 1) - phz(z, -1)
        factor = flux_factor(gx, ydiff(zr[side, 0]), gz, jnp.where(inner, zr[side, 2], 0.0))
        fz[z + 1] = factor * gz
    plane(0)
    plane(CZ - 1)
    for z in (0, 1, CZ - 2, CZ - 1):
        sums = gather_rhs(z, sums)
    facing, away = jnp.where(up, sums[0], sums[1]), jnp.where(up, sums[1], sums[0])
    pvs[0] = facing
    pvs[1] = away
    pvs[2] = jnp.where(middle, facing - own_k * away, facing)
    pvr[g] = pvs[...]
    for cond, cp in pv_out:
        pl.when(cond)(cp.start)

    for side, x in ((0, 0), (1, CX - 1)):
        near = 1 if x == 0 else CX - 2
        for buf, which, xx in ((cin, 0, x), (cnx, 0, near), (cs0, 2, x)):
            buf[side, 7:8] = zr[0, which, xx:xx + 1, :]
            buf[side, 40:41] = zr[1, which, xx:xx + 1, :]
        cin[side, 6:7] = zr[0, 1, x:x + 1, :]
        cin[side, 41:42] = zr[1, 1, x:x + 1, :]
        a = cin[side, 7:47]
        cgy[side] = next_y(a, last_e) - prev_y(a, first_e)
        cgz[side] = cin[side, 8:48] - cin[side, 6:46]

    for cond, cp in x_in + c_in:
        pl.when(cond)(cp.wait_recv)
    sub = lax.broadcasted_iota(jnp.int32, (8, NY), 0)
    tile_p = jnp.zeros((8, NY), F32)
    tile_q = jnp.zeros((8, NY), F32)
    for side, x in ((0, 0), (1, CX - 1)):
        near = 1 if x == 0 else CX - 2
        pick = slice(7, 8) if side == 0 else slice(0, 1)
        outer = xr[side, 0]
        cout[side, 7:8] = cr[side, pick]
        cout[side, 8:40] = outer
        cout[side, 40:41] = cr[2 + side, pick]
        gin = cnx[side, 7:47] - cout[side, 7:47]
        factor = flux_factor(gin, cgy[side], cgz[side], cs0[side, 7:47])
        cfa[side] = factor
        cfz[side] = factor * cgz[side]
        g_out2 = xs[side, 0] - xr[side, 1]
        f_out = flux_factor(
            g_out2, ydiff(outer), cout[side, 9:41] - cout[side, 7:39], xr[side, 3]
        ) * g_out2
        own = cfa[side, 1:33]
        d_near = -own * (xs[side, 1] - outer)
        d_edge = (
            coupling(xs[side, 0], outer) * (xr[side, 2] - xs[side, 2])
            - f_out
            + ydiff(own * cgy[side, 1:33])
            + (cfz[side, 2:34] - cfz[side, 0:32])
        )
        at, at_near = (0, 1) if side == 0 else (7, 6)
        for d, where, k in ((d_edge, at, 0), (d_near, at_near, 2)):
            tile_p = jnp.where(sub == where, jnp.sum(cpq[side, k] * d, axis=0, keepdims=True), tile_p)
            tile_q = jnp.where(sub == where, jnp.sum(cpq[side, k + 1] * d, axis=0, keepdims=True), tile_q)
        cfa[side, 0:32] = d_edge
        cfz[side, 0:32] = d_near
    left_rows = sub < 4
    tile_facing, tile_away = jnp.where(up, tile_p, tile_q), jnp.where(up, tile_q, tile_p)
    tile_k = jnp.where(left_rows, own_k[0:8], own_k[CX - 8:CX])
    es[0] = tile_facing
    es[1] = tile_away
    es[2] = jnp.where(middle, tile_facing - tile_k * tile_away, tile_facing)
    er[g] = es[...]
    for _, cp in e_out:
        cp.start()
    for side, x in ((0, 0), (1, CX - 1)):
        near = 1 if x == 0 else CX - 2
        rh[:, x, :] = rh[:, x, :] + cfa[side, 0:32]
        rh[:, near, :] = rh[:, near, :] + cfz[side, 0:32]

    ee[0] = rh[0]
    bb[CZ - 1] = rh[CZ - 1]

    def sweep(i, carry):
        f, b = carry
        j = CZ - 1 - i
        f = rh[i] + wf[i - 1] * f
        b = rh[j] + vb[j + 1] * b
        ee[i] = f
        bb[j] = b
        return f, b

    def sweep3(k, carry):
        for r in range(3):
            carry = sweep(2 + 3 * k + r, carry)
        return carry

    lax.fori_loop(0, 10, sweep3, sweep(1, (rh[0], rh[CZ - 1])))

    def local(k, _):
        for r in range(BZ):
            z = k * BZ + r
            ee[z] = (ee[z] + bb[z] - rh[z]) * dd[z]
        return 0

    lax.fori_loop(0, CZ // BZ, local, 0)

    for cond, cp in t_in:
        pl.when(cond)(cp.wait_recv)
    t_far, t_own = tr[far_inner, 1], tr[inner_dev, 1]
    k1 = t_far / tr[far_inner, 2]
    m1 = 1.0 / (tr[inner_dev, 0] - t_far * k1)
    k2 = t_own * m1
    m2 = 1.0 / (ts[2] - t_own * k2)
    for cond, cp in pv_in:
        pl.when(cond)(cp.wait_recv)
    b1 = pvr[far_inner, 2] + k1 * pvr[far_outer, 2] - pvr[inner_dev, 0]
    b2 = pvr[inner_dev, 1] - pvr[outer_dev, 2]
    tile_k1 = jnp.where(left_rows, k1[0:8], k1[CX - 8:CX])
    for o in others:
        remote(es, er.at[o], e_ss.at[0], e_rs.at[o], (o, l)).wait_recv()

    def widen(tile):
        full = jnp.concatenate([tile, jnp.zeros((CX - 16, NY), F32), tile], axis=0)
        return jnp.where((row < 2) | (row >= CX - 2), full, 0.0)

    b1 = b1 + widen(er[far_inner, 2] + tile_k1 * er[far_outer, 2] - er[inner_dev, 0])
    b2 = b2 + widen(er[inner_dev, 1] - er[outer_dev, 2])
    r2 = (b2 + k2 * b1) * m2
    r1 = (b1 + t_own * r2) * m1
    below = jnp.where(g == 3, r2, jnp.where(g == 2, r1, jnp.where(g == 1, -r2, 0.0)))
    above = jnp.where(g == 0, -r2, jnp.where(g == 1, -r1, jnp.where(g == 2, r2, 0.0)))

    def close(k, _):
        for r in range(BZ):
            z = k * BZ + r
            out[z] = ee[z] + pp[z] * below - qq[z] * above
        return 0

    lax.fori_loop(0, CZ // BZ, close, 0)

    for cond, cp in x_out + z_out + c_out + w_out + t_out + pv_out:
        pl.when(cond)(cp.wait_send)
    for _, cp in e_out:
        cp.wait_send()


def step(phase, old, solute, blocks, count):
    def buf(*shape):
        return pltpu.VMEM(shape + (NY,), F32)

    slab = buf(CZ, CX)
    dma = pltpu.SemaphoreType.DMA
    return pl.pallas_call(
        kernel,
        out_shape=pltpu.VMEM((CZ, CX, NY), F32),
        in_specs=[pl.BlockSpec(memory_space=pl.ANY)] * 5,
        out_specs=pl.BlockSpec(memory_space=pltpu.VMEM),
        scratch_shapes=[
            buf(CZ + 2, ROW), buf(CZ, ROW), slab, slab, buf(CZ, ROW), buf(CZ + 2, CX),
            slab, slab, slab, slab, slab, slab, slab, slab, slab, slab, slab, slab,
            buf(2, 56), buf(2, 56), buf(2, 56), buf(2, 56),
            buf(2, 40), buf(2, 40), buf(2, 40), buf(2, 40), buf(2, 4, CZ),
            buf(2, 4, CZ), buf(2, 4, CZ),
            buf(2, 4, CX), buf(2, 4, CX),
            buf(4, 8), buf(4, 8),
            buf(3, CX), buf(NG, 3, CX),
            buf(3, CX), buf(NG, 3, CX),
            buf(3, 8), buf(NG, 3, 8),
            pltpu.SMEM((1, 1, 6), jnp.int32),
            pltpu.SMEM((1, 1), jnp.int32),
            dma((5,)),
            dma((2,)), dma((2,)),
            dma((4,)), dma((4,)),
            dma((4,)), dma((4,)),
            dma((3,)), dma((NG,)),
            dma((3,)), dma((NG,)),
            dma((3,)), dma((NG,)),
            pltpu.SemaphoreType.REGULAR,
        ],
        compiler_params=pltpu.CompilerParams(
            collective_id=0, has_side_effects=True, vmem_limit_bytes=66000000
        ),
    )(phase, old, solute, blocks, count)


def solution(mesh):
    spec = P("growth", "lateral", None)
    return jax.shard_map(
        step,
        mesh=mesh,
        in_specs=(spec, spec, spec, spec, P("growth", "lateral")),
        out_specs=spec,
        check_vma=False,
    )
```

```python
import jax
import jax.numpy as jnp
from jax import lax
from jax.experimental import pallas as pl
from jax.experimental.pallas import tpu as pltpu
from jax.sharding import PartitionSpec as P

BZ = 4
MESH = pl.DeviceIdType.MESH
NG = 4
NL = 32
CZ = 32
CX = 32
NY = 128
PAD = 8
ROW = CX + 2 * PAD
F32 = jnp.float32


def flux_factor(gx, gy, gz, pre):
    x2 = gx * gx
    y2 = gy * gy
    z2 = gz * gz
    inv = lax.rsqrt(x2 + y2 + z2 + 1.0)
    inv2 = inv * inv
    quartic = x2 * x2 + y2 * y2 + z2 * z2
    return pre * inv * (0.1 + 1.2 * quartic * (inv2 * inv2))


def next_y(a, last):
    return jnp.where(last, 0.0, pltpu.roll(a, NY - 1, 1))


def prev_y(a, first):
    return jnp.where(first, 0.0, pltpu.roll(a, 1, 1))


def kernel(
    phase, old, solute, blocks, count, out,
    ph, so, po, s0, fx, fz, rh, ee, bb, wf, pf, vb, qf, dd, pp, qq, ea, eb,
    cin, cnx, cout, cs0, cgy, cgz, cfa, cfz, cpq, cgo, w8,
    xs, xr, zs, zr, cs, cr, ts, tr, ss, sr, pvs, pvr, es, er, blk, cnt,
    in_sem, x_ss, x_rs, z_ss, z_rs, c_ss, c_rs, t_ss, t_rs, s_ss, s_rs, pv_ss, pv_rs, e_ss, e_rs, met,
):
    g = lax.axis_index("growth")
    l = lax.axis_index("lateral")
    has_lo, has_hi = g > 0, g < NG - 1
    has_xl, has_xr = l > 0, l < NL - 1
    g_lo, g_hi = jnp.maximum(g - 1, 0), jnp.minimum(g + 1, NG - 1)
    l_lo, l_hi = jnp.maximum(l - 1, 0), jnp.minimum(l + 1, NL - 1)
    others = [lax.rem(g + d, NG) for d in (2, 1, 3)]

    barrier = pltpu.get_barrier_semaphore()

    def greet(cond, dev):
        @pl.when(cond)
        def _():
            pl.semaphore_signal(barrier, inc=1, device_id=dev, device_id_type=MESH)

    diag = [
        (has_lo & has_xl, (g_lo, l_lo)),
        (has_lo & has_xr, (g_lo, l_hi)),
        (has_hi & has_xl, (g_hi, l_lo)),
        (has_hi & has_xr, (g_hi, l_hi)),
    ]
    ends = jnp.logical_not(has_lo & has_hi)
    greet(has_lo, (g_lo, l))
    greet(has_hi, (g_hi, l))
    greet(has_xl, (g, l_lo))
    greet(has_xr, (g, l_hi))
    greet(ends, (NG - 1 - g, l))

    ins = [
        pltpu.make_async_copy(phase, ph.at[pl.ds(1, CZ), pl.ds(PAD, CX), :], in_sem.at[0]),
        pltpu.make_async_copy(old, po, in_sem.at[1]),
        pltpu.make_async_copy(solute, so.at[:, pl.ds(PAD, CX), :], in_sem.at[2]),
        pltpu.make_async_copy(blocks, blk, in_sem.at[3]),
        pltpu.make_async_copy(count, cnt, in_sem.at[4]),
    ]
    for c in ins:
        c.start()

    lane = lax.broadcasted_iota(jnp.int32, (CX, NY), 1)
    row = lax.broadcasted_iota(jnp.int32, (CX, NY), 0)
    first, last = lane == 0, lane == NY - 1
    inner = (row > 0) & (row < CX - 1)
    zero = jnp.zeros((CX, NY), F32)
    one = zero + 1.0
    EXT = 40
    lane_e = lax.broadcasted_iota(jnp.int32, (EXT, NY), 1)
    first_e, last_e = lane_e == 0, lane_e == NY - 1

    def face(a, b):
        return 220.0 - 90.0 * (a + b)

    def coupling(a, b):
        return 0.055 - 0.0225 * (a + b)

    def ydiff(a):
        return next_y(a, last) - prev_y(a, first)

    def phz(z, off=0):
        return ph[z + 1, pl.ds(PAD + off, CX), :]

    def soz(z, off=0):
        return so[z, pl.ds(PAD + off, CX), :]

    for c in ins:
        c.wait()

    live = [jnp.where(s < cnt[0, 0], blk[0, 0, s], -1) for s in range(6)]

    def masked(k):
        hit = k == live[0]
        for b in live[1:]:
            hit = hit | (k == b)
        return jnp.where(hit, 0.25, 0.0)

    column_mask = masked(row // BZ)
    sub = lax.broadcasted_iota(jnp.int32, (8, NY), 0)
    for side, x in ((0, 0), (1, CX - 1)):
        near = 1 if x == 0 else CX - 2
        here, s = ph[1:CZ + 1, PAD + x, :], so[:, PAD + x, :]
        xs[side, 0] = here
        xs[side, 1] = ph[1:CZ + 1, PAD + near, :]
        xs[side, 2] = s
        xs[side, 3] = (1.0 + 0.7 * s) * (here - po[:, x, :]) * column_mask
    for side, z in ((0, 0), (1, CZ - 1)):
        zs[side, 0] = phz(z)
        zs[side, 1] = phz(1 if z == 0 else CZ - 2)
        zs[side, 2] = (1.0 + 0.7 * soz(z)) * (phz(z) - po[z]) * masked(jnp.int32(z // BZ))
        for right, x in ((0, 0), (1, CX - 1)):
            slot = 3 - (2 * side + right)
            want = (sub // 4 == slot % 2) & (sub % 2 == slot // 2)
            corner = jnp.broadcast_to(phz(z)[x:x + 1], (8, NY))
            cs[2 * side + right] = jnp.where(want, corner, 0.0)

    def many(*conds):
        return sum(c.astype(jnp.int32) for c in conds)

    pl.semaphore_wait(barrier, many(has_lo, has_hi, has_xl, has_xr, ends))

    def remote(src, dst, ss, rs, dev):
        return pltpu.make_async_remote_copy(
            src_ref=src, dst_ref=dst, send_sem=ss, recv_sem=rs, device_id=dev, device_id_type=MESH
        )

    x_out = [
        (has_xl, remote(xs.at[0], xr.at[1], x_ss.at[0], x_rs.at[1], (g, l_lo))),
        (has_xr, remote(xs.at[1], xr.at[0], x_ss.at[1], x_rs.at[0], (g, l_hi))),
    ]
    z_out = [
        (has_lo, remote(zs.at[0, 0:3], zr.at[1, 0:3], z_ss.at[0], z_rs.at[1], (g_lo, l))),
        (has_hi, remote(zs.at[1, 0:3], zr.at[0, 0:3], z_ss.at[1], z_rs.at[0], (g_hi, l))),
    ]
    w_out = [
        (has_lo, remote(zs.at[0, 3], zr.at[1, 3], z_ss.at[2], z_rs.at[3], (g_lo, l))),
        (has_hi, remote(zs.at[1, 3], zr.at[0, 3], z_ss.at[3], z_rs.at[2], (g_hi, l))),
    ]
    w_in = [
        (has_lo, remote(zs.at[1, 3], zr.at[0, 3], z_ss.at[3], z_rs.at[2], (g_lo, l))),
        (has_hi, remote(zs.at[0, 3], zr.at[1, 3], z_ss.at[2], z_rs.at[3], (g_hi, l))),
    ]
    c_out = [
        (cond, remote(cs.at[i], cr.at[3 - i], c_ss.at[i], c_rs.at[3 - i], dev))
        for i, (cond, dev) in enumerate(diag)
    ]
    for i, (cond, o) in enumerate(((has_lo, g_lo), (has_hi, g_hi))):
        @pl.when(cond)
        def _():
            pl.semaphore_signal(met, inc=1, device_id=(o, l), device_id_type=MESH)
    for cond, cp in z_out + x_out:
        pl.when(cond)(cp.start)
    x_in = [
        (has_xl, remote(xs.at[1], xr.at[0], x_ss.at[1], x_rs.at[0], (g, l_lo))),
        (has_xr, remote(xs.at[0], xr.at[1], x_ss.at[0], x_rs.at[1], (g, l_hi))),
    ]
    z_in = [
        (has_lo, remote(zs.at[1, 0:3], zr.at[0, 0:3], z_ss.at[1], z_rs.at[0], (g_lo, l))),
        (has_hi, remote(zs.at[0, 0:3], zr.at[1, 0:3], z_ss.at[0], z_rs.at[1], (g_hi, l))),
    ]
    c_in = [
        (cond, remote(cs.at[3 - i], cr.at[i], c_ss.at[3 - i], c_rs.at[i], dev))
        for i, (cond, dev) in enumerate(diag)
    ]

    middle = has_lo & has_hi
    up = g >= NG // 2
    half = up.astype(jnp.int32)
    inner_dev, outer_dev = 1 + half, 3 * half
    far_inner, far_outer = 2 - half, 3 - 3 * half
    beside = [(has_lo, g_lo), (has_hi, g_hi)]
    t_out = [
        (middle & cond, remote(ts, tr.at[g], t_ss.at[i], t_rs.at[g], (o, l)))
        for i, (cond, o) in enumerate(beside)
    ]
    t_far_out = [(middle, remote(ts, tr.at[g], t_ss.at[2], t_rs.at[g], (far_outer, l)))]
    t_in = [
        (cond & (o > 0) & (o < NG - 1), remote(ts, tr.at[o], t_ss.at[0], t_rs.at[o], (o, l)))
        for cond, o in beside
    ]
    t_in.append(
        (ends, remote(ts, tr.at[far_inner], t_ss.at[0], t_rs.at[far_inner], (far_inner, l)))
    )
    s_out, pv_out, e_out = [], [], []
    for d, o in enumerate(others):
        to_end = middle & (o == outer_dev)
        to_far = middle & (o != outer_dev)
        for cond, at in ((to_end, pl.ds(0, 1)), (to_far, pl.ds(1, 1))):
            s_out.append((cond, remote(ss.at[at], sr.at[g, at], s_ss.at[d], s_rs.at[g], (o, l))))
        for cond, at in ((to_end, pl.ds(0, 2)), (jnp.logical_not(to_end), pl.ds(2, 1))):
            pv_out.append((cond, remote(pvs.at[at], pvr.at[g, at], pv_ss.at[d], pv_rs.at[g], (o, l))))
            e_out.append((cond, remote(es.at[at], er.at[g, at], e_ss.at[d], e_rs.at[g], (o, l))))
    s_in, pv_in, e_in = [], [], []
    for k in range(NG):
        from_inner = ends & (inner_dev == k)
        from_other = (g != k) & jnp.logical_not(from_inner)
        if k in (1, 2):
            for cond, at in ((from_inner, pl.ds(0, 1)), (from_other, pl.ds(1, 1))):
                s_in.append((cond, remote(ss.at[at], sr.at[k, at], s_ss.at[0], s_rs.at[k], (k, l))))
        for cond, at in ((from_inner, pl.ds(0, 2)), (from_other, pl.ds(2, 1))):
            pv_in.append((cond, remote(pvs.at[at], pvr.at[k, at], pv_ss.at[0], pv_rs.at[k], (k, l))))
            e_in.append((cond, remote(es.at[at], er.at[k, at], e_ss.at[0], e_rs.at[k], (k, l))))

    bottom = jnp.where(g == 0, face(phz(0), 0.0), zero) + 1.0
    top = jnp.where(g == NG - 1, face(phz(CZ - 1), 0.0), zero) + 1.0
    ea[0] = bottom
    pf[0] = one
    eb[CZ - 1] = top
    qf[CZ - 1] = one

    def eliminate(i, carry):
        e, prod, ebar, qprod = carry
        j = CZ - 1 - i
        u = face(phz(i), phz(i + 1))
        v = face(phz(j), phz(j - 1))
        w = u / (u + e)
        y = v / (v + ebar)
        e = 1.0 + w * e
        ebar = 1.0 + y * ebar
        prod = prod * w
        qprod = qprod * y
        wf[i] = w
        vb[j] = y
        ea[i + 1] = e
        eb[j - 1] = ebar
        pf[i + 1] = prod
        qf[j - 1] = qprod
        return e, prod, ebar, qprod

    def eliminate3(k, carry):
        for r in range(3):
            carry = eliminate(1 + 3 * k + r, carry)
        return carry

    lax.fori_loop(0, 10, eliminate3, eliminate(0, (bottom, one, top, one)))

    def finish(k, _):
        for r in range(BZ):
            i = k * BZ + r
            d = 1.0 / (ea[i] + eb[i] - 1.0)
            dd[i] = d
            pp[i] = pf[i] * d
            qq[i] = qf[i] * d
        return 0

    lax.fori_loop(0, CZ // BZ, finish, 0)
    zs[0, 3] = pp[0]
    zs[1, 3] = qq[CZ - 1]
    ts[...] = pp[CZ - 1]
    tr[g] = ts[...]
    for cond, cp in w_out + t_out:
        pl.when(cond)(cp.start)
    pl.semaphore_wait(met, many(has_lo, has_hi))
    for cond, cp in c_out + t_far_out:
        pl.when(cond)(cp.start)


    for side, x in ((0, -1), (1, CX)):
        ph[0:CZ, PAD + x, :] = zero
        ph[CZ:CZ + 2, PAD + x, :] = zero[0:2]
        fx[:, PAD + x, :] = zero
        so[:, PAD + x, :] = xs[side, 2]
        for buf in (cin, cnx, cout, cs0):
            buf[side, 0:8] = zero[0:8]
            buf[side, 40:56] = zero[0:16]
        @pl.when(jnp.logical_not((has_xl, has_xr)[side]))
        def _():
            xr[side] = jnp.zeros((4, CZ, NY), F32)
        @pl.when(jnp.logical_not((has_lo, has_hi)[side]))
        def _():
            zr[side] = jnp.zeros((4, CX, NY), F32)
    for i, (cond, _) in enumerate(diag):
        @pl.when(jnp.logical_not(cond))
        def _():
            cr[i] = jnp.zeros((8, NY), F32)

    def prefactor(k, _):
        mask = masked(k)
        for r in range(BZ):
            z = k * BZ + r
            s0[z] = (1.0 + 0.7 * soz(z)) * (phz(z) - po[z]) * mask
        return 0

    lax.fori_loop(0, CZ // BZ, prefactor, 0)

    def plane(z):
        here = phz(z)
        right, left = phz(z, 1), phz(z, -1)
        yn, yp = next_y(here, last), prev_y(here, first)
        gx = right - left
        gy = yn - yp
        gz = phz(z + 1) - phz(z - 1)
        factor = flux_factor(gx, gy, gz, jnp.where(inner, s0[z], 0.0))
        fx[z, pl.ds(PAD, CX), :] = factor * gx
        fz[z + 1] = factor * gz
        flux_y = factor * gy
        s = soz(z)
        side = coupling(here, right) * (soz(z, 1) - s) + coupling(here, left) * (soz(z, -1) - s)
        step_y = coupling(here, yn) * (next_y(s, last) - s)
        back = jnp.where(first, coupling(here, 0.0) * s, pltpu.roll(step_y + flux_y, 1, 1))
        rh[z] = s + side + (step_y + next_y(flux_y, last) - back)

    def gather_rhs(z, sums):
        r = (
            rh[z]
            + (fx[z, pl.ds(PAD + 1, CX), :] - fx[z, pl.ds(PAD - 1, CX), :])
            + (fz[z + 2] - fz[z])
        )
        rh[z] = r
        return sums[0] + pp[z] * r, sums[1] + qq[z] * r

    def planes(k, _):
        for r in range(6):
            plane(1 + 6 * k + r)
        return 0

    lax.fori_loop(0, 5, planes, 0)

    def rows(k, sums):
        for r in range(BZ):
            sums = gather_rhs(2 + BZ * k + r, sums)
        return sums

    sums = lax.fori_loop(0, 7, rows, (zero, zero))

    for side, x in ((0, 0), (1, CX - 1)):
        near = 1 if x == 0 else CX - 2
        cin[side, 8:40] = xs[side, 0]
        cnx[side, 8:40] = xs[side, 1]
        cs0[side, 8:40] = xs[side, 3]
        cpq[side, 0] = pp[:, x, :]
        cpq[side, 1] = qq[:, x, :]
        cpq[side, 2] = pp[:, near, :]
        cpq[side, 3] = qq[:, near, :]

    for cond, cp in z_in + w_in:
        pl.when(cond)(cp.wait_recv)
    self_hi = 1.0 / face(phz(CZ - 1), zr[1, 0]) + qq[CZ - 1] + zr[1, 3]
    self_lo = 1.0 / face(phz(0), zr[0, 0]) + pp[0] + zr[0, 3]
    even = lax.rem(g, 2) == 0
    self_out = jnp.where(even, self_hi, self_lo)
    ss[0] = jnp.where(even, self_lo, self_hi)
    ss[1] = self_out
    sr[g] = ss[...]
    for cond, cp in s_out:
        pl.when(cond)(cp.start)
    own_k = ts[...] / self_out
    ph[0, pl.ds(PAD, CX), :] = zr[0, 0]
    ph[CZ + 1, pl.ds(PAD, CX), :] = zr[1, 0]
    for side, z in ((0, -1), (1, CZ)):
        gz = phz(0) - zr[side, 1] if side == 0 else zr[side, 1] - phz(CZ - 1)
        gx = phz(z, 1) - phz(z, -1)
        factor = flux_factor(gx, ydiff(zr[side, 0]), gz, jnp.where(inner, zr[side, 2], 0.0))
        fz[z + 1] = factor * gz
    plane(0)
    plane(CZ - 1)
    for z in (0, 1, CZ - 2, CZ - 1):
        sums = gather_rhs(z, sums)
    facing, away = jnp.where(up, sums[0], sums[1]), jnp.where(up, sums[1], sums[0])
    pvs[0] = facing
    pvs[1] = away
    pvs[2] = jnp.where(middle, facing - own_k * away, facing)
    pvr[g] = pvs[...]
    for cond, cp in pv_out:
        pl.when(cond)(cp.start)

    for side, x in ((0, 0), (1, CX - 1)):
        near = 1 if x == 0 else CX - 2
        for buf, which, xx in ((cin, 0, x), (cnx, 0, near)):
            buf[side, 7:8] = zr[0, which, xx:xx + 1, :]
            buf[side, 40:41] = zr[1, which, xx:xx + 1, :]
        cin[side, 6:7] = zr[0, 1, x:x + 1, :]
        cin[side, 41:42] = zr[1, 1, x:x + 1, :]
        a = cin[side, 7:47]
        cgy[side] = next_y(a, last_e) - prev_y(a, first_e)
        cgz[side] = cin[side, 8:48] - cin[side, 6:46]

    for cond, cp in x_in:
        pl.when(cond)(cp.wait_recv)
    tile_p = jnp.zeros((8, NY), F32)
    tile_q = jnp.zeros((8, NY), F32)
    for side, x in ((0, 0), (1, CX - 1)):
        near = 1 if x == 0 else CX - 2
        outer = xr[side, 0]
        cout[side, 8:40] = outer
        gin = cnx[side, 7:47] - cout[side, 7:47]
        factor = flux_factor(gin, cgy[side], cgz[side], cs0[side, 7:47])
        cfa[side] = factor
        cfz[side] = factor * cgz[side]
        g_out2 = xs[side, 0] - xr[side, 1]
        gy_out = ydiff(outer)
        f_out = flux_factor(
            g_out2, gy_out, cout[side, 9:41] - cout[side, 7:39], xr[side, 3]
        ) * jnp.where(inner, g_out2, 0.0)
        own = cfa[side, 1:33]
        d_near = -own * (xs[side, 1] - outer)
        d_edge = (
            coupling(xs[side, 0], outer) * (xr[side, 2] - xs[side, 2])
            - f_out
            + ydiff(own * cgy[side, 1:33])
            + (cfz[side, 2:34] - cfz[side, 0:32])
        )
        at, at_near = (0, 1) if side == 0 else (7, 6)
        for d, where, k in ((d_edge, at, 0), (d_near, at_near, 2)):
            tile_p = jnp.where(sub == where, jnp.sum(cpq[side, k] * d, axis=0, keepdims=True), tile_p)
            tile_q = jnp.where(sub == where, jnp.sum(cpq[side, k + 1] * d, axis=0, keepdims=True), tile_q)
        cfa[side, 0:32] = d_edge
        cfz[side, 0:32] = d_near
        cgo[side, 0] = g_out2
        cgo[side, 1] = gy_out
        for end, z in ((0, 0), (1, CZ - 1)):
            at_a, at_b = 4 * side + end, 4 * side + 2 + end
            zb = 7 if end == 0 else 40
            inz = 1 if end == 0 else CZ - 2
            w8[0, at_a:at_a + 1] = xr[side, 0, inz:inz + 1, :]
            w8[1, at_a:at_a + 1] = cgo[side, 0, z:z + 1]
            w8[2, at_a:at_a + 1] = cgo[side, 1, z:z + 1]
            w8[3, at_a:at_a + 1] = -xr[side, 3, z:z + 1, :]
            w8[0, at_b:at_b + 1] = cnx[side, zb:zb + 1]
            w8[1, at_b:at_b + 1] = cgz[side, zb - 7:zb - 6]
            w8[2, at_b:at_b + 1] = cgy[side, zb - 7:zb - 6]
            w8[3, at_b:at_b + 1] = zr[end, 2, x:x + 1, :] * (-1.0 if end == 0 else 1.0)
            for at in (at_a, at_b):
                w8[4, at:at + 1] = cpq[side, 0, z:z + 1]
                w8[5, at:at + 1] = cpq[side, 1, z:z + 1]
    carry2 = w8[1] * w8[1]
    side2 = w8[2] * w8[2]
    known2 = carry2 + side2 + 1.0
    known4 = carry2 * carry2 + side2 * side2
    scale = w8[3] * w8[1]
    base8, weight_p, weight_q = w8[0], w8[4], w8[5]
    for cond, cp in c_in:
        pl.when(cond)(cp.wait_recv)
    v = base8 - ((cr[0] + cr[1]) + (cr[2] + cr[3]))
    v2 = v * v
    inv = lax.rsqrt(known2 + v2)
    inv2 = inv * inv
    d8 = scale * inv * (0.1 + 1.2 * (known4 + v2 * v2) * (inv2 * inv2))

    def corner_rows(y):
        y = y + pltpu.roll(y, 7, 0)
        y = y + pltpu.roll(y, 6, 0)
        return jnp.where(sub == 0, y, jnp.where(sub == 7, pltpu.roll(y, 3, 0), 0.0))

    tile_p = tile_p + corner_rows(weight_p * d8)
    tile_q = tile_q + corner_rows(weight_q * d8)
    left_rows = sub < 4
    tile_facing, tile_away = jnp.where(up, tile_p, tile_q), jnp.where(up, tile_q, tile_p)
    tile_k = jnp.where(left_rows, own_k[0:8], own_k[CX - 8:CX])
    es[0] = tile_facing
    es[1] = tile_away
    es[2] = jnp.where(middle, tile_facing - tile_k * tile_away, tile_facing)
    er[g] = es[...]
    for cond, cp in e_out:
        pl.when(cond)(cp.start)
    w8[0] = d8
    for side in (0, 1):
        for end, z in ((0, 0), (1, CZ - 1)):
            at_a, at_b = 4 * side + end, 4 * side + 2 + end
            cfa[side, z:z + 1] = cfa[side, z:z + 1] + w8[0, at_a:at_a + 1] + w8[0, at_b:at_b + 1]
    for side, x in ((0, 0), (1, CX - 1)):
        near = 1 if x == 0 else CX - 2
        rh[:, x, :] = rh[:, x, :] + cfa[side, 0:32]
        rh[:, near, :] = rh[:, near, :] + cfz[side, 0:32]

    ee[0] = rh[0]
    bb[CZ - 1] = rh[CZ - 1]

    def sweep(i, carry):
        f, b = carry
        j = CZ - 1 - i
        f = rh[i] + wf[i - 1] * f
        b = rh[j] + vb[j + 1] * b
        ee[i] = f
        bb[j] = b
        return f, b

    def sweep3(k, carry):
        for r in range(3):
            carry = sweep(2 + 3 * k + r, carry)
        return carry

    lax.fori_loop(0, 10, sweep3, sweep(1, (rh[0], rh[CZ - 1])))

    def local(k, _):
        for r in range(BZ):
            z = k * BZ + r
            ee[z] = (ee[z] + bb[z] - rh[z]) * dd[z]
        return 0

    lax.fori_loop(0, CZ // BZ, local, 0)

    for cond, cp in t_in + s_in + pv_in:
        pl.when(cond)(cp.wait_recv)
    t_far = tr[far_inner]
    t_own = tr[inner_dev]
    k1 = t_far / sr[far_inner, 1]
    m1 = 1.0 / (sr[inner_dev, 0] - t_far * k1)
    k2 = t_own * m1
    m2 = 1.0 / (ss[1] - t_own * k2)
    b1 = pvr[far_inner, 2] + k1 * pvr[far_outer, 2] - pvr[inner_dev, 0]
    b2 = pvr[inner_dev, 1] - pvr[outer_dev, 2]
    tile_k1 = jnp.where(left_rows, k1[0:8], k1[CX - 8:CX])
    for cond, cp in e_in:
        pl.when(cond)(cp.wait_recv)

    def widen(tile):
        full = jnp.concatenate([tile, jnp.zeros((CX - 16, NY), F32), tile], axis=0)
        return jnp.where((row < 2) | (row >= CX - 2), full, 0.0)

    b1 = b1 + widen(er[far_inner, 2] + tile_k1 * er[far_outer, 2] - er[inner_dev, 0])
    b2 = b2 + widen(er[inner_dev, 1] - er[outer_dev, 2])
    r2 = (b2 + k2 * b1) * m2
    r1 = (b1 + t_own * r2) * m1
    below = jnp.where(g == 3, r2, jnp.where(g == 2, r1, jnp.where(g == 1, -r2, 0.0)))
    above = jnp.where(g == 0, -r2, jnp.where(g == 1, -r1, jnp.where(g == 2, r2, 0.0)))

    def close(k, _):
        for r in range(BZ):
            z = k * BZ + r
            out[z] = ee[z] + pp[z] * below - qq[z] * above
        return 0

    lax.fori_loop(0, CZ // BZ, close, 0)

    for cond, cp in x_out + z_out + c_out + w_out + t_out + t_far_out + s_out + pv_out + e_out:
        pl.when(cond)(cp.wait_send)


def step(phase, old, solute, blocks, count):
    def buf(*shape):
        return pltpu.VMEM(shape + (NY,), F32)

    slab = buf(CZ, CX)
    dma = pltpu.SemaphoreType.DMA
    return pl.pallas_call(
        kernel,
        out_shape=pltpu.VMEM((CZ, CX, NY), F32),
        in_specs=[pl.BlockSpec(memory_space=pl.ANY)] * 5,
        out_specs=pl.BlockSpec(memory_space=pltpu.VMEM),
        scratch_shapes=[
            buf(CZ + 2, ROW), buf(CZ, ROW), slab, slab, buf(CZ, ROW), buf(CZ + 2, CX),
            slab, slab, slab, slab, slab, slab, slab, slab, slab, slab, slab, slab,
            buf(2, 56), buf(2, 56), buf(2, 56), buf(2, 56),
            buf(2, 40), buf(2, 40), buf(2, 40), buf(2, 40), buf(2, 4, CZ),
            buf(2, 2, CZ), buf(6, 8),
            buf(2, 4, CZ), buf(2, 4, CZ),
            buf(2, 4, CX), buf(2, 4, CX),
            buf(4, 8), buf(4, 8),
            buf(CX), buf(NG, CX),
            buf(2, CX), buf(NG, 2, CX),
            buf(3, CX), buf(NG, 3, CX),
            buf(3, 8), buf(NG, 3, 8),
            pltpu.SMEM((1, 1, 6), jnp.int32),
            pltpu.SMEM((1, 1), jnp.int32),
            dma((5,)),
            dma((2,)), dma((2,)),
            dma((4,)), dma((4,)),
            dma((4,)), dma((4,)),
            dma((3,)), dma((NG,)),
            dma((3,)), dma((NG,)),
            dma((3,)), dma((NG,)),
            dma((3,)), dma((NG,)),
            pltpu.SemaphoreType.REGULAR,
        ],
        compiler_params=pltpu.CompilerParams(
            collective_id=0, has_side_effects=True, vmem_limit_bytes=66000000
        ),
    )(phase, old, solute, blocks, count)


def solution(mesh):
    spec = P("growth", "lateral", None)
    return jax.shard_map(
        step,
        mesh=mesh,
        in_specs=(spec, spec, spec, spec, P("growth", "lateral")),
        out_specs=spec,
        check_vma=False,
    )
```

```python
import jax
import jax.numpy as jnp
from jax import lax
from jax.experimental import pallas as pl
from jax.experimental.pallas import tpu as pltpu
from jax.sharding import PartitionSpec as P

BZ = 4
MESH = pl.DeviceIdType.MESH
NG = 4
NL = 32
CZ = 32
CX = 32
NY = 128
PAD = 8
ROW = CX + 2 * PAD
F32 = jnp.float32


def flux_factor(gx, gy, gz, pre):
    x2 = gx * gx
    y2 = gy * gy
    z2 = gz * gz
    inv = lax.rsqrt(x2 + y2 + z2 + 1.0)
    inv2 = inv * inv
    quartic = x2 * x2 + y2 * y2 + z2 * z2
    return pre * inv * (0.1 + 1.2 * quartic * (inv2 * inv2))


def next_y(a, last):
    return jnp.where(last, 0.0, pltpu.roll(a, NY - 1, 1))


def prev_y(a, first):
    return jnp.where(first, 0.0, pltpu.roll(a, 1, 1))


def kernel(
    phase, old, solute, blocks, count, ee, pp, qq, below_out, above_out,
    ph, so, po, s0, fx, fz, rh, bb, wf, pf, vb, qf, dd, ea, eb,
    cin, cnx, cout, cs0, cgy, cgz, cfa, cfz, cpq, cgo, w8,
    xs, xr, zs, zr, cs, cr, ts, tr, ss, sr, pvs, pvr, es, er, blk, cnt,
    in_sem, x_ss, x_rs, z_ss, z_rs, c_ss, c_rs, t_ss, t_rs, s_ss, s_rs, pv_ss, pv_rs, e_ss, e_rs, met,
):
    g = lax.axis_index("growth")
    l = lax.axis_index("lateral")
    has_lo, has_hi = g > 0, g < NG - 1
    has_xl, has_xr = l > 0, l < NL - 1
    g_lo, g_hi = jnp.maximum(g - 1, 0), jnp.minimum(g + 1, NG - 1)
    l_lo, l_hi = jnp.maximum(l - 1, 0), jnp.minimum(l + 1, NL - 1)
    others = [lax.rem(g + d, NG) for d in (2, 1, 3)]

    barrier = pltpu.get_barrier_semaphore()

    def greet(cond, dev):
        @pl.when(cond)
        def _():
            pl.semaphore_signal(barrier, inc=1, device_id=dev, device_id_type=MESH)

    diag = [
        (has_lo & has_xl, (g_lo, l_lo)),
        (has_lo & has_xr, (g_lo, l_hi)),
        (has_hi & has_xl, (g_hi, l_lo)),
        (has_hi & has_xr, (g_hi, l_hi)),
    ]
    ends = jnp.logical_not(has_lo & has_hi)
    greet(has_lo, (g_lo, l))
    greet(has_hi, (g_hi, l))
    greet(has_xl, (g, l_lo))
    greet(has_xr, (g, l_hi))
    greet(ends, (NG - 1 - g, l))

    ins = [
        pltpu.make_async_copy(phase, ph.at[pl.ds(1, CZ), pl.ds(PAD, CX), :], in_sem.at[0]),
        pltpu.make_async_copy(old, po, in_sem.at[1]),
        pltpu.make_async_copy(solute, so.at[:, pl.ds(PAD, CX), :], in_sem.at[2]),
        pltpu.make_async_copy(blocks, blk, in_sem.at[3]),
        pltpu.make_async_copy(count, cnt, in_sem.at[4]),
    ]
    for c in ins:
        c.start()

    lane = lax.broadcasted_iota(jnp.int32, (CX, NY), 1)
    row = lax.broadcasted_iota(jnp.int32, (CX, NY), 0)
    first, last = lane == 0, lane == NY - 1
    inner = (row > 0) & (row < CX - 1)
    zero = jnp.zeros((CX, NY), F32)
    one = zero + 1.0
    EXT = 40
    lane_e = lax.broadcasted_iota(jnp.int32, (EXT, NY), 1)
    first_e, last_e = lane_e == 0, lane_e == NY - 1

    def face(a, b):
        return 220.0 - 90.0 * (a + b)

    def coupling(a, b):
        return 0.055 - 0.0225 * (a + b)

    def ydiff(a):
        return next_y(a, last) - prev_y(a, first)

    def phz(z, off=0):
        return ph[z + 1, pl.ds(PAD + off, CX), :]

    def soz(z, off=0):
        return so[z, pl.ds(PAD + off, CX), :]

    for c in ins:
        c.wait()

    live = [jnp.where(s < cnt[0, 0], blk[0, 0, s], -1) for s in range(6)]

    def masked(k):
        hit = k == live[0]
        for b in live[1:]:
            hit = hit | (k == b)
        return jnp.where(hit, 0.25, 0.0)

    column_mask = masked(row // BZ)
    sub = lax.broadcasted_iota(jnp.int32, (8, NY), 0)
    for side, x in ((0, 0), (1, CX - 1)):
        near = 1 if x == 0 else CX - 2
        here, s = ph[1:CZ + 1, PAD + x, :], so[:, PAD + x, :]
        xs[side, 0] = here
        xs[side, 1] = ph[1:CZ + 1, PAD + near, :]
        xs[side, 2] = s
        xs[side, 3] = (1.0 + 0.7 * s) * (here - po[:, x, :]) * column_mask
    for side, z in ((0, 0), (1, CZ - 1)):
        zs[side, 0] = phz(z)
        zs[side, 1] = phz(1 if z == 0 else CZ - 2)
        zs[side, 2] = (1.0 + 0.7 * soz(z)) * (phz(z) - po[z]) * masked(jnp.int32(z // BZ))
        for right, x in ((0, 0), (1, CX - 1)):
            slot = 3 - (2 * side + right)
            want = (sub // 4 == slot % 2) & (sub % 2 == slot // 2)
            corner = jnp.broadcast_to(phz(z)[x:x + 1], (8, NY))
            cs[2 * side + right] = jnp.where(want, corner, 0.0)

    def many(*conds):
        return sum(c.astype(jnp.int32) for c in conds)

    pl.semaphore_wait(barrier, many(has_lo, has_hi, has_xl, has_xr, ends))

    def remote(src, dst, ss, rs, dev):
        return pltpu.make_async_remote_copy(
            src_ref=src, dst_ref=dst, send_sem=ss, recv_sem=rs, device_id=dev, device_id_type=MESH
        )

    x_out = [
        (has_xl, remote(xs.at[0], xr.at[1], x_ss.at[0], x_rs.at[1], (g, l_lo))),
        (has_xr, remote(xs.at[1], xr.at[0], x_ss.at[1], x_rs.at[0], (g, l_hi))),
    ]
    z_out = [
        (has_lo, remote(zs.at[0, 0:3], zr.at[1, 0:3], z_ss.at[0], z_rs.at[1], (g_lo, l))),
        (has_hi, remote(zs.at[1, 0:3], zr.at[0, 0:3], z_ss.at[1], z_rs.at[0], (g_hi, l))),
    ]
    w_out = [
        (has_lo, remote(zs.at[0, 3], zr.at[1, 3], z_ss.at[2], z_rs.at[3], (g_lo, l))),
        (has_hi, remote(zs.at[1, 3], zr.at[0, 3], z_ss.at[3], z_rs.at[2], (g_hi, l))),
    ]
    w_in = [
        (has_lo, remote(zs.at[1, 3], zr.at[0, 3], z_ss.at[3], z_rs.at[2], (g_lo, l))),
        (has_hi, remote(zs.at[0, 3], zr.at[1, 3], z_ss.at[2], z_rs.at[3], (g_hi, l))),
    ]
    c_out = [
        (cond, remote(cs.at[i], cr.at[3 - i], c_ss.at[i], c_rs.at[3 - i], dev))
        for i, (cond, dev) in enumerate(diag)
    ]
    for i, (cond, o) in enumerate(((has_lo, g_lo), (has_hi, g_hi))):
        @pl.when(cond)
        def _():
            pl.semaphore_signal(met, inc=1, device_id=(o, l), device_id_type=MESH)
    for cond, cp in z_out + x_out:
        pl.when(cond)(cp.start)
    x_in = [
        (has_xl, remote(xs.at[1], xr.at[0], x_ss.at[1], x_rs.at[0], (g, l_lo))),
        (has_xr, remote(xs.at[0], xr.at[1], x_ss.at[0], x_rs.at[1], (g, l_hi))),
    ]
    z_in = [
        (has_lo, remote(zs.at[1, 0:3], zr.at[0, 0:3], z_ss.at[1], z_rs.at[0], (g_lo, l))),
        (has_hi, remote(zs.at[0, 0:3], zr.at[1, 0:3], z_ss.at[0], z_rs.at[1], (g_hi, l))),
    ]
    c_in = [
        (cond, remote(cs.at[3 - i], cr.at[i], c_ss.at[3 - i], c_rs.at[i], dev))
        for i, (cond, dev) in enumerate(diag)
    ]

    middle = has_lo & has_hi
    up = g >= NG // 2
    half = up.astype(jnp.int32)
    inner_dev, outer_dev = 1 + half, 3 * half
    far_inner, far_outer = 2 - half, 3 - 3 * half
    beside = [(has_lo, g_lo), (has_hi, g_hi)]
    t_out = [
        (middle & cond, remote(ts, tr.at[g], t_ss.at[i], t_rs.at[g], (o, l)))
        for i, (cond, o) in enumerate(beside)
    ]
    t_far_out = [(middle, remote(ts, tr.at[g], t_ss.at[2], t_rs.at[g], (far_outer, l)))]
    t_in = [
        (cond & (o > 0) & (o < NG - 1), remote(ts, tr.at[o], t_ss.at[0], t_rs.at[o], (o, l)))
        for cond, o in beside
    ]
    t_in.append(
        (ends, remote(ts, tr.at[far_inner], t_ss.at[0], t_rs.at[far_inner], (far_inner, l)))
    )
    s_out, pv_out, e_out = [], [], []
    for d, o in enumerate(others):
        to_end = middle & (o == outer_dev)
        to_far = middle & (o != outer_dev)
        for cond, at in ((to_end, pl.ds(0, 1)), (to_far, pl.ds(1, 1))):
            s_out.append((cond, remote(ss.at[at], sr.at[g, at], s_ss.at[d], s_rs.at[g], (o, l))))
        for cond, at in ((to_end, pl.ds(0, 2)), (jnp.logical_not(to_end), pl.ds(2, 1))):
            pv_out.append((cond, remote(pvs.at[at], pvr.at[g, at], pv_ss.at[d], pv_rs.at[g], (o, l))))
            e_out.append((cond, remote(es.at[at], er.at[g, at], e_ss.at[d], e_rs.at[g], (o, l))))
    s_in, pv_in, e_in = [], [], []
    for k in range(NG):
        from_inner = ends & (inner_dev == k)
        from_other = (g != k) & jnp.logical_not(from_inner)
        if k in (1, 2):
            for cond, at in ((from_inner, pl.ds(0, 1)), (from_other, pl.ds(1, 1))):
                s_in.append((cond, remote(ss.at[at], sr.at[k, at], s_ss.at[0], s_rs.at[k], (k, l))))
        for cond, at in ((from_inner, pl.ds(0, 2)), (from_other, pl.ds(2, 1))):
            pv_in.append((cond, remote(pvs.at[at], pvr.at[k, at], pv_ss.at[0], pv_rs.at[k], (k, l))))
            e_in.append((cond, remote(es.at[at], er.at[k, at], e_ss.at[0], e_rs.at[k], (k, l))))

    bottom = jnp.where(g == 0, face(phz(0), 0.0), zero) + 1.0
    top = jnp.where(g == NG - 1, face(phz(CZ - 1), 0.0), zero) + 1.0
    ea[0] = bottom
    pf[0] = one
    eb[CZ - 1] = top
    qf[CZ - 1] = one

    def eliminate(i, carry):
        e, prod, ebar, qprod = carry
        j = CZ - 1 - i
        u = face(phz(i), phz(i + 1))
        v = face(phz(j), phz(j - 1))
        w = u / (u + e)
        y = v / (v + ebar)
        e = 1.0 + w * e
        ebar = 1.0 + y * ebar
        prod = prod * w
        qprod = qprod * y
        wf[i] = w
        vb[j] = y
        ea[i + 1] = e
        eb[j - 1] = ebar
        pf[i + 1] = prod
        qf[j - 1] = qprod
        return e, prod, ebar, qprod

    def eliminate3(k, carry):
        for r in range(3):
            carry = eliminate(1 + 3 * k + r, carry)
        return carry

    lax.fori_loop(0, 10, eliminate3, eliminate(0, (bottom, one, top, one)))

    def finish(k, _):
        for r in range(BZ):
            i = k * BZ + r
            d = 1.0 / (ea[i] + eb[i] - 1.0)
            dd[i] = d
            pp[i] = pf[i] * d
            qq[i] = qf[i] * d
        return 0

    lax.fori_loop(0, CZ // BZ, finish, 0)
    zs[0, 3] = pp[0]
    zs[1, 3] = qq[CZ - 1]
    ts[...] = pp[CZ - 1]
    tr[g] = ts[...]
    for cond, cp in w_out + t_out:
        pl.when(cond)(cp.start)
    pl.semaphore_wait(met, many(has_lo, has_hi))
    for cond, cp in c_out + t_far_out:
        pl.when(cond)(cp.start)


    for side, x in ((0, -1), (1, CX)):
        ph[0:CZ, PAD + x, :] = zero
        ph[CZ:CZ + 2, PAD + x, :] = zero[0:2]
        fx[:, PAD + x, :] = zero
        so[:, PAD + x, :] = xs[side, 2]
        for buf in (cin, cnx, cout, cs0):
            buf[side, 0:8] = zero[0:8]
            buf[side, 40:56] = zero[0:16]
        @pl.when(jnp.logical_not((has_xl, has_xr)[side]))
        def _():
            xr[side] = jnp.zeros((4, CZ, NY), F32)
        @pl.when(jnp.logical_not((has_lo, has_hi)[side]))
        def _():
            zr[side] = jnp.zeros((4, CX, NY), F32)
    for i, (cond, _) in enumerate(diag):
        @pl.when(jnp.logical_not(cond))
        def _():
            cr[i] = jnp.zeros((8, NY), F32)

    def prefactor(k, _):
        mask = masked(k)
        for r in range(BZ):
            z = k * BZ + r
            s0[z] = (1.0 + 0.7 * soz(z)) * (phz(z) - po[z]) * mask
        return 0

    lax.fori_loop(0, CZ // BZ, prefactor, 0)

    def plane(z):
        here = phz(z)
        right, left = phz(z, 1), phz(z, -1)
        yn, yp = next_y(here, last), prev_y(here, first)
        gx = right - left
        gy = yn - yp
        gz = phz(z + 1) - phz(z - 1)
        factor = flux_factor(gx, gy, gz, jnp.where(inner, s0[z], 0.0))
        fx[z, pl.ds(PAD, CX), :] = factor * gx
        fz[z + 1] = factor * gz
        flux_y = factor * gy
        s = soz(z)
        side = coupling(here, right) * (soz(z, 1) - s) + coupling(here, left) * (soz(z, -1) - s)
        step_y = coupling(here, yn) * (next_y(s, last) - s)
        back = jnp.where(first, coupling(here, 0.0) * s, pltpu.roll(step_y + flux_y, 1, 1))
        rh[z] = s + side + (step_y + next_y(flux_y, last) - back)

    def gather_rhs(z, sums):
        r = (
            rh[z]
            + (fx[z, pl.ds(PAD + 1, CX), :] - fx[z, pl.ds(PAD - 1, CX), :])
            + (fz[z + 2] - fz[z])
        )
        rh[z] = r
        return sums[0] + pp[z] * r, sums[1] + qq[z] * r

    def planes(k, _):
        for r in range(6):
            plane(1 + 6 * k + r)
        return 0

    lax.fori_loop(0, 5, planes, 0)

    def rows(k, sums):
        for r in range(BZ):
            sums = gather_rhs(2 + BZ * k + r, sums)
        return sums

    sums = lax.fori_loop(0, 7, rows, (zero, zero))

    for side, x in ((0, 0), (1, CX - 1)):
        near = 1 if x == 0 else CX - 2
        cin[side, 8:40] = xs[side, 0]
        cnx[side, 8:40] = xs[side, 1]
        cs0[side, 8:40] = xs[side, 3]
        cpq[side, 0] = pp[:, x, :]
        cpq[side, 1] = qq[:, x, :]
        cpq[side, 2] = pp[:, near, :]
        cpq[side, 3] = qq[:, near, :]

    for cond, cp in z_in + w_in:
        pl.when(cond)(cp.wait_recv)
    self_hi = 1.0 / face(phz(CZ - 1), zr[1, 0]) + qq[CZ - 1] + zr[1, 3]
    self_lo = 1.0 / face(phz(0), zr[0, 0]) + pp[0] + zr[0, 3]
    even = lax.rem(g, 2) == 0
    self_out = jnp.where(even, self_hi, self_lo)
    ss[0] = jnp.where(even, self_lo, self_hi)
    ss[1] = self_out
    sr[g] = ss[...]
    for cond, cp in s_out:
        pl.when(cond)(cp.start)
    own_k = ts[...] / self_out
    ph[0, pl.ds(PAD, CX), :] = zr[0, 0]
    ph[CZ + 1, pl.ds(PAD, CX), :] = zr[1, 0]
    for side, z in ((0, -1), (1, CZ)):
        gz = phz(0) - zr[side, 1] if side == 0 else zr[side, 1] - phz(CZ - 1)
        gx = phz(z, 1) - phz(z, -1)
        factor = flux_factor(gx, ydiff(zr[side, 0]), gz, jnp.where(inner, zr[side, 2], 0.0))
        fz[z + 1] = factor * gz
    plane(0)
    plane(CZ - 1)
    for z in (0, 1, CZ - 2, CZ - 1):
        sums = gather_rhs(z, sums)
    facing, away = jnp.where(up, sums[0], sums[1]), jnp.where(up, sums[1], sums[0])
    pvs[0] = facing
    pvs[1] = away
    pvs[2] = jnp.where(middle, facing - own_k * away, facing)
    pvr[g] = pvs[...]
    for cond, cp in pv_out:
        pl.when(cond)(cp.start)

    for side, x in ((0, 0), (1, CX - 1)):
        near = 1 if x == 0 else CX - 2
        for buf, which, xx in ((cin, 0, x), (cnx, 0, near)):
            buf[side, 7:8] = zr[0, which, xx:xx + 1, :]
            buf[side, 40:41] = zr[1, which, xx:xx + 1, :]
        cin[side, 6:7] = zr[0, 1, x:x + 1, :]
        cin[side, 41:42] = zr[1, 1, x:x + 1, :]
        a = cin[side, 7:47]
        cgy[side] = next_y(a, last_e) - prev_y(a, first_e)
        cgz[side] = cin[side, 8:48] - cin[side, 6:46]

    for side, x in ((0, 0), (1, CX - 1)):
        for end, z in ((0, 0), (1, CZ - 1)):
            at_a, at_b = 4 * side + end, 4 * side + 2 + end
            zb = 7 if end == 0 else 40
            w8[0, at_b:at_b + 1] = cnx[side, zb:zb + 1]
            w8[1, at_b:at_b + 1] = cgz[side, zb - 7:zb - 6]
            w8[2, at_b:at_b + 1] = cgy[side, zb - 7:zb - 6]
            w8[3, at_b:at_b + 1] = zr[end, 2, x:x + 1, :] * (-1.0 if end == 0 else 1.0)
            for at in (at_a, at_b):
                w8[4, at:at + 1] = cpq[side, 0, z:z + 1]
                w8[5, at:at + 1] = cpq[side, 1, z:z + 1]

    for cond, cp in x_in:
        pl.when(cond)(cp.wait_recv)
    tile_p = jnp.zeros((8, NY), F32)
    tile_q = jnp.zeros((8, NY), F32)
    for side, x in ((0, 0), (1, CX - 1)):
        near = 1 if x == 0 else CX - 2
        outer = xr[side, 0]
        cout[side, 8:40] = outer
        gin = cnx[side, 7:47] - cout[side, 7:47]
        factor = flux_factor(gin, cgy[side], cgz[side], cs0[side, 7:47])
        cfa[side] = factor
        cfz[side] = factor * cgz[side]
        g_out2 = xs[side, 0] - xr[side, 1]
        gy_out = ydiff(outer)
        f_out = flux_factor(
            g_out2, gy_out, cout[side, 9:41] - cout[side, 7:39], xr[side, 3]
        ) * jnp.where(inner, g_out2, 0.0)
        own = cfa[side, 1:33]
        d_near = -own * (xs[side, 1] - outer)
        d_edge = (
            coupling(xs[side, 0], outer) * (xr[side, 2] - xs[side, 2])
            - f_out
            + ydiff(own * cgy[side, 1:33])
            + (cfz[side, 2:34] - cfz[side, 0:32])
        )
        at, at_near = (0, 1) if side == 0 else (7, 6)
        for d, where, k in ((d_edge, at, 0), (d_near, at_near, 2)):
            tile_p = jnp.where(sub == where, jnp.sum(cpq[side, k] * d, axis=0, keepdims=True), tile_p)
            tile_q = jnp.where(sub == where, jnp.sum(cpq[side, k + 1] * d, axis=0, keepdims=True), tile_q)
        cfa[side, 0:32] = d_edge
        cfz[side, 0:32] = d_near
        cgo[side, 0] = g_out2
        cgo[side, 1] = gy_out
        for end, z in ((0, 0), (1, CZ - 1)):
            at_a, at_b = 4 * side + end, 4 * side + 2 + end
            inz = 1 if end == 0 else CZ - 2
            w8[0, at_a:at_a + 1] = xr[side, 0, inz:inz + 1, :]
            w8[1, at_a:at_a + 1] = cgo[side, 0, z:z + 1]
            w8[2, at_a:at_a + 1] = cgo[side, 1, z:z + 1]
            w8[3, at_a:at_a + 1] = -xr[side, 3, z:z + 1, :]
    carry2 = w8[1] * w8[1]
    side2 = w8[2] * w8[2]
    known2 = carry2 + side2 + 1.0
    known4 = carry2 * carry2 + side2 * side2
    scale = w8[3] * w8[1]
    base8, weight_p, weight_q = w8[0], w8[4], w8[5]
    for cond, cp in c_in:
        pl.when(cond)(cp.wait_recv)
    v = base8 - ((cr[0] + cr[1]) + (cr[2] + cr[3]))
    v2 = v * v
    inv = lax.rsqrt(known2 + v2)
    inv2 = inv * inv
    d8 = scale * inv * (0.1 + 1.2 * (known4 + v2 * v2) * (inv2 * inv2))

    def corner_rows(y):
        y = y + pltpu.roll(y, 7, 0)
        y = y + pltpu.roll(y, 6, 0)
        return jnp.where(sub == 0, y, jnp.where(sub == 7, pltpu.roll(y, 3, 0), 0.0))

    tile_p = tile_p + corner_rows(weight_p * d8)
    tile_q = tile_q + corner_rows(weight_q * d8)
    left_rows = sub < 4
    tile_facing, tile_away = jnp.where(up, tile_p, tile_q), jnp.where(up, tile_q, tile_p)
    tile_k = jnp.where(left_rows, own_k[0:8], own_k[CX - 8:CX])
    es[0] = tile_facing
    es[1] = tile_away
    es[2] = jnp.where(middle, tile_facing - tile_k * tile_away, tile_facing)
    er[g] = es[...]
    for cond, cp in e_out:
        pl.when(cond)(cp.start)
    w8[0] = d8
    for side in (0, 1):
        for end, z in ((0, 0), (1, CZ - 1)):
            at_a, at_b = 4 * side + end, 4 * side + 2 + end
            cfa[side, z:z + 1] = cfa[side, z:z + 1] + w8[0, at_a:at_a + 1] + w8[0, at_b:at_b + 1]
    for side, x in ((0, 0), (1, CX - 1)):
        near = 1 if x == 0 else CX - 2
        rh[:, x, :] = rh[:, x, :] + cfa[side, 0:32]
        rh[:, near, :] = rh[:, near, :] + cfz[side, 0:32]

    ee[0] = rh[0]
    bb[CZ - 1] = rh[CZ - 1]

    def sweep(i, carry):
        f, b = carry
        j = CZ - 1 - i
        f = rh[i] + wf[i - 1] * f
        b = rh[j] + vb[j + 1] * b
        ee[i] = f
        bb[j] = b
        return f, b

    def sweep3(k, carry):
        for r in range(3):
            carry = sweep(2 + 3 * k + r, carry)
        return carry

    lax.fori_loop(0, 10, sweep3, sweep(1, (rh[0], rh[CZ - 1])))

    def local(k, _):
        for r in range(BZ):
            z = k * BZ + r
            ee[z] = (ee[z] + bb[z] - rh[z]) * dd[z]
        return 0

    lax.fori_loop(0, CZ // BZ, local, 0)

    for cond, cp in t_in + s_in + pv_in:
        pl.when(cond)(cp.wait_recv)
    t_far = tr[far_inner]
    t_own = tr[inner_dev]
    k1 = t_far / sr[far_inner, 1]
    m1 = 1.0 / (sr[inner_dev, 0] - t_far * k1)
    k2 = t_own * m1
    m2 = 1.0 / (ss[1] - t_own * k2)
    b1 = pvr[far_inner, 2] + k1 * pvr[far_outer, 2] - pvr[inner_dev, 0]
    b2 = pvr[inner_dev, 1] - pvr[outer_dev, 2]
    tile_k1 = jnp.where(left_rows, k1[0:8], k1[CX - 8:CX])
    for cond, cp in e_in:
        pl.when(cond)(cp.wait_recv)

    def widen(tile):
        full = jnp.concatenate([tile, jnp.zeros((CX - 16, NY), F32), tile], axis=0)
        return jnp.where((row < 2) | (row >= CX - 2), full, 0.0)

    b1 = b1 + widen(er[far_inner, 2] + tile_k1 * er[far_outer, 2] - er[inner_dev, 0])
    b2 = b2 + widen(er[inner_dev, 1] - er[outer_dev, 2])
    r2 = (b2 + k2 * b1) * m2
    r1 = (b1 + t_own * r2) * m1
    below = jnp.where(g == 3, r2, jnp.where(g == 2, r1, jnp.where(g == 1, -r2, 0.0)))
    above = jnp.where(g == 0, -r2, jnp.where(g == 1, -r1, jnp.where(g == 2, r2, 0.0)))

    below_out[...] = below
    above_out[...] = above

    for cond, cp in x_out + z_out + c_out + w_out + t_out + t_far_out + s_out + pv_out + e_out:
        pl.when(cond)(cp.wait_send)


def step(phase, old, solute, blocks, count):
    def buf(*shape):
        return pltpu.VMEM(shape + (NY,), F32)

    slab = buf(CZ, CX)
    dma = pltpu.SemaphoreType.DMA
    parts = pl.pallas_call(
        kernel,
        out_shape=[pltpu.VMEM((CZ, CX, NY), F32)] * 3 + [pltpu.VMEM((CX, NY), F32)] * 2,
        in_specs=[pl.BlockSpec(memory_space=pl.ANY)] * 5,
        out_specs=[pl.BlockSpec(memory_space=pltpu.VMEM)] * 5,
        scratch_shapes=[
            buf(CZ + 2, ROW), buf(CZ, ROW), slab, slab, buf(CZ, ROW), buf(CZ + 2, CX),
            slab, slab, slab, slab, slab, slab, slab, slab, slab,
            buf(2, 56), buf(2, 56), buf(2, 56), buf(2, 56),
            buf(2, 40), buf(2, 40), buf(2, 40), buf(2, 40), buf(2, 4, CZ),
            buf(2, 2, CZ), buf(6, 8),
            buf(2, 4, CZ), buf(2, 4, CZ),
            buf(2, 4, CX), buf(2, 4, CX),
            buf(4, 8), buf(4, 8),
            buf(CX), buf(NG, CX),
            buf(2, CX), buf(NG, 2, CX),
            buf(3, CX), buf(NG, 3, CX),
            buf(3, 8), buf(NG, 3, 8),
            pltpu.SMEM((1, 1, 6), jnp.int32),
            pltpu.SMEM((1, 1), jnp.int32),
            dma((5,)),
            dma((2,)), dma((2,)),
            dma((4,)), dma((4,)),
            dma((4,)), dma((4,)),
            dma((3,)), dma((NG,)),
            dma((3,)), dma((NG,)),
            dma((3,)), dma((NG,)),
            dma((3,)), dma((NG,)),
            pltpu.SemaphoreType.REGULAR,
        ],
        compiler_params=pltpu.CompilerParams(
            collective_id=0, has_side_effects=True, vmem_limit_bytes=65400000
        ),
    )(phase, old, solute, blocks, count)
    chunks = 4
    deep = CZ // chunks

    def close(ee, pp, qq, below, above, dst, stage, sems):
        lo, hi = below[...], above[...]
        cps = []
        for c in range(chunks):
            for z in range(c * deep, (c + 1) * deep):
                stage[z] = ee[z] + pp[z] * lo - qq[z] * hi
            at = pl.ds(c * deep, deep)
            cps.append(pltpu.make_async_copy(stage.at[at], dst.at[at], sems.at[c]))
            cps[-1].start()
        for cp in cps:
            cp.wait()

    return pl.pallas_call(
        close,
        out_shape=jax.ShapeDtypeStruct((CZ, CX, NY), F32),
        in_specs=[pl.BlockSpec(memory_space=pltpu.VMEM)] * 5,
        out_specs=pl.BlockSpec(memory_space=pl.ANY),
        scratch_shapes=[slab, dma((chunks,))],
        compiler_params=pltpu.CompilerParams(vmem_limit_bytes=4194304),
    )(*[pltpu.with_memory_space_constraint(a, pltpu.VMEM) for a in parts])


def solution(mesh):
    spec = P("growth", "lateral", None)
    return jax.shard_map(
        step,
        mesh=mesh,
        in_specs=(spec, spec, spec, spec, P("growth", "lateral")),
        out_specs=spec,
        check_vma=False,
    )
```

```python
import jax
import jax.numpy as jnp
from jax import lax
from jax.experimental import pallas as pl
from jax.experimental.pallas import tpu as pltpu
from jax.sharding import PartitionSpec as P

BZ = 4
MESH = pl.DeviceIdType.MESH
NG = 4
NL = 32
CZ = 32
CX = 32
NY = 128
PAD = 8
ROW = CX + 2 * PAD
F32 = jnp.float32


def flux_factor(gx, gy, gz, pre):
    x2 = gx * gx
    y2 = gy * gy
    z2 = gz * gz
    inv = lax.rsqrt(x2 + y2 + z2 + 1.0)
    inv2 = inv * inv
    quartic = x2 * x2 + y2 * y2 + z2 * z2
    return pre * inv * (0.1 + 1.2 * quartic * (inv2 * inv2))


def next_y(a, last):
    return jnp.where(last, 0.0, pltpu.roll(a, NY - 1, 1))


def prev_y(a, first):
    return jnp.where(first, 0.0, pltpu.roll(a, 1, 1))


def kernel(
    phase, old, solute, blocks, count, ee, pp, qq, below_out, above_out,
    ph, so, po, s0, fx, fz, rh, bb, wf, pf, vb, qf, dd, ea, eb,
    cin, cnx, cout, cs0, cgy, cgz, cfa, cfz, cpq, cgo, w8,
    xs, xr, zs, zr, cs, cr, ts, tr, ss, sr, pvs, pvr, es, er, blk, cnt,
    in_sem, x_ss, x_rs, z_ss, z_rs, c_ss, c_rs, t_ss, t_rs, s_ss, s_rs, pv_ss, pv_rs, e_ss, e_rs, met,
):
    g = lax.axis_index("growth")
    l = lax.axis_index("lateral")
    has_lo, has_hi = g > 0, g < NG - 1
    has_xl, has_xr = l > 0, l < NL - 1
    g_lo, g_hi = jnp.maximum(g - 1, 0), jnp.minimum(g + 1, NG - 1)
    l_lo, l_hi = jnp.maximum(l - 1, 0), jnp.minimum(l + 1, NL - 1)
    others = [lax.rem(g + d, NG) for d in (2, 1, 3)]

    barrier = pltpu.get_barrier_semaphore()

    def greet(cond, dev):
        @pl.when(cond)
        def _():
            pl.semaphore_signal(barrier, inc=1, device_id=dev, device_id_type=MESH)

    diag = [
        (has_lo & has_xl, (g_lo, l_lo)),
        (has_lo & has_xr, (g_lo, l_hi)),
        (has_hi & has_xl, (g_hi, l_lo)),
        (has_hi & has_xr, (g_hi, l_hi)),
    ]
    ends = jnp.logical_not(has_lo & has_hi)
    greet(has_lo, (g_lo, l))
    greet(has_hi, (g_hi, l))
    greet(has_xl, (g, l_lo))
    greet(has_xr, (g, l_hi))
    greet(ends, (NG - 1 - g, l))

    ins = [
        pltpu.make_async_copy(phase, ph.at[pl.ds(1, CZ), pl.ds(PAD, CX), :], in_sem.at[0]),
        pltpu.make_async_copy(old, po, in_sem.at[1]),
        pltpu.make_async_copy(solute, so.at[:, pl.ds(PAD, CX), :], in_sem.at[2]),
        pltpu.make_async_copy(blocks, blk, in_sem.at[3]),
        pltpu.make_async_copy(count, cnt, in_sem.at[4]),
    ]
    for c in ins:
        c.start()

    lane = lax.broadcasted_iota(jnp.int32, (CX, NY), 1)
    row = lax.broadcasted_iota(jnp.int32, (CX, NY), 0)
    first, last = lane == 0, lane == NY - 1
    inner = (row > 0) & (row < CX - 1)
    zero = jnp.zeros((CX, NY), F32)
    one = zero + 1.0
    EXT = 40
    lane_e = lax.broadcasted_iota(jnp.int32, (EXT, NY), 1)
    first_e, last_e = lane_e == 0, lane_e == NY - 1

    def face(a, b):
        return 220.0 - 90.0 * (a + b)

    def coupling(a, b):
        return 0.055 - 0.0225 * (a + b)

    def ydiff(a):
        return next_y(a, last) - prev_y(a, first)

    def phz(z, off=0):
        return ph[z + 1, pl.ds(PAD + off, CX), :]

    def soz(z, off=0):
        return so[z, pl.ds(PAD + off, CX), :]

    for c in ins:
        c.wait()

    live = [jnp.where(s < cnt[0, 0], blk[0, 0, s], -1) for s in range(6)]

    def masked(k):
        hit = k == live[0]
        for b in live[1:]:
            hit = hit | (k == b)
        return jnp.where(hit, 0.25, 0.0)

    column_mask = masked(row // BZ)
    sub = lax.broadcasted_iota(jnp.int32, (8, NY), 0)
    for side, x in ((0, 0), (1, CX - 1)):
        near = 1 if x == 0 else CX - 2
        here, s = ph[1:CZ + 1, PAD + x, :], so[:, PAD + x, :]
        xs[side, 0] = here
        xs[side, 1] = ph[1:CZ + 1, PAD + near, :]
        xs[side, 2] = s
        xs[side, 3] = (1.0 + 0.7 * s) * (here - po[:, x, :]) * column_mask
    for side, z in ((0, 0), (1, CZ - 1)):
        zs[side, 0] = phz(z)
        zs[side, 1] = phz(1 if z == 0 else CZ - 2)
        zs[side, 2] = (1.0 + 0.7 * soz(z)) * (phz(z) - po[z]) * masked(jnp.int32(z // BZ))
        for right, x in ((0, 0), (1, CX - 1)):
            slot = 3 - (2 * side + right)
            want = (sub // 4 == slot % 2) & (sub % 2 == slot // 2)
            corner = jnp.broadcast_to(phz(z)[x:x + 1], (8, NY))
            cs[2 * side + right] = jnp.where(want, corner, 0.0)

    def many(*conds):
        return sum(c.astype(jnp.int32) for c in conds)

    pl.semaphore_wait(barrier, many(has_lo, has_hi, has_xl, has_xr, ends))

    def remote(src, dst, ss, rs, dev):
        return pltpu.make_async_remote_copy(
            src_ref=src, dst_ref=dst, send_sem=ss, recv_sem=rs, device_id=dev, device_id_type=MESH
        )

    x_out = [
        (has_xl, remote(xs.at[0], xr.at[1], x_ss.at[0], x_rs.at[1], (g, l_lo))),
        (has_xr, remote(xs.at[1], xr.at[0], x_ss.at[1], x_rs.at[0], (g, l_hi))),
    ]
    z_out = [
        (has_lo, remote(zs.at[0, 0:3], zr.at[1, 0:3], z_ss.at[0], z_rs.at[1], (g_lo, l))),
        (has_hi, remote(zs.at[1, 0:3], zr.at[0, 0:3], z_ss.at[1], z_rs.at[0], (g_hi, l))),
    ]
    w_out = [
        (has_lo, remote(zs.at[0, 3], zr.at[1, 3], z_ss.at[2], z_rs.at[3], (g_lo, l))),
        (has_hi, remote(zs.at[1, 3], zr.at[0, 3], z_ss.at[3], z_rs.at[2], (g_hi, l))),
    ]
    w_in = [
        (has_lo, remote(zs.at[1, 3], zr.at[0, 3], z_ss.at[3], z_rs.at[2], (g_lo, l))),
        (has_hi, remote(zs.at[0, 3], zr.at[1, 3], z_ss.at[2], z_rs.at[3], (g_hi, l))),
    ]
    c_out = [
        (cond, remote(cs.at[i], cr.at[3 - i], c_ss.at[i], c_rs.at[3 - i], dev))
        for i, (cond, dev) in enumerate(diag)
    ]
    for i, (cond, o) in enumerate(((has_lo, g_lo), (has_hi, g_hi))):
        @pl.when(cond)
        def _():
            pl.semaphore_signal(met, inc=1, device_id=(o, l), device_id_type=MESH)
    for cond, cp in z_out + x_out:
        pl.when(cond)(cp.start)
    x_in = [
        (has_xl, remote(xs.at[1], xr.at[0], x_ss.at[1], x_rs.at[0], (g, l_lo))),
        (has_xr, remote(xs.at[0], xr.at[1], x_ss.at[0], x_rs.at[1], (g, l_hi))),
    ]
    z_in = [
        (has_lo, remote(zs.at[1, 0:3], zr.at[0, 0:3], z_ss.at[1], z_rs.at[0], (g_lo, l))),
        (has_hi, remote(zs.at[0, 0:3], zr.at[1, 0:3], z_ss.at[0], z_rs.at[1], (g_hi, l))),
    ]
    c_in = [
        (cond, remote(cs.at[3 - i], cr.at[i], c_ss.at[3 - i], c_rs.at[i], dev))
        for i, (cond, dev) in enumerate(diag)
    ]

    middle = has_lo & has_hi
    up = g >= NG // 2
    half = up.astype(jnp.int32)
    inner_dev, outer_dev = 1 + half, 3 * half
    far_inner, far_outer = 2 - half, 3 - 3 * half
    beside = [(has_lo, g_lo), (has_hi, g_hi)]
    t_out = [
        (middle & cond, remote(ts, tr.at[g], t_ss.at[i], t_rs.at[g], (o, l)))
        for i, (cond, o) in enumerate(beside)
    ]
    t_far_out = [(middle, remote(ts, tr.at[g], t_ss.at[2], t_rs.at[g], (far_outer, l)))]
    t_in = [
        (cond & (o > 0) & (o < NG - 1), remote(ts, tr.at[o], t_ss.at[0], t_rs.at[o], (o, l)))
        for cond, o in beside
    ]
    t_in.append(
        (ends, remote(ts, tr.at[far_inner], t_ss.at[0], t_rs.at[far_inner], (far_inner, l)))
    )
    s_out, pv_out, e_out = [], [], []
    for d, o in enumerate(others):
        to_end = middle & (o == outer_dev)
        to_far = middle & (o != outer_dev)
        for cond, at in ((to_end, pl.ds(0, 1)), (to_far, pl.ds(1, 1))):
            s_out.append((cond, remote(ss.at[at], sr.at[g, at], s_ss.at[d], s_rs.at[g], (o, l))))
        for cond, at in ((to_end, pl.ds(0, 2)), (jnp.logical_not(to_end), pl.ds(2, 1))):
            pv_out.append((cond, remote(pvs.at[at], pvr.at[g, at], pv_ss.at[d], pv_rs.at[g], (o, l))))
            e_out.append((cond, remote(es.at[at], er.at[g, at], e_ss.at[d], e_rs.at[g], (o, l))))
    s_in, pv_in, e_in = [], [], []
    for k in range(NG):
        from_inner = ends & (inner_dev == k)
        from_other = (g != k) & jnp.logical_not(from_inner)
        if k in (1, 2):
            for cond, at in ((from_inner, pl.ds(0, 1)), (from_other, pl.ds(1, 1))):
                s_in.append((cond, remote(ss.at[at], sr.at[k, at], s_ss.at[0], s_rs.at[k], (k, l))))
        for cond, at in ((from_inner, pl.ds(0, 2)), (from_other, pl.ds(2, 1))):
            pv_in.append((cond, remote(pvs.at[at], pvr.at[k, at], pv_ss.at[0], pv_rs.at[k], (k, l))))
            e_in.append((cond, remote(es.at[at], er.at[k, at], e_ss.at[0], e_rs.at[k], (k, l))))

    bottom = jnp.where(g == 0, face(phz(0), 0.0), zero) + 1.0
    top = jnp.where(g == NG - 1, face(phz(CZ - 1), 0.0), zero) + 1.0
    ea[0] = bottom
    pf[0] = one
    eb[CZ - 1] = top
    qf[CZ - 1] = one

    def eliminate(i, carry):
        e, prod, ebar, qprod = carry
        j = CZ - 1 - i
        u = face(phz(i), phz(i + 1))
        v = face(phz(j), phz(j - 1))
        w = u / (u + e)
        y = v / (v + ebar)
        e = 1.0 + w * e
        ebar = 1.0 + y * ebar
        prod = prod * w
        qprod = qprod * y
        wf[i] = w
        vb[j] = y
        ea[i + 1] = e
        eb[j - 1] = ebar
        pf[i + 1] = prod
        qf[j - 1] = qprod
        return e, prod, ebar, qprod

    def eliminate3(k, carry):
        for r in range(3):
            carry = eliminate(1 + 3 * k + r, carry)
        return carry

    lax.fori_loop(0, 10, eliminate3, eliminate(0, (bottom, one, top, one)))

    def finish(k, _):
        for r in range(BZ):
            i = k * BZ + r
            d = 1.0 / (ea[i] + eb[i] - 1.0)
            dd[i] = d
            pp[i] = pf[i] * d
            qq[i] = qf[i] * d
        return 0

    lax.fori_loop(0, CZ // BZ, finish, 0)
    zs[0, 3] = pp[0]
    zs[1, 3] = qq[CZ - 1]
    ts[...] = pp[CZ - 1]
    tr[g] = ts[...]
    for cond, cp in w_out + t_out:
        pl.when(cond)(cp.start)
    pl.semaphore_wait(met, many(has_lo, has_hi))
    for cond, cp in c_out + t_far_out:
        pl.when(cond)(cp.start)


    for side, x in ((0, -1), (1, CX)):
        ph[0:CZ, PAD + x, :] = zero
        ph[CZ:CZ + 2, PAD + x, :] = zero[0:2]
        fx[:, PAD + x, :] = zero
        so[:, PAD + x, :] = xs[side, 2]
        for buf in (cin, cnx, cout, cs0):
            buf[side, 0:8] = zero[0:8]
            buf[side, 40:56] = zero[0:16]
        @pl.when(jnp.logical_not((has_xl, has_xr)[side]))
        def _():
            xr[side] = jnp.zeros((4, CZ, NY), F32)
        @pl.when(jnp.logical_not((has_lo, has_hi)[side]))
        def _():
            zr[side] = jnp.zeros((4, CX, NY), F32)
    for i, (cond, _) in enumerate(diag):
        @pl.when(jnp.logical_not(cond))
        def _():
            cr[i] = jnp.zeros((8, NY), F32)

    def prefactor(k, _):
        mask = masked(k)
        for r in range(BZ):
            z = k * BZ + r
            s0[z] = (1.0 + 0.7 * soz(z)) * (phz(z) - po[z]) * mask
        return 0

    lax.fori_loop(0, CZ // BZ, prefactor, 0)

    def plane(z):
        here = phz(z)
        right, left = phz(z, 1), phz(z, -1)
        yn, yp = next_y(here, last), prev_y(here, first)
        gx = right - left
        gy = yn - yp
        gz = phz(z + 1) - phz(z - 1)
        factor = flux_factor(gx, gy, gz, jnp.where(inner, s0[z], 0.0))
        fx[z, pl.ds(PAD, CX), :] = factor * gx
        fz[z + 1] = factor * gz
        flux_y = factor * gy
        s = soz(z)
        side = coupling(here, right) * (soz(z, 1) - s) + coupling(here, left) * (soz(z, -1) - s)
        step_y = coupling(here, yn) * (next_y(s, last) - s)
        back = jnp.where(first, coupling(here, 0.0) * s, pltpu.roll(step_y + flux_y, 1, 1))
        rh[z] = s + side + (step_y + next_y(flux_y, last) - back)

    def gather_rhs(z, sums):
        r = (
            rh[z]
            + (fx[z, pl.ds(PAD + 1, CX), :] - fx[z, pl.ds(PAD - 1, CX), :])
            + (fz[z + 2] - fz[z])
        )
        rh[z] = r
        return sums[0] + pp[z] * r, sums[1] + qq[z] * r

    def planes(k, _):
        for r in range(6):
            plane(1 + 6 * k + r)
        return 0

    lax.fori_loop(0, 5, planes, 0)

    def rows(k, sums):
        for r in range(BZ):
            sums = gather_rhs(2 + BZ * k + r, sums)
        return sums

    sums = lax.fori_loop(0, 7, rows, (zero, zero))

    for side, x in ((0, 0), (1, CX - 1)):
        near = 1 if x == 0 else CX - 2
        cin[side, 8:40] = xs[side, 0]
        cnx[side, 8:40] = xs[side, 1]
        cs0[side, 8:40] = xs[side, 3]
        cpq[side, 0] = pp[:, x, :]
        cpq[side, 1] = qq[:, x, :]
        cpq[side, 2] = pp[:, near, :]
        cpq[side, 3] = qq[:, near, :]

    for cond, cp in z_in + w_in:
        pl.when(cond)(cp.wait_recv)
    self_hi = 1.0 / face(phz(CZ - 1), zr[1, 0]) + qq[CZ - 1] + zr[1, 3]
    self_lo = 1.0 / face(phz(0), zr[0, 0]) + pp[0] + zr[0, 3]
    even = lax.rem(g, 2) == 0
    self_out = jnp.where(even, self_hi, self_lo)
    ss[0] = jnp.where(even, self_lo, self_hi)
    ss[1] = self_out
    sr[g] = ss[...]
    for cond, cp in s_out:
        pl.when(cond)(cp.start)
    own_k = ts[...] / self_out
    ph[0, pl.ds(PAD, CX), :] = zr[0, 0]
    ph[CZ + 1, pl.ds(PAD, CX), :] = zr[1, 0]
    for side, z in ((0, -1), (1, CZ)):
        gz = phz(0) - zr[side, 1] if side == 0 else zr[side, 1] - phz(CZ - 1)
        gx = phz(z, 1) - phz(z, -1)
        factor = flux_factor(gx, ydiff(zr[side, 0]), gz, jnp.where(inner, zr[side, 2], 0.0))
        fz[z + 1] = factor * gz
    plane(0)
    plane(CZ - 1)
    for z in (0, 1, CZ - 2, CZ - 1):
        sums = gather_rhs(z, sums)
    facing, away = jnp.where(up, sums[0], sums[1]), jnp.where(up, sums[1], sums[0])
    pvs[0] = facing
    pvs[1] = away
    pvs[2] = jnp.where(middle, facing - own_k * away, facing)
    pvr[g] = pvs[...]
    for cond, cp in pv_out:
        pl.when(cond)(cp.start)

    for side, x in ((0, 0), (1, CX - 1)):
        near = 1 if x == 0 else CX - 2
        for buf, which, xx in ((cin, 0, x), (cnx, 0, near)):
            buf[side, 7:8] = zr[0, which, xx:xx + 1, :]
            buf[side, 40:41] = zr[1, which, xx:xx + 1, :]
        cin[side, 6:7] = zr[0, 1, x:x + 1, :]
        cin[side, 41:42] = zr[1, 1, x:x + 1, :]
        a = cin[side, 7:47]
        cgy[side] = next_y(a, last_e) - prev_y(a, first_e)
        cgz[side] = cin[side, 8:48] - cin[side, 6:46]

    for side, x in ((0, 0), (1, CX - 1)):
        for end, z in ((0, 0), (1, CZ - 1)):
            at_a, at_b = 4 * side + end, 4 * side + 2 + end
            zb = 7 if end == 0 else 40
            w8[0, at_b:at_b + 1] = cnx[side, zb:zb + 1]
            w8[1, at_b:at_b + 1] = cgz[side, zb - 7:zb - 6]
            w8[2, at_b:at_b + 1] = cgy[side, zb - 7:zb - 6]
            w8[3, at_b:at_b + 1] = zr[end, 2, x:x + 1, :] * (-1.0 if end == 0 else 1.0)
            for at in (at_a, at_b):
                w8[4, at:at + 1] = cpq[side, 0, z:z + 1]
                w8[5, at:at + 1] = cpq[side, 1, z:z + 1]

    for cond, cp in x_in:
        pl.when(cond)(cp.wait_recv)
    tile_p = jnp.zeros((8, NY), F32)
    tile_q = jnp.zeros((8, NY), F32)
    for side, x in ((0, 0), (1, CX - 1)):
        near = 1 if x == 0 else CX - 2
        outer = xr[side, 0]
        cout[side, 8:40] = outer
        gin = cnx[side, 7:47] - cout[side, 7:47]
        factor = flux_factor(gin, cgy[side], cgz[side], cs0[side, 7:47])
        cfa[side] = factor
        cfz[side] = factor * cgz[side]
        g_out2 = xs[side, 0] - xr[side, 1]
        gy_out = ydiff(outer)
        f_out = flux_factor(
            g_out2, gy_out, cout[side, 9:41] - cout[side, 7:39], xr[side, 3]
        ) * jnp.where(inner, g_out2, 0.0)
        own = cfa[side, 1:33]
        d_near = -own * (xs[side, 1] - outer)
        d_edge = (
            coupling(xs[side, 0], outer) * (xr[side, 2] - xs[side, 2])
            - f_out
            + ydiff(own * cgy[side, 1:33])
            + (cfz[side, 2:34] - cfz[side, 0:32])
        )
        at, at_near = (0, 1) if side == 0 else (7, 6)
        for d, where, k in ((d_edge, at, 0), (d_near, at_near, 2)):
            tile_p = jnp.where(sub == where, jnp.sum(cpq[side, k] * d, axis=0, keepdims=True), tile_p)
            tile_q = jnp.where(sub == where, jnp.sum(cpq[side, k + 1] * d, axis=0, keepdims=True), tile_q)
        cfa[side, 0:32] = d_edge
        cfz[side, 0:32] = d_near
        cgo[side, 0] = g_out2
        cgo[side, 1] = gy_out
        for end, z in ((0, 0), (1, CZ - 1)):
            at_a, at_b = 4 * side + end, 4 * side + 2 + end
            inz = 1 if end == 0 else CZ - 2
            w8[0, at_a:at_a + 1] = xr[side, 0, inz:inz + 1, :]
            w8[1, at_a:at_a + 1] = cgo[side, 0, z:z + 1]
            w8[2, at_a:at_a + 1] = cgo[side, 1, z:z + 1]
            w8[3, at_a:at_a + 1] = -xr[side, 3, z:z + 1, :]
    carry2 = w8[1] * w8[1]
    side2 = w8[2] * w8[2]
    known2 = carry2 + side2 + 1.0
    known4 = carry2 * carry2 + side2 * side2
    scale = w8[3] * w8[1]
    base8, weight_p, weight_q = w8[0], w8[4], w8[5]
    for cond, cp in c_in:
        pl.when(cond)(cp.wait_recv)
    v = base8 - ((cr[0] + cr[1]) + (cr[2] + cr[3]))
    v2 = v * v
    inv = lax.rsqrt(known2 + v2)
    inv2 = inv * inv
    d8 = scale * inv * (0.1 + 1.2 * (known4 + v2 * v2) * (inv2 * inv2))

    def corner_rows(y):
        y = y + pltpu.roll(y, 7, 0)
        y = y + pltpu.roll(y, 6, 0)
        return jnp.where(sub == 0, y, jnp.where(sub == 7, pltpu.roll(y, 3, 0), 0.0))

    tile_p = tile_p + corner_rows(weight_p * d8)
    tile_q = tile_q + corner_rows(weight_q * d8)
    left_rows = sub < 4
    tile_facing, tile_away = jnp.where(up, tile_p, tile_q), jnp.where(up, tile_q, tile_p)
    tile_k = jnp.where(left_rows, own_k[0:8], own_k[CX - 8:CX])
    es[0] = tile_facing
    es[1] = tile_away
    es[2] = jnp.where(middle, tile_facing - tile_k * tile_away, tile_facing)
    er[g] = es[...]
    for cond, cp in e_out:
        pl.when(cond)(cp.start)
    w8[0] = d8
    for side in (0, 1):
        for end, z in ((0, 0), (1, CZ - 1)):
            at_a, at_b = 4 * side + end, 4 * side + 2 + end
            cfa[side, z:z + 1] = cfa[side, z:z + 1] + w8[0, at_a:at_a + 1] + w8[0, at_b:at_b + 1]
    for side, x in ((0, 0), (1, CX - 1)):
        near = 1 if x == 0 else CX - 2
        rh[:, x, :] = rh[:, x, :] + cfa[side, 0:32]
        rh[:, near, :] = rh[:, near, :] + cfz[side, 0:32]

    ee[0] = rh[0]
    bb[CZ - 1] = rh[CZ - 1]

    def sweep(i, carry):
        f, b = carry
        j = CZ - 1 - i
        f = rh[i] + wf[i - 1] * f
        b = rh[j] + vb[j + 1] * b
        ee[i] = f
        bb[j] = b
        return f, b

    def sweep3(k, carry):
        for r in range(3):
            carry = sweep(2 + 3 * k + r, carry)
        return carry

    lax.fori_loop(0, 10, sweep3, sweep(1, (rh[0], rh[CZ - 1])))

    def local(k, _):
        for r in range(BZ):
            z = k * BZ + r
            ee[z] = (ee[z] + bb[z] - rh[z]) * dd[z]
        return 0

    lax.fori_loop(0, CZ // BZ, local, 0)

    for cond, cp in t_in + s_in + pv_in:
        pl.when(cond)(cp.wait_recv)
    t_far = tr[far_inner]
    t_own = tr[inner_dev]
    k1 = t_far / sr[far_inner, 1]
    m1 = 1.0 / (sr[inner_dev, 0] - t_far * k1)
    k2 = t_own * m1
    m2 = 1.0 / (ss[1] - t_own * k2)
    b1 = pvr[far_inner, 2] + k1 * pvr[far_outer, 2] - pvr[inner_dev, 0]
    b2 = pvr[inner_dev, 1] - pvr[outer_dev, 2]
    tile_k1 = jnp.where(left_rows, k1[0:8], k1[CX - 8:CX])
    for cond, cp in x_out + z_out + c_out + w_out + t_out + t_far_out + s_out + pv_out + e_out:
        pl.when(cond)(cp.wait_send)
    for cond, cp in e_in:
        pl.when(cond)(cp.wait_recv)

    def widen(tile):
        full = jnp.concatenate([tile, jnp.zeros((CX - 16, NY), F32), tile], axis=0)
        return jnp.where((row < 2) | (row >= CX - 2), full, 0.0)

    b1 = b1 + widen(er[far_inner, 2] + tile_k1 * er[far_outer, 2] - er[inner_dev, 0])
    b2 = b2 + widen(er[inner_dev, 1] - er[outer_dev, 2])
    r2 = (b2 + k2 * b1) * m2
    r1 = (b1 + t_own * r2) * m1
    below = jnp.where(g == 3, r2, jnp.where(g == 2, r1, jnp.where(g == 1, -r2, 0.0)))
    above = jnp.where(g == 0, -r2, jnp.where(g == 1, -r1, jnp.where(g == 2, r2, 0.0)))

    below_out[...] = below
    above_out[...] = above


def step(phase, old, solute, blocks, count):
    def buf(*shape):
        return pltpu.VMEM(shape + (NY,), F32)

    slab = buf(CZ, CX)
    dma = pltpu.SemaphoreType.DMA
    parts = pl.pallas_call(
        kernel,
        out_shape=[pltpu.VMEM((CZ, CX, NY), F32)] * 3 + [pltpu.VMEM((CX, NY), F32)] * 2,
        in_specs=[pl.BlockSpec(memory_space=pl.ANY)] * 5,
        out_specs=[pl.BlockSpec(memory_space=pltpu.VMEM)] * 5,
        scratch_shapes=[
            buf(CZ + 2, ROW), buf(CZ, ROW), slab, slab, buf(CZ, ROW), buf(CZ + 2, CX),
            slab, slab, slab, slab, slab, slab, slab, slab, slab,
            buf(2, 56), buf(2, 56), buf(2, 56), buf(2, 56),
            buf(2, 40), buf(2, 40), buf(2, 40), buf(2, 40), buf(2, 4, CZ),
            buf(2, 2, CZ), buf(6, 8),
            buf(2, 4, CZ), buf(2, 4, CZ),
            buf(2, 4, CX), buf(2, 4, CX),
            buf(4, 8), buf(4, 8),
            buf(CX), buf(NG, CX),
            buf(2, CX), buf(NG, 2, CX),
            buf(3, CX), buf(NG, 3, CX),
            buf(3, 8), buf(NG, 3, 8),
            pltpu.SMEM((1, 1, 6), jnp.int32),
            pltpu.SMEM((1, 1), jnp.int32),
            dma((5,)),
            dma((2,)), dma((2,)),
            dma((4,)), dma((4,)),
            dma((4,)), dma((4,)),
            dma((3,)), dma((NG,)),
            dma((3,)), dma((NG,)),
            dma((3,)), dma((NG,)),
            dma((3,)), dma((NG,)),
            pltpu.SemaphoreType.REGULAR,
        ],
        compiler_params=pltpu.CompilerParams(
            collective_id=0, has_side_effects=True, vmem_limit_bytes=65400000
        ),
    )(phase, old, solute, blocks, count)
    chunks = 4
    deep = CZ // chunks

    def close(ee, pp, qq, below, above, dst, stage, sems):
        lo, hi = below[...], above[...]
        cps = []
        for c in range(chunks):
            for z in range(c * deep, (c + 1) * deep):
                stage[z] = ee[z] + pp[z] * lo - qq[z] * hi
            at = pl.ds(c * deep, deep)
            cps.append(pltpu.make_async_copy(stage.at[at], dst.at[at], sems.at[c]))
            cps[-1].start()
        for cp in cps:
            cp.wait()

    return pl.pallas_call(
        close,
        out_shape=jax.ShapeDtypeStruct((CZ, CX, NY), F32),
        in_specs=[pl.BlockSpec(memory_space=pltpu.VMEM)] * 5,
        out_specs=pl.BlockSpec(memory_space=pl.ANY),
        scratch_shapes=[slab, dma((chunks,))],
        compiler_params=pltpu.CompilerParams(vmem_limit_bytes=4194304),
    )(*[pltpu.with_memory_space_constraint(a, pltpu.VMEM) for a in parts])


def solution(mesh):
    spec = P("growth", "lateral", None)
    return jax.shard_map(
        step,
        mesh=mesh,
        in_specs=(spec, spec, spec, spec, P("growth", "lateral")),
        out_specs=spec,
        check_vma=False,
    )
```

```python
import jax
import jax.numpy as jnp
from jax import lax
from jax.experimental import pallas as pl
from jax.experimental.pallas import tpu as pltpu
from jax.sharding import PartitionSpec as P

BZ = 4
MESH = pl.DeviceIdType.MESH
NG = 4
NL = 32
CZ = 32
CX = 32
NY = 128
PAD = 8
ROW = CX + 2 * PAD
F32 = jnp.float32


def flux_factor(gx, gy, gz, pre):
    x2 = gx * gx
    y2 = gy * gy
    z2 = gz * gz
    inv = lax.rsqrt(x2 + y2 + z2 + 1.0)
    inv2 = inv * inv
    quartic = x2 * x2 + y2 * y2 + z2 * z2
    return pre * inv * (0.1 + 1.2 * quartic * (inv2 * inv2))


def next_y(a, last):
    return jnp.where(last, 0.0, pltpu.roll(a, NY - 1, 1))


def prev_y(a, first):
    return jnp.where(first, 0.0, pltpu.roll(a, 1, 1))


def kernel(
    phase, old, solute, blocks, count, ee, pp, qq, below_out, above_out,
    ph, so, po, s0, fx, fz, rh, bb, wf, pf, vb, qf, dd, ea, eb,
    cin, cnx, cout, cs0, cgy, cgz, cfa, cfz, cpq, cgo, w8,
    xs, xr, zs, zr, cs, cr, ts, tr, ss, sr, pvs, pvr, es, er, blk, cnt,
    in_sem, x_ss, x_rs, z_ss, z_rs, c_ss, c_rs, t_ss, t_rs, s_ss, s_rs, pv_ss, pv_rs, e_ss, e_rs, met,
):
    g = lax.axis_index("growth")
    l = lax.axis_index("lateral")
    has_lo, has_hi = g > 0, g < NG - 1
    has_xl, has_xr = l > 0, l < NL - 1
    g_lo, g_hi = jnp.maximum(g - 1, 0), jnp.minimum(g + 1, NG - 1)
    l_lo, l_hi = jnp.maximum(l - 1, 0), jnp.minimum(l + 1, NL - 1)
    others = [lax.rem(g + d, NG) for d in (2, 3, 1)]

    barrier = pltpu.get_barrier_semaphore()

    def greet(cond, dev):
        @pl.when(cond)
        def _():
            pl.semaphore_signal(barrier, inc=1, device_id=dev, device_id_type=MESH)

    diag = [
        (has_lo & has_xl, (g_lo, l_lo)),
        (has_lo & has_xr, (g_lo, l_hi)),
        (has_hi & has_xl, (g_hi, l_lo)),
        (has_hi & has_xr, (g_hi, l_hi)),
    ]
    ends = jnp.logical_not(has_lo & has_hi)
    greet(has_lo, (g_lo, l))
    greet(has_hi, (g_hi, l))
    greet(has_xl, (g, l_lo))
    greet(has_xr, (g, l_hi))
    greet(ends, (NG - 1 - g, l))

    ins = [
        pltpu.make_async_copy(phase, ph.at[pl.ds(1, CZ), pl.ds(PAD, CX), :], in_sem.at[0]),
        pltpu.make_async_copy(old, po, in_sem.at[1]),
        pltpu.make_async_copy(solute, so.at[:, pl.ds(PAD, CX), :], in_sem.at[2]),
        pltpu.make_async_copy(blocks, blk, in_sem.at[3]),
        pltpu.make_async_copy(count, cnt, in_sem.at[4]),
    ]
    for c in ins:
        c.start()

    lane = lax.broadcasted_iota(jnp.int32, (CX, NY), 1)
    row = lax.broadcasted_iota(jnp.int32, (CX, NY), 0)
    first, last = lane == 0, lane == NY - 1
    inner = (row > 0) & (row < CX - 1)
    zero = jnp.zeros((CX, NY), F32)
    one = zero + 1.0
    EXT = 40
    lane_e = lax.broadcasted_iota(jnp.int32, (EXT, NY), 1)
    first_e, last_e = lane_e == 0, lane_e == NY - 1

    def face(a, b):
        return 220.0 - 90.0 * (a + b)

    def coupling(a, b):
        return 0.055 - 0.0225 * (a + b)

    def ydiff(a):
        return next_y(a, last) - prev_y(a, first)

    def phz(z, off=0):
        return ph[z + 1, pl.ds(PAD + off, CX), :]

    def soz(z, off=0):
        return so[z, pl.ds(PAD + off, CX), :]

    for c in ins:
        c.wait()

    live = [jnp.where(s < cnt[0, 0], blk[0, 0, s], -1) for s in range(6)]

    def masked(k):
        hit = k == live[0]
        for b in live[1:]:
            hit = hit | (k == b)
        return jnp.where(hit, 0.25, 0.0)

    column_mask = masked(row // BZ)
    sub = lax.broadcasted_iota(jnp.int32, (8, NY), 0)
    for side, x in ((0, 0), (1, CX - 1)):
        near = 1 if x == 0 else CX - 2
        here, s = ph[1:CZ + 1, PAD + x, :], so[:, PAD + x, :]
        xs[side, 0] = here
        xs[side, 1] = ph[1:CZ + 1, PAD + near, :]
        xs[side, 2] = s
        xs[side, 3] = (1.0 + 0.7 * s) * (here - po[:, x, :]) * column_mask
    for side, z in ((0, 0), (1, CZ - 1)):
        zs[side, 0] = phz(z)
        zs[side, 1] = phz(1 if z == 0 else CZ - 2)
        zs[side, 2] = (1.0 + 0.7 * soz(z)) * (phz(z) - po[z]) * masked(jnp.int32(z // BZ))
        for right, x in ((0, 0), (1, CX - 1)):
            cs[2 * side + right] = phz(z)[x:x + 1]

    def many(*conds):
        return sum(c.astype(jnp.int32) for c in conds)

    pl.semaphore_wait(barrier, many(has_lo, has_hi, has_xl, has_xr, ends))

    def remote(src, dst, ss, rs, dev):
        return pltpu.make_async_remote_copy(
            src_ref=src, dst_ref=dst, send_sem=ss, recv_sem=rs, device_id=dev, device_id_type=MESH
        )

    x_out = [
        (has_xl, remote(xs.at[0], xr.at[1], x_ss.at[0], x_rs.at[1], (g, l_lo))),
        (has_xr, remote(xs.at[1], xr.at[0], x_ss.at[1], x_rs.at[0], (g, l_hi))),
    ]
    z_out = [
        (has_lo, remote(zs.at[0, 0:3], zr.at[1, 0:3], z_ss.at[0], z_rs.at[1], (g_lo, l))),
        (has_hi, remote(zs.at[1, 0:3], zr.at[0, 0:3], z_ss.at[1], z_rs.at[0], (g_hi, l))),
    ]
    w_out = [
        (has_lo, remote(zs.at[0, 3], zr.at[1, 3], z_ss.at[2], z_rs.at[3], (g_lo, l))),
        (has_hi, remote(zs.at[1, 3], zr.at[0, 3], z_ss.at[3], z_rs.at[2], (g_hi, l))),
    ]
    w_in = [
        (has_lo, remote(zs.at[1, 3], zr.at[0, 3], z_ss.at[3], z_rs.at[2], (g_lo, l))),
        (has_hi, remote(zs.at[0, 3], zr.at[1, 3], z_ss.at[2], z_rs.at[3], (g_hi, l))),
    ]
    c_out = [
        (cond, remote(cs.at[i], cr.at[3 - i], c_ss.at[i], c_rs.at[3 - i], dev))
        for i, (cond, dev) in enumerate(diag)
    ]
    for i, (cond, o) in enumerate(((has_lo, g_lo), (has_hi, g_hi))):
        @pl.when(cond)
        def _():
            pl.semaphore_signal(met, inc=1, device_id=(o, l), device_id_type=MESH)
    for cond, cp in z_out + x_out:
        pl.when(cond)(cp.start)
    x_in = [
        (has_xl, remote(xs.at[1], xr.at[0], x_ss.at[1], x_rs.at[0], (g, l_lo))),
        (has_xr, remote(xs.at[0], xr.at[1], x_ss.at[0], x_rs.at[1], (g, l_hi))),
    ]
    z_in = [
        (has_lo, remote(zs.at[1, 0:3], zr.at[0, 0:3], z_ss.at[1], z_rs.at[0], (g_lo, l))),
        (has_hi, remote(zs.at[0, 0:3], zr.at[1, 0:3], z_ss.at[0], z_rs.at[1], (g_hi, l))),
    ]
    c_in = [
        (cond, remote(cs.at[3 - i], cr.at[i], c_ss.at[3 - i], c_rs.at[i], dev))
        for i, (cond, dev) in enumerate(diag)
    ]

    middle = has_lo & has_hi
    up = g >= NG // 2
    half = up.astype(jnp.int32)
    inner_dev, outer_dev = 1 + half, 3 * half
    far_inner, far_outer = 2 - half, 3 - 3 * half
    beside = [(has_lo, g_lo), (has_hi, g_hi)]
    t_out = [
        (middle & cond, remote(ts, tr.at[g], t_ss.at[i], t_rs.at[g], (o, l)))
        for i, (cond, o) in enumerate(beside)
    ]
    t_far_out = [(middle, remote(ts, tr.at[g], t_ss.at[2], t_rs.at[g], (far_outer, l)))]
    t_in = [
        (cond & (o > 0) & (o < NG - 1), remote(ts, tr.at[o], t_ss.at[0], t_rs.at[o], (o, l)))
        for cond, o in beside
    ]
    t_in.append(
        (ends, remote(ts, tr.at[far_inner], t_ss.at[0], t_rs.at[far_inner], (far_inner, l)))
    )
    s_out, pv_out, e_out = [], [], []
    for d, o in enumerate(others):
        to_end = middle & (o == outer_dev)
        to_far = middle & (o != outer_dev)
        for cond, at in ((to_end, pl.ds(0, 1)), (to_far, pl.ds(1, 1))):
            s_out.append((cond, remote(ss.at[at], sr.at[g, at], s_ss.at[d], s_rs.at[g], (o, l))))
        for cond, at in ((to_end, pl.ds(0, 2)), (jnp.logical_not(to_end), pl.ds(2, 1))):
            pv_out.append((cond, remote(pvs.at[at], pvr.at[g, at], pv_ss.at[d], pv_rs.at[g], (o, l))))
            e_out.append((cond, remote(es.at[at], er.at[g, at], e_ss.at[d], e_rs.at[g], (o, l))))
    s_in, pv_in, e_in = [], [], []
    for k in range(NG):
        from_inner = ends & (inner_dev == k)
        from_other = (g != k) & jnp.logical_not(from_inner)
        if k in (1, 2):
            for cond, at in ((from_inner, pl.ds(0, 1)), (from_other, pl.ds(1, 1))):
                s_in.append((cond, remote(ss.at[at], sr.at[k, at], s_ss.at[0], s_rs.at[k], (k, l))))
        for cond, at in ((from_inner, pl.ds(0, 2)), (from_other, pl.ds(2, 1))):
            pv_in.append((cond, remote(pvs.at[at], pvr.at[k, at], pv_ss.at[0], pv_rs.at[k], (k, l))))
            e_in.append((cond, remote(es.at[at], er.at[k, at], e_ss.at[0], e_rs.at[k], (k, l))))

    bottom = jnp.where(g == 0, face(phz(0), 0.0), zero) + 1.0
    top = jnp.where(g == NG - 1, face(phz(CZ - 1), 0.0), zero) + 1.0
    ea[0] = bottom
    pf[0] = one
    eb[CZ - 1] = top
    qf[CZ - 1] = one

    def eliminate(i, carry):
        e, prod, ebar, qprod = carry
        j = CZ - 1 - i
        u = face(phz(i), phz(i + 1))
        v = face(phz(j), phz(j - 1))
        w = u / (u + e)
        y = v / (v + ebar)
        e = 1.0 + w * e
        ebar = 1.0 + y * ebar
        prod = prod * w
        qprod = qprod * y
        wf[i] = w
        vb[j] = y
        ea[i + 1] = e
        eb[j - 1] = ebar
        pf[i + 1] = prod
        qf[j - 1] = qprod
        return e, prod, ebar, qprod

    def eliminate3(k, carry):
        for r in range(3):
            carry = eliminate(1 + 3 * k + r, carry)
        return carry

    lax.fori_loop(0, 10, eliminate3, eliminate(0, (bottom, one, top, one)))

    def finish(k, _):
        for r in range(BZ):
            i = k * BZ + r
            d = 1.0 / (ea[i] + eb[i] - 1.0)
            dd[i] = d
            pp[i] = pf[i] * d
            qq[i] = qf[i] * d
        return 0

    lax.fori_loop(0, CZ // BZ, finish, 0)
    zs[0, 3] = pp[0]
    zs[1, 3] = qq[CZ - 1]
    ts[...] = pp[CZ - 1]
    tr[g] = ts[...]
    for cond, cp in w_out + t_out:
        pl.when(cond)(cp.start)
    pl.semaphore_wait(met, many(has_lo, has_hi))
    for cond, cp in c_out + t_far_out:
        pl.when(cond)(cp.start)


    for side, x in ((0, -1), (1, CX)):
        ph[0:CZ, PAD + x, :] = zero
        ph[CZ:CZ + 2, PAD + x, :] = zero[0:2]
        fx[:, PAD + x, :] = zero
        so[:, PAD + x, :] = xs[side, 2]
        for buf in (cin, cnx, cout, cs0):
            buf[side, 0:8] = zero[0:8]
            buf[side, 40:56] = zero[0:16]
        @pl.when(jnp.logical_not((has_xl, has_xr)[side]))
        def _():
            xr[side] = jnp.zeros((4, CZ, NY), F32)
        @pl.when(jnp.logical_not((has_lo, has_hi)[side]))
        def _():
            zr[side] = jnp.zeros((4, CX, NY), F32)
    for i, (cond, _) in enumerate(diag):
        @pl.when(jnp.logical_not(cond))
        def _():
            cr[i] = jnp.zeros((1, NY), F32)

    def prefactor(k, _):
        mask = masked(k)
        for r in range(BZ):
            z = k * BZ + r
            s0[z] = (1.0 + 0.7 * soz(z)) * (phz(z) - po[z]) * mask
        return 0

    lax.fori_loop(0, CZ // BZ, prefactor, 0)

    def plane(z):
        here = phz(z)
        right, left = phz(z, 1), phz(z, -1)
        yn, yp = next_y(here, last), prev_y(here, first)
        gx = right - left
        gy = yn - yp
        gz = phz(z + 1) - phz(z - 1)
        factor = flux_factor(gx, gy, gz, jnp.where(inner, s0[z], 0.0))
        fx[z, pl.ds(PAD, CX), :] = factor * gx
        fz[z + 1] = factor * gz
        flux_y = factor * gy
        s = soz(z)
        side = coupling(here, right) * (soz(z, 1) - s) + coupling(here, left) * (soz(z, -1) - s)
        step_y = coupling(here, yn) * (next_y(s, last) - s)
        back = jnp.where(first, coupling(here, 0.0) * s, pltpu.roll(step_y + flux_y, 1, 1))
        rh[z] = s + side + (step_y + next_y(flux_y, last) - back)

    def gather_rhs(z, sums):
        r = (
            rh[z]
            + (fx[z, pl.ds(PAD + 1, CX), :] - fx[z, pl.ds(PAD - 1, CX), :])
            + (fz[z + 2] - fz[z])
        )
        rh[z] = r
        return sums[0] + pp[z] * r, sums[1] + qq[z] * r

    def planes(k, _):
        for r in range(6):
            plane(1 + 6 * k + r)
        return 0

    lax.fori_loop(0, 5, planes, 0)

    def rows(k, sums):
        for r in range(BZ):
            sums = gather_rhs(2 + BZ * k + r, sums)
        return sums

    sums = lax.fori_loop(0, 7, rows, (zero, zero))

    for side, x in ((0, 0), (1, CX - 1)):
        near = 1 if x == 0 else CX - 2
        cin[side, 8:40] = xs[side, 0]
        cnx[side, 8:40] = xs[side, 1]
        cs0[side, 8:40] = xs[side, 3]
        cpq[side, 0] = pp[:, x, :]
        cpq[side, 1] = qq[:, x, :]
        cpq[side, 2] = pp[:, near, :]
        cpq[side, 3] = qq[:, near, :]

    for cond, cp in z_in + w_in:
        pl.when(cond)(cp.wait_recv)
    self_hi = 1.0 / face(phz(CZ - 1), zr[1, 0]) + qq[CZ - 1] + zr[1, 3]
    self_lo = 1.0 / face(phz(0), zr[0, 0]) + pp[0] + zr[0, 3]
    even = lax.rem(g, 2) == 0
    self_out = jnp.where(even, self_hi, self_lo)
    ss[0] = jnp.where(even, self_lo, self_hi)
    ss[1] = self_out
    sr[g] = ss[...]
    for cond, cp in s_out:
        pl.when(cond)(cp.start)
    own_k = ts[...] / self_out
    ph[0, pl.ds(PAD, CX), :] = zr[0, 0]
    ph[CZ + 1, pl.ds(PAD, CX), :] = zr[1, 0]
    for side, z in ((0, -1), (1, CZ)):
        gz = phz(0) - zr[side, 1] if side == 0 else zr[side, 1] - phz(CZ - 1)
        gx = phz(z, 1) - phz(z, -1)
        factor = flux_factor(gx, ydiff(zr[side, 0]), gz, jnp.where(inner, zr[side, 2], 0.0))
        fz[z + 1] = factor * gz
    plane(0)
    plane(CZ - 1)
    for z in (0, 1, CZ - 2, CZ - 1):
        sums = gather_rhs(z, sums)
    facing, away = jnp.where(up, sums[0], sums[1]), jnp.where(up, sums[1], sums[0])
    pvs[0] = facing
    pvs[1] = away
    pvs[2] = jnp.where(middle, facing - own_k * away, facing)
    pvr[g] = pvs[...]
    for cond, cp in pv_out:
        pl.when(cond)(cp.start)

    for side, x in ((0, 0), (1, CX - 1)):
        near = 1 if x == 0 else CX - 2
        for buf, which, xx in ((cin, 0, x), (cnx, 0, near)):
            buf[side, 7:8] = zr[0, which, xx:xx + 1, :]
            buf[side, 40:41] = zr[1, which, xx:xx + 1, :]
        cin[side, 6:7] = zr[0, 1, x:x + 1, :]
        cin[side, 41:42] = zr[1, 1, x:x + 1, :]
        a = cin[side, 7:47]
        cgy[side] = next_y(a, last_e) - prev_y(a, first_e)
        cgz[side] = cin[side, 8:48] - cin[side, 6:46]

    for side, x in ((0, 0), (1, CX - 1)):
        for end, z in ((0, 0), (1, CZ - 1)):
            at_a, at_b = 4 * side + end, 4 * side + 2 + end
            zb = 7 if end == 0 else 40
            w8[0, at_b:at_b + 1] = cnx[side, zb:zb + 1]
            w8[1, at_b:at_b + 1] = cgz[side, zb - 7:zb - 6]
            w8[2, at_b:at_b + 1] = cgy[side, zb - 7:zb - 6]
            w8[3, at_b:at_b + 1] = zr[end, 2, x:x + 1, :] * (-1.0 if end == 0 else 1.0)
            for at in (at_a, at_b):
                w8[4, at:at + 1] = cpq[side, 0, z:z + 1]
                w8[5, at:at + 1] = cpq[side, 1, z:z + 1]

    for cond, cp in x_in:
        pl.when(cond)(cp.wait_recv)
    tile_p = jnp.zeros((8, NY), F32)
    tile_q = jnp.zeros((8, NY), F32)
    for side, x in ((0, 0), (1, CX - 1)):
        near = 1 if x == 0 else CX - 2
        outer = xr[side, 0]
        cout[side, 8:40] = outer
        gin = cnx[side, 7:47] - cout[side, 7:47]
        factor = flux_factor(gin, cgy[side], cgz[side], cs0[side, 7:47])
        cfa[side] = factor
        cfz[side] = factor * cgz[side]
        g_out2 = xs[side, 0] - xr[side, 1]
        gy_out = ydiff(outer)
        f_out = flux_factor(
            g_out2, gy_out, cout[side, 9:41] - cout[side, 7:39], xr[side, 3]
        ) * jnp.where(inner, g_out2, 0.0)
        own = cfa[side, 1:33]
        d_near = -own * (xs[side, 1] - outer)
        d_edge = (
            coupling(xs[side, 0], outer) * (xr[side, 2] - xs[side, 2])
            - f_out
            + ydiff(own * cgy[side, 1:33])
            + (cfz[side, 2:34] - cfz[side, 0:32])
        )
        at, at_near = (0, 1) if side == 0 else (7, 6)
        for d, where, k in ((d_edge, at, 0), (d_near, at_near, 2)):
            tile_p = jnp.where(sub == where, jnp.sum(cpq[side, k] * d, axis=0, keepdims=True), tile_p)
            tile_q = jnp.where(sub == where, jnp.sum(cpq[side, k + 1] * d, axis=0, keepdims=True), tile_q)
        cfa[side, 0:32] = d_edge
        cfz[side, 0:32] = d_near
        cgo[side, 0] = g_out2
        cgo[side, 1] = gy_out
        for end, z in ((0, 0), (1, CZ - 1)):
            at_a, at_b = 4 * side + end, 4 * side + 2 + end
            inz = 1 if end == 0 else CZ - 2
            w8[0, at_a:at_a + 1] = xr[side, 0, inz:inz + 1, :]
            w8[1, at_a:at_a + 1] = cgo[side, 0, z:z + 1]
            w8[2, at_a:at_a + 1] = cgo[side, 1, z:z + 1]
            w8[3, at_a:at_a + 1] = -xr[side, 3, z:z + 1, :]
    carry2 = w8[1] * w8[1]
    side2 = w8[2] * w8[2]
    known2 = carry2 + side2 + 1.0
    known4 = carry2 * carry2 + side2 * side2
    scale = w8[3] * w8[1]
    base8, weight_p, weight_q = w8[0], w8[4], w8[5]
    for cond, cp in c_in:
        pl.when(cond)(cp.wait_recv)
    lower, left_half = sub % 2 == 0, sub // 4 == 0
    corner = [jnp.broadcast_to(cr[i], (8, NY)) for i in range(4)]
    v = base8 - jnp.where(
        lower, jnp.where(left_half, corner[0], corner[1]), jnp.where(left_half, corner[2], corner[3])
    )
    v2 = v * v
    inv = lax.rsqrt(known2 + v2)
    inv2 = inv * inv
    d8 = scale * inv * (0.1 + 1.2 * (known4 + v2 * v2) * (inv2 * inv2))

    def corner_rows(y):
        y = y + pltpu.roll(y, 7, 0)
        y = y + pltpu.roll(y, 6, 0)
        return jnp.where(sub == 0, y, jnp.where(sub == 7, pltpu.roll(y, 3, 0), 0.0))

    tile_p = tile_p + corner_rows(weight_p * d8)
    tile_q = tile_q + corner_rows(weight_q * d8)
    left_rows = sub < 4
    tile_facing, tile_away = jnp.where(up, tile_p, tile_q), jnp.where(up, tile_q, tile_p)
    tile_k = jnp.where(left_rows, own_k[0:8], own_k[CX - 8:CX])
    es[0] = tile_facing
    es[1] = tile_away
    es[2] = jnp.where(middle, tile_facing - tile_k * tile_away, tile_facing)
    er[g] = es[...]
    for cond, cp in e_out:
        pl.when(cond)(cp.start)
    w8[0] = d8
    for side in (0, 1):
        for end, z in ((0, 0), (1, CZ - 1)):
            at_a, at_b = 4 * side + end, 4 * side + 2 + end
            cfa[side, z:z + 1] = cfa[side, z:z + 1] + w8[0, at_a:at_a + 1] + w8[0, at_b:at_b + 1]
    for side, x in ((0, 0), (1, CX - 1)):
        near = 1 if x == 0 else CX - 2
        rh[:, x, :] = rh[:, x, :] + cfa[side, 0:32]
        rh[:, near, :] = rh[:, near, :] + cfz[side, 0:32]

    ee[0] = rh[0]
    bb[CZ - 1] = rh[CZ - 1]

    def sweep(i, carry):
        f, b = carry
        j = CZ - 1 - i
        f = rh[i] + wf[i - 1] * f
        b = rh[j] + vb[j + 1] * b
        ee[i] = f
        bb[j] = b
        return f, b

    def sweep3(k, carry):
        for r in range(3):
            carry = sweep(2 + 3 * k + r, carry)
        return carry

    lax.fori_loop(0, 10, sweep3, sweep(1, (rh[0], rh[CZ - 1])))

    def local(k, _):
        for r in range(BZ):
            z = k * BZ + r
            ee[z] = (ee[z] + bb[z] - rh[z]) * dd[z]
        return 0

    lax.fori_loop(0, CZ // BZ, local, 0)

    for cond, cp in t_in + s_in + pv_in:
        pl.when(cond)(cp.wait_recv)
    t_far = tr[far_inner]
    t_own = tr[inner_dev]
    k1 = t_far / sr[far_inner, 1]
    m1 = 1.0 / (sr[inner_dev, 0] - t_far * k1)
    k2 = t_own * m1
    m2 = 1.0 / (ss[1] - t_own * k2)
    b1 = pvr[far_inner, 2] + k1 * pvr[far_outer, 2] - pvr[inner_dev, 0]
    b2 = pvr[inner_dev, 1] - pvr[outer_dev, 2]
    tile_k1 = jnp.where(left_rows, k1[0:8], k1[CX - 8:CX])
    for cond, cp in x_out + z_out + c_out + w_out + t_out + t_far_out + s_out + pv_out + e_out:
        pl.when(cond)(cp.wait_send)
    for cond, cp in e_in:
        pl.when(cond)(cp.wait_recv)

    def widen(tile):
        full = jnp.concatenate([tile, jnp.zeros((CX - 16, NY), F32), tile], axis=0)
        return jnp.where((row < 2) | (row >= CX - 2), full, 0.0)

    b1 = b1 + widen(er[far_inner, 2] + tile_k1 * er[far_outer, 2] - er[inner_dev, 0])
    b2 = b2 + widen(er[inner_dev, 1] - er[outer_dev, 2])
    r2 = (b2 + k2 * b1) * m2
    r1 = (b1 + t_own * r2) * m1
    below = jnp.where(g == 3, r2, jnp.where(g == 2, r1, jnp.where(g == 1, -r2, 0.0)))
    above = jnp.where(g == 0, -r2, jnp.where(g == 1, -r1, jnp.where(g == 2, r2, 0.0)))

    below_out[...] = below
    above_out[...] = above


def step(phase, old, solute, blocks, count):
    def buf(*shape):
        return pltpu.VMEM(shape + (NY,), F32)

    slab = buf(CZ, CX)
    dma = pltpu.SemaphoreType.DMA
    parts = pl.pallas_call(
        kernel,
        out_shape=[pltpu.VMEM((CZ, CX, NY), F32)] * 3 + [pltpu.VMEM((CX, NY), F32)] * 2,
        in_specs=[pl.BlockSpec(memory_space=pl.ANY)] * 5,
        out_specs=[pl.BlockSpec(memory_space=pltpu.VMEM)] * 5,
        scratch_shapes=[
            buf(CZ + 2, ROW), buf(CZ, ROW), slab, slab, buf(CZ, ROW), buf(CZ + 2, CX),
            slab, slab, slab, slab, slab, slab, slab, slab, slab,
            buf(2, 56), buf(2, 56), buf(2, 56), buf(2, 56),
            buf(2, 40), buf(2, 40), buf(2, 40), buf(2, 40), buf(2, 4, CZ),
            buf(2, 2, CZ), buf(6, 8),
            buf(2, 4, CZ), buf(2, 4, CZ),
            buf(2, 4, CX), buf(2, 4, CX),
            buf(4, 1), buf(4, 1),
            buf(CX), buf(NG, CX),
            buf(2, CX), buf(NG, 2, CX),
            buf(3, CX), buf(NG, 3, CX),
            buf(3, 8), buf(NG, 3, 8),
            pltpu.SMEM((1, 1, 6), jnp.int32),
            pltpu.SMEM((1, 1), jnp.int32),
            dma((5,)),
            dma((2,)), dma((2,)),
            dma((4,)), dma((4,)),
            dma((4,)), dma((4,)),
            dma((3,)), dma((NG,)),
            dma((3,)), dma((NG,)),
            dma((3,)), dma((NG,)),
            dma((3,)), dma((NG,)),
            pltpu.SemaphoreType.REGULAR,
        ],
        compiler_params=pltpu.CompilerParams(
            collective_id=0, has_side_effects=True, vmem_limit_bytes=65400000
        ),
    )(phase, old, solute, blocks, count)
    chunks = 4
    deep = CZ // chunks

    def close(ee, pp, qq, below, above, dst, stage, sems):
        lo, hi = below[...], above[...]
        cps = []
        for c in range(chunks):
            for z in range(c * deep, (c + 1) * deep):
                stage[z] = ee[z] + pp[z] * lo - qq[z] * hi
            at = pl.ds(c * deep, deep)
            cps.append(pltpu.make_async_copy(stage.at[at], dst.at[at], sems.at[c]))
            cps[-1].start()
        for cp in cps:
            cp.wait()

    return pl.pallas_call(
        close,
        out_shape=jax.ShapeDtypeStruct((CZ, CX, NY), F32),
        in_specs=[pl.BlockSpec(memory_space=pltpu.VMEM)] * 5,
        out_specs=pl.BlockSpec(memory_space=pl.ANY),
        scratch_shapes=[slab, dma((chunks,))],
        compiler_params=pltpu.CompilerParams(vmem_limit_bytes=4194304),
    )(*[pltpu.with_memory_space_constraint(a, pltpu.VMEM) for a in parts])


def solution(mesh):
    spec = P("growth", "lateral", None)
    return jax.shard_map(
        step,
        mesh=mesh,
        in_specs=(spec, spec, spec, spec, P("growth", "lateral")),
        out_specs=spec,
        check_vma=False,
    )
```

```python
import jax
import jax.numpy as jnp
from jax import lax
from jax.experimental import pallas as pl
from jax.experimental.pallas import tpu as pltpu
from jax.sharding import PartitionSpec as P

BZ = 4
MESH = pl.DeviceIdType.MESH
NG = 4
NL = 32
CZ = 32
CX = 32
NY = 128
PAD = 8
ROW = CX + 2 * PAD
F32 = jnp.float32


def flux_factor(gx, gy, gz, pre):
    x2 = gx * gx
    y2 = gy * gy
    z2 = gz * gz
    inv = lax.rsqrt(x2 + y2 + z2 + 1.0)
    inv2 = inv * inv
    quartic = x2 * x2 + y2 * y2 + z2 * z2
    return pre * inv * (0.1 + 1.2 * quartic * (inv2 * inv2))


def next_y(a, last):
    return jnp.where(last, 0.0, pltpu.roll(a, NY - 1, 1))


def prev_y(a, first):
    return jnp.where(first, 0.0, pltpu.roll(a, 1, 1))


def kernel(
    phase, old, solute, blocks, count, ee, pp, qq, below_out, above_out,
    ph, so, po, s0, fx, fz, rh, bb, wf, pf, vb, qf, dd, ea, eb,
    cin, cnx, cout, cs0, cgy, cgz, cfa, cfz, cpq, cgo, w8,
    xs, xr, zs, zr, cs, cr, ts, tr, ss, sr, pvs, pvr, es, er, blk, cnt,
    in_sem, x_ss, x_rs, z_ss, z_rs, c_ss, c_rs, t_ss, t_rs, s_ss, s_rs, pv_ss, pv_rs, e_ss, e_rs, met,
):
    g = lax.axis_index("growth")
    l = lax.axis_index("lateral")
    has_lo, has_hi = g > 0, g < NG - 1
    has_xl, has_xr = l > 0, l < NL - 1
    g_lo, g_hi = jnp.maximum(g - 1, 0), jnp.minimum(g + 1, NG - 1)
    l_lo, l_hi = jnp.maximum(l - 1, 0), jnp.minimum(l + 1, NL - 1)
    others = [lax.rem(g + d, NG) for d in (2, 3, 1)]

    barrier = pltpu.get_barrier_semaphore()

    def greet(cond, dev):
        @pl.when(cond)
        def _():
            pl.semaphore_signal(barrier, inc=1, device_id=dev, device_id_type=MESH)

    diag = [
        (has_lo & has_xl, (g_lo, l_lo)),
        (has_lo & has_xr, (g_lo, l_hi)),
        (has_hi & has_xl, (g_hi, l_lo)),
        (has_hi & has_xr, (g_hi, l_hi)),
    ]
    ends = jnp.logical_not(has_lo & has_hi)
    greet(has_lo, (g_lo, l))
    greet(has_hi, (g_hi, l))
    greet(has_xl, (g, l_lo))
    greet(has_xr, (g, l_hi))
    greet(ends, (NG - 1 - g, l))

    ins = [
        pltpu.make_async_copy(phase, ph.at[pl.ds(1, CZ), pl.ds(PAD, CX), :], in_sem.at[0]),
        pltpu.make_async_copy(old, po, in_sem.at[1]),
        pltpu.make_async_copy(solute, so.at[:, pl.ds(PAD, CX), :], in_sem.at[2]),
        pltpu.make_async_copy(blocks, blk, in_sem.at[3]),
        pltpu.make_async_copy(count, cnt, in_sem.at[4]),
    ]
    for c in ins:
        c.start()

    lane = lax.broadcasted_iota(jnp.int32, (CX, NY), 1)
    row = lax.broadcasted_iota(jnp.int32, (CX, NY), 0)
    first, last = lane == 0, lane == NY - 1
    inner = (row > 0) & (row < CX - 1)
    zero = jnp.zeros((CX, NY), F32)
    one = zero + 1.0
    EXT = 40
    lane_e = lax.broadcasted_iota(jnp.int32, (EXT, NY), 1)
    first_e, last_e = lane_e == 0, lane_e == NY - 1

    def face(a, b):
        return 220.0 - 90.0 * (a + b)

    def coupling(a, b):
        return 0.055 - 0.0225 * (a + b)

    def ydiff(a):
        return next_y(a, last) - prev_y(a, first)

    def phz(z, off=0):
        return ph[z + 1, pl.ds(PAD + off, CX), :]

    def soz(z, off=0):
        return so[z, pl.ds(PAD + off, CX), :]

    for c in ins:
        c.wait()

    live = [jnp.where(s < cnt[0, 0], blk[0, 0, s], -1) for s in range(6)]

    def masked(k):
        hit = k == live[0]
        for b in live[1:]:
            hit = hit | (k == b)
        return jnp.where(hit, 0.25, 0.0)

    column_mask = masked(row // BZ)
    sub = lax.broadcasted_iota(jnp.int32, (8, NY), 0)
    for side, x in ((0, 0), (1, CX - 1)):
        near = 1 if x == 0 else CX - 2
        here, s = ph[1:CZ + 1, PAD + x, :], so[:, PAD + x, :]
        xs[side, 0] = here
        xs[side, 1] = ph[1:CZ + 1, PAD + near, :]
        xs[side, 2] = s
        xs[side, 3] = (1.0 + 0.7 * s) * (here - po[:, x, :]) * column_mask
    for side, z in ((0, 0), (1, CZ - 1)):
        zs[side, 0] = phz(z)
        zs[side, 1] = phz(1 if z == 0 else CZ - 2)
        zs[side, 2] = (1.0 + 0.7 * soz(z)) * (phz(z) - po[z]) * masked(jnp.int32(z // BZ))
        for right, x in ((0, 0), (1, CX - 1)):
            cs[2 * side + right] = phz(z)[x:x + 1]

    def many(*conds):
        return sum(c.astype(jnp.int32) for c in conds)

    pl.semaphore_wait(barrier, many(has_lo, has_hi, has_xl, has_xr, ends))

    def remote(src, dst, ss, rs, dev):
        return pltpu.make_async_remote_copy(
            src_ref=src, dst_ref=dst, send_sem=ss, recv_sem=rs, device_id=dev, device_id_type=MESH
        )

    x_out = [
        (has_xl, remote(xs.at[0], xr.at[1], x_ss.at[0], x_rs.at[1], (g, l_lo))),
        (has_xr, remote(xs.at[1], xr.at[0], x_ss.at[1], x_rs.at[0], (g, l_hi))),
    ]
    z_out = [
        (has_lo, remote(zs.at[0, 0:3], zr.at[1, 0:3], z_ss.at[0], z_rs.at[1], (g_lo, l))),
        (has_hi, remote(zs.at[1, 0:3], zr.at[0, 0:3], z_ss.at[1], z_rs.at[0], (g_hi, l))),
    ]
    w_out = [
        (has_lo, remote(zs.at[0, 3], zr.at[1, 3], z_ss.at[2], z_rs.at[3], (g_lo, l))),
        (has_hi, remote(zs.at[1, 3], zr.at[0, 3], z_ss.at[3], z_rs.at[2], (g_hi, l))),
    ]
    w_in = [
        (has_lo, remote(zs.at[1, 3], zr.at[0, 3], z_ss.at[3], z_rs.at[2], (g_lo, l))),
        (has_hi, remote(zs.at[0, 3], zr.at[1, 3], z_ss.at[2], z_rs.at[3], (g_hi, l))),
    ]
    c_out = [
        (cond, remote(cs.at[i], cr.at[3 - i], c_ss.at[i], c_rs.at[3 - i], dev))
        for i, (cond, dev) in enumerate(diag)
    ]
    for i, (cond, o) in enumerate(((has_lo, g_lo), (has_hi, g_hi))):
        @pl.when(cond)
        def _():
            pl.semaphore_signal(met, inc=1, device_id=(o, l), device_id_type=MESH)
    for cond, cp in z_out + x_out:
        pl.when(cond)(cp.start)
    x_in = [
        (has_xl, remote(xs.at[1], xr.at[0], x_ss.at[1], x_rs.at[0], (g, l_lo))),
        (has_xr, remote(xs.at[0], xr.at[1], x_ss.at[0], x_rs.at[1], (g, l_hi))),
    ]
    z_in = [
        (has_lo, remote(zs.at[1, 0:3], zr.at[0, 0:3], z_ss.at[1], z_rs.at[0], (g_lo, l))),
        (has_hi, remote(zs.at[0, 0:3], zr.at[1, 0:3], z_ss.at[0], z_rs.at[1], (g_hi, l))),
    ]
    c_in = [
        (cond, remote(cs.at[3 - i], cr.at[i], c_ss.at[3 - i], c_rs.at[i], dev))
        for i, (cond, dev) in enumerate(diag)
    ]

    middle = has_lo & has_hi
    up = g >= NG // 2
    half = up.astype(jnp.int32)
    inner_dev, outer_dev = 1 + half, 3 * half
    far_inner, far_outer = 2 - half, 3 - 3 * half
    beside = [(has_lo, g_lo), (has_hi, g_hi)]
    t_out = [
        (middle & cond, remote(ts, tr.at[g], t_ss.at[i], t_rs.at[g], (o, l)))
        for i, (cond, o) in enumerate(beside)
    ]
    t_far_out = [(middle, remote(ts, tr.at[g], t_ss.at[2], t_rs.at[g], (far_outer, l)))]
    t_in = [
        (cond & (o > 0) & (o < NG - 1), remote(ts, tr.at[o], t_ss.at[0], t_rs.at[o], (o, l)))
        for cond, o in beside
    ]
    t_in.append(
        (ends, remote(ts, tr.at[far_inner], t_ss.at[0], t_rs.at[far_inner], (far_inner, l)))
    )
    s_out, pv_out, e_out = [], [], []
    for d, o in enumerate(others):
        to_end = middle & (o == outer_dev)
        to_far = middle & (o != outer_dev)
        for cond, at in ((to_end, pl.ds(0, 1)), (to_far, pl.ds(1, 1))):
            s_out.append((cond, remote(ss.at[at], sr.at[g, at], s_ss.at[d], s_rs.at[g], (o, l))))
        for cond, at in ((to_end, pl.ds(0, 2)), (jnp.logical_not(to_end), pl.ds(2, 1))):
            pv_out.append((cond, remote(pvs.at[at], pvr.at[g, at], pv_ss.at[d], pv_rs.at[g], (o, l))))
            e_out.append((cond, remote(es.at[at], er.at[g, at], e_ss.at[d], e_rs.at[g], (o, l))))
    s_in, pv_in, e_in = [], [], []
    for k in range(NG):
        from_inner = ends & (inner_dev == k)
        from_other = (g != k) & jnp.logical_not(from_inner)
        if k in (1, 2):
            for cond, at in ((from_inner, pl.ds(0, 1)), (from_other, pl.ds(1, 1))):
                s_in.append((cond, remote(ss.at[at], sr.at[k, at], s_ss.at[0], s_rs.at[k], (k, l))))
        for cond, at in ((from_inner, pl.ds(0, 2)), (from_other, pl.ds(2, 1))):
            pv_in.append((cond, remote(pvs.at[at], pvr.at[k, at], pv_ss.at[0], pv_rs.at[k], (k, l))))
            e_in.append((cond, remote(es.at[at], er.at[k, at], e_ss.at[0], e_rs.at[k], (k, l))))

    bottom = jnp.where(g == 0, face(phz(0), 0.0), zero) + 1.0
    top = jnp.where(g == NG - 1, face(phz(CZ - 1), 0.0), zero) + 1.0
    ea[0] = bottom
    pf[0] = one
    eb[CZ - 1] = top
    qf[CZ - 1] = one

    def eliminate(i, carry):
        e, prod, ebar, qprod = carry
        j = CZ - 1 - i
        u = face(phz(i), phz(i + 1))
        v = face(phz(j), phz(j - 1))
        w = u / (u + e)
        y = v / (v + ebar)
        e = 1.0 + w * e
        ebar = 1.0 + y * ebar
        prod = prod * w
        qprod = qprod * y
        wf[i] = w
        vb[j] = y
        ea[i + 1] = e
        eb[j - 1] = ebar
        pf[i + 1] = prod
        qf[j - 1] = qprod
        return e, prod, ebar, qprod

    def eliminate3(k, carry):
        for r in range(3):
            carry = eliminate(1 + 3 * k + r, carry)
        return carry

    lax.fori_loop(0, 10, eliminate3, eliminate(0, (bottom, one, top, one)))

    def finish(k, _):
        for r in range(BZ):
            i = k * BZ + r
            d = 1.0 / (ea[i] + eb[i] - 1.0)
            dd[i] = d
            pp[i] = pf[i] * d
            qq[i] = qf[i] * d
        return 0

    lax.fori_loop(0, CZ // BZ, finish, 0)
    zs[0, 3] = pp[0]
    zs[1, 3] = qq[CZ - 1]
    ts[...] = pp[CZ - 1]
    tr[g] = ts[...]
    for cond, cp in w_out + t_out:
        pl.when(cond)(cp.start)
    pl.semaphore_wait(met, many(has_lo, has_hi))
    for cond, cp in c_out + t_far_out:
        pl.when(cond)(cp.start)


    for side, x in ((0, -1), (1, CX)):
        ph[0:CZ, PAD + x, :] = zero
        ph[CZ:CZ + 2, PAD + x, :] = zero[0:2]
        fx[:, PAD + x, :] = zero
        so[:, PAD + x, :] = xs[side, 2]
        for buf in (cin, cnx, cout, cs0):
            buf[side, 0:8] = zero[0:8]
            buf[side, 40:56] = zero[0:16]
        @pl.when(jnp.logical_not((has_xl, has_xr)[side]))
        def _():
            xr[side] = jnp.zeros((4, CZ, NY), F32)
        @pl.when(jnp.logical_not((has_lo, has_hi)[side]))
        def _():
            zr[side] = jnp.zeros((4, CX, NY), F32)
    for i, (cond, _) in enumerate(diag):
        @pl.when(jnp.logical_not(cond))
        def _():
            cr[i] = jnp.zeros((1, NY), F32)

    def prefactor(k, _):
        mask = masked(k)
        for r in range(BZ):
            z = k * BZ + r
            s0[z] = (1.0 + 0.7 * soz(z)) * (phz(z) - po[z]) * mask
        return 0

    lax.fori_loop(0, CZ // BZ, prefactor, 0)

    def plane(z):
        here = phz(z)
        right, left = phz(z, 1), phz(z, -1)
        yn, yp = next_y(here, last), prev_y(here, first)
        gx = right - left
        gy = yn - yp
        gz = phz(z + 1) - phz(z - 1)
        factor = flux_factor(gx, gy, gz, jnp.where(inner, s0[z], 0.0))
        fx[z, pl.ds(PAD, CX), :] = factor * gx
        fz[z + 1] = factor * gz
        flux_y = factor * gy
        s = soz(z)
        side = coupling(here, right) * (soz(z, 1) - s) + coupling(here, left) * (soz(z, -1) - s)
        step_y = coupling(here, yn) * (next_y(s, last) - s)
        back = jnp.where(first, coupling(here, 0.0) * s, pltpu.roll(step_y + flux_y, 1, 1))
        rh[z] = s + side + (step_y + next_y(flux_y, last) - back)

    def gather_rhs(z, sums):
        r = (
            rh[z]
            + (fx[z, pl.ds(PAD + 1, CX), :] - fx[z, pl.ds(PAD - 1, CX), :])
            + (fz[z + 2] - fz[z])
        )
        rh[z] = r
        return sums[0] + pp[z] * r, sums[1] + qq[z] * r

    def planes(k, _):
        for r in range(6):
            plane(1 + 6 * k + r)
        return 0

    lax.fori_loop(0, 5, planes, 0)

    def rows(k, sums):
        for r in range(BZ):
            sums = gather_rhs(2 + BZ * k + r, sums)
        return sums

    sums = lax.fori_loop(0, 7, rows, (zero, zero))

    for side, x in ((0, 0), (1, CX - 1)):
        near = 1 if x == 0 else CX - 2
        cin[side, 8:40] = xs[side, 0]
        cnx[side, 8:40] = xs[side, 1]
        cs0[side, 8:40] = xs[side, 3]
        cpq[side, 0] = pp[:, x, :]
        cpq[side, 1] = qq[:, x, :]
        cpq[side, 2] = pp[:, near, :]
        cpq[side, 3] = qq[:, near, :]

    for cond, cp in z_in + w_in:
        pl.when(cond)(cp.wait_recv)
    self_hi = 1.0 / face(phz(CZ - 1), zr[1, 0]) + qq[CZ - 1] + zr[1, 3]
    self_lo = 1.0 / face(phz(0), zr[0, 0]) + pp[0] + zr[0, 3]
    even = lax.rem(g, 2) == 0
    self_out = jnp.where(even, self_hi, self_lo)
    ss[0] = jnp.where(even, self_lo, self_hi)
    ss[1] = self_out
    sr[g] = ss[...]
    for cond, cp in s_out:
        pl.when(cond)(cp.start)
    own_k = ts[...] / self_out
    ph[0, pl.ds(PAD, CX), :] = zr[0, 0]
    ph[CZ + 1, pl.ds(PAD, CX), :] = zr[1, 0]
    for side, z in ((0, -1), (1, CZ)):
        gz = phz(0) - zr[side, 1] if side == 0 else zr[side, 1] - phz(CZ - 1)
        gx = phz(z, 1) - phz(z, -1)
        factor = flux_factor(gx, ydiff(zr[side, 0]), gz, jnp.where(inner, zr[side, 2], 0.0))
        fz[z + 1] = factor * gz
    plane(0)
    plane(CZ - 1)
    for z in (0, 1, CZ - 2, CZ - 1):
        sums = gather_rhs(z, sums)
    facing, away = jnp.where(up, sums[0], sums[1]), jnp.where(up, sums[1], sums[0])
    pvs[0] = facing
    pvs[1] = away
    pvs[2] = jnp.where(middle, facing - own_k * away, facing)
    pvr[g] = pvs[...]
    for cond, cp in pv_out:
        pl.when(cond)(cp.start)

    for side, x in ((0, 0), (1, CX - 1)):
        near = 1 if x == 0 else CX - 2
        for buf, which, xx in ((cin, 0, x), (cnx, 0, near)):
            buf[side, 7:8] = zr[0, which, xx:xx + 1, :]
            buf[side, 40:41] = zr[1, which, xx:xx + 1, :]
        cin[side, 6:7] = zr[0, 1, x:x + 1, :]
        cin[side, 41:42] = zr[1, 1, x:x + 1, :]
        a = cin[side, 7:47]
        cgy[side] = next_y(a, last_e) - prev_y(a, first_e)
        cgz[side] = cin[side, 8:48] - cin[side, 6:46]

    for side, x in ((0, 0), (1, CX - 1)):
        for end, z in ((0, 0), (1, CZ - 1)):
            at_a, at_b = 2 * end + side, 4 + 2 * end + side
            zb = 7 if end == 0 else 40
            w8[0, at_b:at_b + 1] = cnx[side, zb:zb + 1]
            w8[1, at_b:at_b + 1] = cgz[side, zb - 7:zb - 6]
            w8[2, at_b:at_b + 1] = cgy[side, zb - 7:zb - 6]
            w8[3, at_b:at_b + 1] = zr[end, 2, x:x + 1, :] * (-1.0 if end == 0 else 1.0)
            for at in (at_a, at_b):
                w8[4, at:at + 1] = cpq[side, 0, z:z + 1]
                w8[5, at:at + 1] = cpq[side, 1, z:z + 1]

    for cond, cp in x_in:
        pl.when(cond)(cp.wait_recv)
    tile_p = jnp.zeros((8, NY), F32)
    tile_q = jnp.zeros((8, NY), F32)
    for side, x in ((0, 0), (1, CX - 1)):
        near = 1 if x == 0 else CX - 2
        outer = xr[side, 0]
        cout[side, 8:40] = outer
        gin = cnx[side, 7:47] - cout[side, 7:47]
        factor = flux_factor(gin, cgy[side], cgz[side], cs0[side, 7:47])
        cfa[side] = factor
        cfz[side] = factor * cgz[side]
        g_out2 = xs[side, 0] - xr[side, 1]
        gy_out = ydiff(outer)
        f_out = flux_factor(
            g_out2, gy_out, cout[side, 9:41] - cout[side, 7:39], xr[side, 3]
        ) * jnp.where(inner, g_out2, 0.0)
        own = cfa[side, 1:33]
        d_near = -own * (xs[side, 1] - outer)
        d_edge = (
            coupling(xs[side, 0], outer) * (xr[side, 2] - xs[side, 2])
            - f_out
            + ydiff(own * cgy[side, 1:33])
            + (cfz[side, 2:34] - cfz[side, 0:32])
        )
        at, at_near = (0, 1) if side == 0 else (7, 6)
        for d, where, k in ((d_edge, at, 0), (d_near, at_near, 2)):
            tile_p = jnp.where(sub == where, jnp.sum(cpq[side, k] * d, axis=0, keepdims=True), tile_p)
            tile_q = jnp.where(sub == where, jnp.sum(cpq[side, k + 1] * d, axis=0, keepdims=True), tile_q)
        cfa[side, 0:32] = d_edge
        cfz[side, 0:32] = d_near
        cgo[side, 0] = g_out2
        cgo[side, 1] = gy_out
        for end, z in ((0, 0), (1, CZ - 1)):
            at_a, at_b = 2 * end + side, 4 + 2 * end + side
            inz = 1 if end == 0 else CZ - 2
            w8[0, at_a:at_a + 1] = xr[side, 0, inz:inz + 1, :]
            w8[1, at_a:at_a + 1] = cgo[side, 0, z:z + 1]
            w8[2, at_a:at_a + 1] = cgo[side, 1, z:z + 1]
            w8[3, at_a:at_a + 1] = -xr[side, 3, z:z + 1, :]
    carry2 = w8[1] * w8[1]
    side2 = w8[2] * w8[2]
    known2 = carry2 + side2 + 1.0
    known4 = carry2 * carry2 + side2 * side2
    scale = w8[3] * w8[1]
    base8, weight_p, weight_q = w8[0], w8[4], w8[5]
    for cond, cp in c_in:
        pl.when(cond)(cp.wait_recv)
    lower, left_half = (sub // 2) % 2 == 0, sub % 2 == 0
    corner = [jnp.broadcast_to(cr[i], (8, NY)) for i in range(4)]
    v = base8 - jnp.where(
        lower, jnp.where(left_half, corner[0], corner[1]), jnp.where(left_half, corner[2], corner[3])
    )
    v2 = v * v
    inv = lax.rsqrt(known2 + v2)
    inv2 = inv * inv
    d8 = scale * inv * (0.1 + 1.2 * (known4 + v2 * v2) * (inv2 * inv2))

    def corner_rows(y):
        y = y + pltpu.roll(y, 4, 0)
        y = y + pltpu.roll(y, 2, 0)
        return jnp.where((sub == 0) | (sub == 7), y, 0.0)

    tile_p = tile_p + corner_rows(weight_p * d8)
    tile_q = tile_q + corner_rows(weight_q * d8)
    left_rows = sub < 4
    tile_facing, tile_away = jnp.where(up, tile_p, tile_q), jnp.where(up, tile_q, tile_p)
    tile_k = jnp.where(left_rows, own_k[0:8], own_k[CX - 8:CX])
    es[0] = tile_facing
    es[1] = tile_away
    es[2] = jnp.where(middle, tile_facing - tile_k * tile_away, tile_facing)
    er[g] = es[...]
    for cond, cp in e_out:
        pl.when(cond)(cp.start)
    w8[0] = d8
    for side in (0, 1):
        for end, z in ((0, 0), (1, CZ - 1)):
            at_a, at_b = 2 * end + side, 4 + 2 * end + side
            cfa[side, z:z + 1] = cfa[side, z:z + 1] + w8[0, at_a:at_a + 1] + w8[0, at_b:at_b + 1]
    for side, x in ((0, 0), (1, CX - 1)):
        near = 1 if x == 0 else CX - 2
        rh[:, x, :] = rh[:, x, :] + cfa[side, 0:32]
        rh[:, near, :] = rh[:, near, :] + cfz[side, 0:32]

    ee[0] = rh[0]
    bb[CZ - 1] = rh[CZ - 1]

    def sweep(i, carry):
        f, b = carry
        j = CZ - 1 - i
        f = rh[i] + wf[i - 1] * f
        b = rh[j] + vb[j + 1] * b
        ee[i] = f
        bb[j] = b
        return f, b

    def sweep3(k, carry):
        for r in range(3):
            carry = sweep(2 + 3 * k + r, carry)
        return carry

    lax.fori_loop(0, 10, sweep3, sweep(1, (rh[0], rh[CZ - 1])))

    def local(k, _):
        for r in range(BZ):
            z = k * BZ + r
            ee[z] = (ee[z] + bb[z] - rh[z]) * dd[z]
        return 0

    lax.fori_loop(0, CZ // BZ, local, 0)

    for cond, cp in t_in + s_in + pv_in:
        pl.when(cond)(cp.wait_recv)
    t_far = tr[far_inner]
    t_own = tr[inner_dev]
    k1 = t_far / sr[far_inner, 1]
    m1 = 1.0 / (sr[inner_dev, 0] - t_far * k1)
    k2 = t_own * m1
    m2 = 1.0 / (ss[1] - t_own * k2)
    b1 = pvr[far_inner, 2] + k1 * pvr[far_outer, 2] - pvr[inner_dev, 0]
    b2 = pvr[inner_dev, 1] - pvr[outer_dev, 2]
    tile_k1 = jnp.where(left_rows, k1[0:8], k1[CX - 8:CX])
    for cond, cp in x_out + z_out + c_out + w_out + t_out + t_far_out + s_out + pv_out + e_out:
        pl.when(cond)(cp.wait_send)
    for cond, cp in e_in:
        pl.when(cond)(cp.wait_recv)

    def widen(tile):
        full = jnp.concatenate([tile, jnp.zeros((CX - 16, NY), F32), tile], axis=0)
        return jnp.where((row < 2) | (row >= CX - 2), full, 0.0)

    b1 = b1 + widen(er[far_inner, 2] + tile_k1 * er[far_outer, 2] - er[inner_dev, 0])
    b2 = b2 + widen(er[inner_dev, 1] - er[outer_dev, 2])
    r2 = (b2 + k2 * b1) * m2
    r1 = (b1 + t_own * r2) * m1
    below = jnp.where(g == 3, r2, jnp.where(g == 2, r1, jnp.where(g == 1, -r2, 0.0)))
    above = jnp.where(g == 0, -r2, jnp.where(g == 1, -r1, jnp.where(g == 2, r2, 0.0)))

    below_out[...] = below
    above_out[...] = above


def step(phase, old, solute, blocks, count):
    def buf(*shape):
        return pltpu.VMEM(shape + (NY,), F32)

    slab = buf(CZ, CX)
    dma = pltpu.SemaphoreType.DMA
    parts = pl.pallas_call(
        kernel,
        out_shape=[pltpu.VMEM((CZ, CX, NY), F32)] * 3 + [pltpu.VMEM((CX, NY), F32)] * 2,
        in_specs=[pl.BlockSpec(memory_space=pl.ANY)] * 5,
        out_specs=[pl.BlockSpec(memory_space=pltpu.VMEM)] * 5,
        scratch_shapes=[
            buf(CZ + 2, ROW), buf(CZ, ROW), slab, slab, buf(CZ, ROW), buf(CZ + 2, CX),
            slab, slab, slab, slab, slab, slab, slab, slab, slab,
            buf(2, 56), buf(2, 56), buf(2, 56), buf(2, 56),
            buf(2, 40), buf(2, 40), buf(2, 40), buf(2, 40), buf(2, 4, CZ),
            buf(2, 2, CZ), buf(6, 8),
            buf(2, 4, CZ), buf(2, 4, CZ),
            buf(2, 4, CX), buf(2, 4, CX),
            buf(4, 1), buf(4, 1),
            buf(CX), buf(NG, CX),
            buf(2, CX), buf(NG, 2, CX),
            buf(3, CX), buf(NG, 3, CX),
            buf(3, 8), buf(NG, 3, 8),
            pltpu.SMEM((1, 1, 6), jnp.int32),
            pltpu.SMEM((1, 1), jnp.int32),
            dma((5,)),
            dma((2,)), dma((2,)),
            dma((4,)), dma((4,)),
            dma((4,)), dma((4,)),
            dma((3,)), dma((NG,)),
            dma((3,)), dma((NG,)),
            dma((3,)), dma((NG,)),
            dma((3,)), dma((NG,)),
            pltpu.SemaphoreType.REGULAR,
        ],
        compiler_params=pltpu.CompilerParams(
            collective_id=0, has_side_effects=True, vmem_limit_bytes=65400000
        ),
    )(phase, old, solute, blocks, count)
    chunks = 4
    deep = CZ // chunks

    def close(ee, pp, qq, below, above, dst, stage, sems):
        lo, hi = below[...], above[...]
        cps = []
        for c in range(chunks):
            for z in range(c * deep, (c + 1) * deep):
                stage[z] = ee[z] + pp[z] * lo - qq[z] * hi
            at = pl.ds(c * deep, deep)
            cps.append(pltpu.make_async_copy(stage.at[at], dst.at[at], sems.at[c]))
            cps[-1].start()
        for cp in cps:
            cp.wait()

    return pl.pallas_call(
        close,
        out_shape=jax.ShapeDtypeStruct((CZ, CX, NY), F32),
        in_specs=[pl.BlockSpec(memory_space=pltpu.VMEM)] * 5,
        out_specs=pl.BlockSpec(memory_space=pl.ANY),
        scratch_shapes=[slab, dma((chunks,))],
        compiler_params=pltpu.CompilerParams(vmem_limit_bytes=4194304),
    )(*[pltpu.with_memory_space_constraint(a, pltpu.VMEM) for a in parts])


def solution(mesh):
    spec = P("growth", "lateral", None)
    return jax.shard_map(
        step,
        mesh=mesh,
        in_specs=(spec, spec, spec, spec, P("growth", "lateral")),
        out_specs=spec,
        check_vma=False,
    )
```

```python
import jax
import jax.numpy as jnp
from jax import lax
from jax.experimental import pallas as pl
from jax.experimental.pallas import tpu as pltpu
from jax.sharding import PartitionSpec as P

BZ = 4
MESH = pl.DeviceIdType.MESH
NG = 4
NL = 32
CZ = 32
CX = 32
NY = 128
PAD = 8
ROW = CX + 2 * PAD
F32 = jnp.float32


def flux_factor(gx, gy, gz, pre):
    x2 = gx * gx
    y2 = gy * gy
    z2 = gz * gz
    inv = lax.rsqrt(x2 + y2 + z2 + 1.0)
    inv2 = inv * inv
    quartic = x2 * x2 + y2 * y2 + z2 * z2
    return pre * inv * (0.1 + 1.2 * quartic * (inv2 * inv2))


def next_y(a, last):
    return jnp.where(last, 0.0, pltpu.roll(a, NY - 1, 1))


def prev_y(a, first):
    return jnp.where(first, 0.0, pltpu.roll(a, 1, 1))


def kernel(
    phase, old, solute, blocks, count, ee, pp, qq, below_out, above_out,
    ph, so, po, s0, fx, fz, rh, bb, wf, pf, vb, qf, dd, ea, eb,
    cin, cnx, cout, cs0, cgy, cgz, cfa, cfz, cpq, cgo, w8,
    xs, xr, zs, zr, cs, cr, ts, tr, ss, sr, pvs, pvr, es, er, blk, cnt,
    in_sem, x_ss, x_rs, z_ss, z_rs, c_ss, c_rs, t_ss, t_rs, s_ss, s_rs, pv_ss, pv_rs, e_ss, e_rs, met,
):
    g = lax.axis_index("growth")
    l = lax.axis_index("lateral")
    has_lo, has_hi = g > 0, g < NG - 1
    has_xl, has_xr = l > 0, l < NL - 1
    g_lo, g_hi = jnp.maximum(g - 1, 0), jnp.minimum(g + 1, NG - 1)
    l_lo, l_hi = jnp.maximum(l - 1, 0), jnp.minimum(l + 1, NL - 1)
    others = [lax.rem(g + d, NG) for d in (2, 3, 1)]

    barrier = pltpu.get_barrier_semaphore()

    def greet(cond, dev):
        @pl.when(cond)
        def _():
            pl.semaphore_signal(barrier, inc=1, device_id=dev, device_id_type=MESH)

    diag = [
        (has_lo & has_xl, (g_lo, l_lo)),
        (has_lo & has_xr, (g_lo, l_hi)),
        (has_hi & has_xl, (g_hi, l_lo)),
        (has_hi & has_xr, (g_hi, l_hi)),
    ]
    ends = jnp.logical_not(has_lo & has_hi)
    greet(has_lo, (g_lo, l))
    greet(has_hi, (g_hi, l))
    greet(has_xl, (g, l_lo))
    greet(has_xr, (g, l_hi))
    greet(ends, (NG - 1 - g, l))

    ins = [
        pltpu.make_async_copy(phase, ph.at[pl.ds(1, CZ), pl.ds(PAD, CX), :], in_sem.at[0]),
        pltpu.make_async_copy(old, po, in_sem.at[1]),
        pltpu.make_async_copy(solute, so.at[:, pl.ds(PAD, CX), :], in_sem.at[2]),
        pltpu.make_async_copy(blocks, blk, in_sem.at[3]),
        pltpu.make_async_copy(count, cnt, in_sem.at[4]),
    ]
    for c in ins:
        c.start()

    lane = lax.broadcasted_iota(jnp.int32, (CX, NY), 1)
    row = lax.broadcasted_iota(jnp.int32, (CX, NY), 0)
    first, last = lane == 0, lane == NY - 1
    inner = (row > 0) & (row < CX - 1)
    zero = jnp.zeros((CX, NY), F32)
    one = zero + 1.0
    EXT = 40
    lane_e = lax.broadcasted_iota(jnp.int32, (EXT, NY), 1)
    first_e, last_e = lane_e == 0, lane_e == NY - 1

    def face(a, b):
        return 220.0 - 90.0 * (a + b)

    def coupling(a, b):
        return 0.055 - 0.0225 * (a + b)

    def ydiff(a):
        return next_y(a, last) - prev_y(a, first)

    def phz(z, off=0):
        return ph[z + 1, pl.ds(PAD + off, CX), :]

    def soz(z, off=0):
        return so[z, pl.ds(PAD + off, CX), :]

    for c in ins:
        c.wait()

    live = [jnp.where(s < cnt[0, 0], blk[0, 0, s], -1) for s in range(6)]

    def masked(k):
        hit = k == live[0]
        for b in live[1:]:
            hit = hit | (k == b)
        return jnp.where(hit, 0.25, 0.0)

    column_mask = masked(row // BZ)
    sub = lax.broadcasted_iota(jnp.int32, (8, NY), 0)
    for side, x in ((0, 0), (1, CX - 1)):
        near = 1 if x == 0 else CX - 2
        here, s = ph[1:CZ + 1, PAD + x, :], so[:, PAD + x, :]
        xs[side, 0] = here
        xs[side, 1] = ph[1:CZ + 1, PAD + near, :]
        xs[side, 2] = s
        xs[side, 3] = (1.0 + 0.7 * s) * (here - po[:, x, :]) * column_mask
    for side, z in ((0, 0), (1, CZ - 1)):
        zs[side, 0] = phz(z)
        zs[side, 1] = phz(1 if z == 0 else CZ - 2)
        zs[side, 2] = (1.0 + 0.7 * soz(z)) * (phz(z) - po[z]) * masked(jnp.int32(z // BZ))
        for right, x in ((0, 0), (1, CX - 1)):
            cs[2 * side + right] = phz(z)[x:x + 1]

    def many(*conds):
        return sum(c.astype(jnp.int32) for c in conds)

    pl.semaphore_wait(barrier, many(has_lo, has_hi, has_xl, has_xr, ends))

    def remote(src, dst, ss, rs, dev):
        return pltpu.make_async_remote_copy(
            src_ref=src, dst_ref=dst, send_sem=ss, recv_sem=rs, device_id=dev, device_id_type=MESH
        )

    x_out = [
        (has_xl, remote(xs.at[0], xr.at[1], x_ss.at[0], x_rs.at[1], (g, l_lo))),
        (has_xr, remote(xs.at[1], xr.at[0], x_ss.at[1], x_rs.at[0], (g, l_hi))),
    ]
    z_out = [
        (has_lo, remote(zs.at[0, 0:3], zr.at[1, 0:3], z_ss.at[0], z_rs.at[1], (g_lo, l))),
        (has_hi, remote(zs.at[1, 0:3], zr.at[0, 0:3], z_ss.at[1], z_rs.at[0], (g_hi, l))),
    ]
    w_out = [
        (has_lo, remote(zs.at[0, 3], zr.at[1, 3], z_ss.at[2], z_rs.at[3], (g_lo, l))),
        (has_hi, remote(zs.at[1, 3], zr.at[0, 3], z_ss.at[3], z_rs.at[2], (g_hi, l))),
    ]
    w_in = [
        (has_lo, remote(zs.at[1, 3], zr.at[0, 3], z_ss.at[3], z_rs.at[2], (g_lo, l))),
        (has_hi, remote(zs.at[0, 3], zr.at[1, 3], z_ss.at[2], z_rs.at[3], (g_hi, l))),
    ]
    c_out = [
        (cond, remote(cs.at[i], cr.at[3 - i], c_ss.at[i], c_rs.at[3 - i], dev))
        for i, (cond, dev) in enumerate(diag)
    ]
    for i, (cond, o) in enumerate(((has_lo, g_lo), (has_hi, g_hi))):
        @pl.when(cond)
        def _():
            pl.semaphore_signal(met, inc=1, device_id=(o, l), device_id_type=MESH)
    for cond, cp in z_out + x_out:
        pl.when(cond)(cp.start)
    x_in = [
        (has_xl, remote(xs.at[1], xr.at[0], x_ss.at[1], x_rs.at[0], (g, l_lo))),
        (has_xr, remote(xs.at[0], xr.at[1], x_ss.at[0], x_rs.at[1], (g, l_hi))),
    ]
    z_in = [
        (has_lo, remote(zs.at[1, 0:3], zr.at[0, 0:3], z_ss.at[1], z_rs.at[0], (g_lo, l))),
        (has_hi, remote(zs.at[0, 0:3], zr.at[1, 0:3], z_ss.at[0], z_rs.at[1], (g_hi, l))),
    ]
    c_in = [
        (cond, remote(cs.at[3 - i], cr.at[i], c_ss.at[3 - i], c_rs.at[i], dev))
        for i, (cond, dev) in enumerate(diag)
    ]

    middle = has_lo & has_hi
    up = g >= NG // 2
    half = up.astype(jnp.int32)
    inner_dev, outer_dev = 1 + half, 3 * half
    far_inner, far_outer = 2 - half, 3 - 3 * half
    beside = [(has_lo, g_lo), (has_hi, g_hi)]
    t_out = [
        (middle & cond, remote(ts, tr.at[g], t_ss.at[i], t_rs.at[g], (o, l)))
        for i, (cond, o) in enumerate(beside)
    ]
    t_far_out = [(middle, remote(ts, tr.at[g], t_ss.at[2], t_rs.at[g], (far_outer, l)))]
    t_in = [
        (cond & (o > 0) & (o < NG - 1), remote(ts, tr.at[o], t_ss.at[0], t_rs.at[o], (o, l)))
        for cond, o in beside
    ]
    t_in.append(
        (ends, remote(ts, tr.at[far_inner], t_ss.at[0], t_rs.at[far_inner], (far_inner, l)))
    )
    s_out, pv_out, e_out = [], [], []
    for d, o in enumerate(others):
        to_end = middle & (o == outer_dev)
        to_far = middle & (o != outer_dev)
        for cond, at in ((to_end, pl.ds(0, 1)), (to_far, pl.ds(1, 1))):
            s_out.append((cond, remote(ss.at[at], sr.at[g, at], s_ss.at[d], s_rs.at[g], (o, l))))
        for cond, at in ((to_end, pl.ds(0, 2)), (jnp.logical_not(to_end), pl.ds(2, 1))):
            pv_out.append((cond, remote(pvs.at[at], pvr.at[g, at], pv_ss.at[d], pv_rs.at[g], (o, l))))
            e_out.append((cond, remote(es.at[at], er.at[g, at], e_ss.at[d], e_rs.at[g], (o, l))))
    s_in, pv_in, e_in = [], [], []
    for k in range(NG):
        from_inner = ends & (inner_dev == k)
        from_other = (g != k) & jnp.logical_not(from_inner)
        if k in (1, 2):
            for cond, at in ((from_inner, pl.ds(0, 1)), (from_other, pl.ds(1, 1))):
                s_in.append((cond, remote(ss.at[at], sr.at[k, at], s_ss.at[0], s_rs.at[k], (k, l))))
        for cond, at in ((from_inner, pl.ds(0, 2)), (from_other, pl.ds(2, 1))):
            pv_in.append((cond, remote(pvs.at[at], pvr.at[k, at], pv_ss.at[0], pv_rs.at[k], (k, l))))
            e_in.append((cond, remote(es.at[at], er.at[k, at], e_ss.at[0], e_rs.at[k], (k, l))))

    bottom = jnp.where(g == 0, face(phz(0), 0.0), zero) + 1.0
    top = jnp.where(g == NG - 1, face(phz(CZ - 1), 0.0), zero) + 1.0
    ea[0] = bottom
    pf[0] = one
    eb[CZ - 1] = top
    qf[CZ - 1] = one

    def eliminate(i, carry):
        e, prod, ebar, qprod = carry
        j = CZ - 1 - i
        u = face(phz(i), phz(i + 1))
        v = face(phz(j), phz(j - 1))
        w = u / (u + e)
        y = v / (v + ebar)
        e = 1.0 + w * e
        ebar = 1.0 + y * ebar
        prod = prod * w
        qprod = qprod * y
        wf[i] = w
        vb[j] = y
        ea[i + 1] = e
        eb[j - 1] = ebar
        pf[i + 1] = prod
        qf[j - 1] = qprod
        return e, prod, ebar, qprod

    def eliminate3(k, carry):
        for r in range(3):
            carry = eliminate(1 + 3 * k + r, carry)
        return carry

    lax.fori_loop(0, 10, eliminate3, eliminate(0, (bottom, one, top, one)))

    def finish(k, _):
        for r in range(BZ):
            i = k * BZ + r
            d = 1.0 / (ea[i] + eb[i] - 1.0)
            dd[i] = d
            pp[i] = pf[i] * d
            qq[i] = qf[i] * d
        return 0

    lax.fori_loop(0, CZ // BZ, finish, 0)
    zs[0, 3] = pp[0]
    zs[1, 3] = qq[CZ - 1]
    ts[...] = pp[CZ - 1]
    tr[g] = ts[...]
    for cond, cp in w_out:
        pl.when(cond)(cp.start)
    pl.semaphore_wait(met, many(has_lo, has_hi))
    for cond, cp in c_out:
        pl.when(cond)(cp.start)


    for side, x in ((0, -1), (1, CX)):
        ph[0:CZ, PAD + x, :] = zero
        ph[CZ:CZ + 2, PAD + x, :] = zero[0:2]
        fx[:, PAD + x, :] = zero
        so[:, PAD + x, :] = xs[side, 2]
        for buf in (cin, cnx, cout, cs0):
            buf[side, 0:8] = zero[0:8]
            buf[side, 40:56] = zero[0:16]
        @pl.when(jnp.logical_not((has_xl, has_xr)[side]))
        def _():
            xr[side] = jnp.zeros((4, CZ, NY), F32)
        @pl.when(jnp.logical_not((has_lo, has_hi)[side]))
        def _():
            zr[side] = jnp.zeros((4, CX, NY), F32)
    for i, (cond, _) in enumerate(diag):
        @pl.when(jnp.logical_not(cond))
        def _():
            cr[i] = jnp.zeros((1, NY), F32)

    def prefactor(k, _):
        mask = masked(k)
        for r in range(BZ):
            z = k * BZ + r
            s0[z] = (1.0 + 0.7 * soz(z)) * (phz(z) - po[z]) * mask
        return 0

    lax.fori_loop(0, CZ // BZ, prefactor, 0)

    def plane(z):
        here = phz(z)
        right, left = phz(z, 1), phz(z, -1)
        yn, yp = next_y(here, last), prev_y(here, first)
        gx = right - left
        gy = yn - yp
        gz = phz(z + 1) - phz(z - 1)
        factor = flux_factor(gx, gy, gz, jnp.where(inner, s0[z], 0.0))
        fx[z, pl.ds(PAD, CX), :] = factor * gx
        fz[z + 1] = factor * gz
        flux_y = factor * gy
        s = soz(z)
        side = coupling(here, right) * (soz(z, 1) - s) + coupling(here, left) * (soz(z, -1) - s)
        step_y = coupling(here, yn) * (next_y(s, last) - s)
        back = jnp.where(first, coupling(here, 0.0) * s, pltpu.roll(step_y + flux_y, 1, 1))
        rh[z] = s + side + (step_y + next_y(flux_y, last) - back)

    def gather_rhs(z, sums):
        r = (
            rh[z]
            + (fx[z, pl.ds(PAD + 1, CX), :] - fx[z, pl.ds(PAD - 1, CX), :])
            + (fz[z + 2] - fz[z])
        )
        rh[z] = r
        return sums[0] + pp[z] * r, sums[1] + qq[z] * r

    def planes(k, _):
        for r in range(6):
            plane(1 + 6 * k + r)
        return 0

    lax.fori_loop(0, 5, planes, 0)
    for cond, cp in t_out + t_far_out:
        pl.when(cond)(cp.start)

    def rows(k, sums):
        for r in range(BZ):
            sums = gather_rhs(2 + BZ * k + r, sums)
        return sums

    sums = lax.fori_loop(0, 7, rows, (zero, zero))

    for side, x in ((0, 0), (1, CX - 1)):
        near = 1 if x == 0 else CX - 2
        cin[side, 8:40] = xs[side, 0]
        cnx[side, 8:40] = xs[side, 1]
        cs0[side, 8:40] = xs[side, 3]
        cpq[side, 0] = pp[:, x, :]
        cpq[side, 1] = qq[:, x, :]
        cpq[side, 2] = pp[:, near, :]
        cpq[side, 3] = qq[:, near, :]

    for cond, cp in z_in + w_in:
        pl.when(cond)(cp.wait_recv)
    self_hi = 1.0 / face(phz(CZ - 1), zr[1, 0]) + qq[CZ - 1] + zr[1, 3]
    self_lo = 1.0 / face(phz(0), zr[0, 0]) + pp[0] + zr[0, 3]
    even = lax.rem(g, 2) == 0
    self_out = jnp.where(even, self_hi, self_lo)
    ss[0] = jnp.where(even, self_lo, self_hi)
    ss[1] = self_out
    sr[g] = ss[...]
    for cond, cp in s_out:
        pl.when(cond)(cp.start)
    own_k = ts[...] / self_out
    ph[0, pl.ds(PAD, CX), :] = zr[0, 0]
    ph[CZ + 1, pl.ds(PAD, CX), :] = zr[1, 0]
    for side, z in ((0, -1), (1, CZ)):
        gz = phz(0) - zr[side, 1] if side == 0 else zr[side, 1] - phz(CZ - 1)
        gx = phz(z, 1) - phz(z, -1)
        factor = flux_factor(gx, ydiff(zr[side, 0]), gz, jnp.where(inner, zr[side, 2], 0.0))
        fz[z + 1] = factor * gz
    plane(0)
    plane(CZ - 1)
    for z in (0, 1, CZ - 2, CZ - 1):
        sums = gather_rhs(z, sums)
    facing, away = jnp.where(up, sums[0], sums[1]), jnp.where(up, sums[1], sums[0])
    pvs[0] = facing
    pvs[1] = away
    pvs[2] = jnp.where(middle, facing - own_k * away, facing)
    pvr[g] = pvs[...]
    for cond, cp in pv_out:
        pl.when(cond)(cp.start)

    for side, x in ((0, 0), (1, CX - 1)):
        near = 1 if x == 0 else CX - 2
        for buf, which, xx in ((cin, 0, x), (cnx, 0, near)):
            buf[side, 7:8] = zr[0, which, xx:xx + 1, :]
            buf[side, 40:41] = zr[1, which, xx:xx + 1, :]
        cin[side, 6:7] = zr[0, 1, x:x + 1, :]
        cin[side, 41:42] = zr[1, 1, x:x + 1, :]
        a = cin[side, 7:47]
        cgy[side] = next_y(a, last_e) - prev_y(a, first_e)
        cgz[side] = cin[side, 8:48] - cin[side, 6:46]

    for side, x in ((0, 0), (1, CX - 1)):
        for end, z in ((0, 0), (1, CZ - 1)):
            at_a, at_b = 4 * side + end, 4 * side + 2 + end
            zb = 7 if end == 0 else 40
            w8[0, at_b:at_b + 1] = cnx[side, zb:zb + 1]
            w8[1, at_b:at_b + 1] = cgz[side, zb - 7:zb - 6]
            w8[2, at_b:at_b + 1] = cgy[side, zb - 7:zb - 6]
            w8[3, at_b:at_b + 1] = zr[end, 2, x:x + 1, :] * (-1.0 if end == 0 else 1.0)
            for at in (at_a, at_b):
                w8[4, at:at + 1] = cpq[side, 0, z:z + 1]
                w8[5, at:at + 1] = cpq[side, 1, z:z + 1]

    for cond, cp in x_in:
        pl.when(cond)(cp.wait_recv)
    tile_p = jnp.zeros((8, NY), F32)
    tile_q = jnp.zeros((8, NY), F32)
    for side, x in ((0, 0), (1, CX - 1)):
        near = 1 if x == 0 else CX - 2
        outer = xr[side, 0]
        cout[side, 8:40] = outer
        gin = cnx[side, 7:47] - cout[side, 7:47]
        factor = flux_factor(gin, cgy[side], cgz[side], cs0[side, 7:47])
        cfa[side] = factor
        cfz[side] = factor * cgz[side]
        g_out2 = xs[side, 0] - xr[side, 1]
        gy_out = ydiff(outer)
        f_out = flux_factor(
            g_out2, gy_out, cout[side, 9:41] - cout[side, 7:39], xr[side, 3]
        ) * jnp.where(inner, g_out2, 0.0)
        own = cfa[side, 1:33]
        d_near = -own * (xs[side, 1] - outer)
        d_edge = (
            coupling(xs[side, 0], outer) * (xr[side, 2] - xs[side, 2])
            - f_out
            + ydiff(own * cgy[side, 1:33])
            + (cfz[side, 2:34] - cfz[side, 0:32])
        )
        at, at_near = (0, 1) if side == 0 else (7, 6)
        for d, where, k in ((d_edge, at, 0), (d_near, at_near, 2)):
            tile_p = jnp.where(sub == where, jnp.sum(cpq[side, k] * d, axis=0, keepdims=True), tile_p)
            tile_q = jnp.where(sub == where, jnp.sum(cpq[side, k + 1] * d, axis=0, keepdims=True), tile_q)
        cfa[side, 0:32] = d_edge
        cfz[side, 0:32] = d_near
        cgo[side, 0] = g_out2
        cgo[side, 1] = gy_out
        for end, z in ((0, 0), (1, CZ - 1)):
            at_a, at_b = 4 * side + end, 4 * side + 2 + end
            inz = 1 if end == 0 else CZ - 2
            w8[0, at_a:at_a + 1] = xr[side, 0, inz:inz + 1, :]
            w8[1, at_a:at_a + 1] = cgo[side, 0, z:z + 1]
            w8[2, at_a:at_a + 1] = cgo[side, 1, z:z + 1]
            w8[3, at_a:at_a + 1] = -xr[side, 3, z:z + 1, :]
    carry2 = w8[1] * w8[1]
    side2 = w8[2] * w8[2]
    known2 = carry2 + side2 + 1.0
    known4 = carry2 * carry2 + side2 * side2
    scale = w8[3] * w8[1]
    base8, weight_p, weight_q = w8[0], w8[4], w8[5]
    for cond, cp in c_in:
        pl.when(cond)(cp.wait_recv)
    lower, left_half = sub % 2 == 0, sub // 4 == 0
    corner = [jnp.broadcast_to(cr[i], (8, NY)) for i in range(4)]
    v = base8 - jnp.where(
        lower, jnp.where(left_half, corner[0], corner[1]), jnp.where(left_half, corner[2], corner[3])
    )
    v2 = v * v
    inv = lax.rsqrt(known2 + v2)
    inv2 = inv * inv
    d8 = scale * inv * (0.1 + 1.2 * (known4 + v2 * v2) * (inv2 * inv2))

    def corner_rows(y):
        y = y + pltpu.roll(y, 7, 0)
        y = y + pltpu.roll(y, 6, 0)
        return jnp.where(sub == 0, y, jnp.where(sub == 7, pltpu.roll(y, 3, 0), 0.0))

    tile_p = tile_p + corner_rows(weight_p * d8)
    tile_q = tile_q + corner_rows(weight_q * d8)
    left_rows = sub < 4
    tile_facing, tile_away = jnp.where(up, tile_p, tile_q), jnp.where(up, tile_q, tile_p)
    tile_k = jnp.where(left_rows, own_k[0:8], own_k[CX - 8:CX])
    es[0] = tile_facing
    es[1] = tile_away
    es[2] = jnp.where(middle, tile_facing - tile_k * tile_away, tile_facing)
    er[g] = es[...]
    for cond, cp in e_out:
        pl.when(cond)(cp.start)
    w8[0] = d8
    for side in (0, 1):
        for end, z in ((0, 0), (1, CZ - 1)):
            at_a, at_b = 4 * side + end, 4 * side + 2 + end
            cfa[side, z:z + 1] = cfa[side, z:z + 1] + w8[0, at_a:at_a + 1] + w8[0, at_b:at_b + 1]
    for side, x in ((0, 0), (1, CX - 1)):
        near = 1 if x == 0 else CX - 2
        rh[:, x, :] = rh[:, x, :] + cfa[side, 0:32]
        rh[:, near, :] = rh[:, near, :] + cfz[side, 0:32]

    ee[0] = rh[0]
    bb[CZ - 1] = rh[CZ - 1]

    def sweep(i, carry):
        f, b = carry
        j = CZ - 1 - i
        f = rh[i] + wf[i - 1] * f
        b = rh[j] + vb[j + 1] * b
        ee[i] = f
        bb[j] = b
        return f, b

    def sweep3(k, carry):
        for r in range(3):
            carry = sweep(2 + 3 * k + r, carry)
        return carry

    lax.fori_loop(0, 10, sweep3, sweep(1, (rh[0], rh[CZ - 1])))

    def local(k, _):
        for r in range(BZ):
            z = k * BZ + r
            ee[z] = (ee[z] + bb[z] - rh[z]) * dd[z]
        return 0

    lax.fori_loop(0, CZ // BZ, local, 0)

    for cond, cp in t_in + s_in + pv_in:
        pl.when(cond)(cp.wait_recv)
    t_far = tr[far_inner]
    t_own = tr[inner_dev]
    k1 = t_far / sr[far_inner, 1]
    m1 = 1.0 / (sr[inner_dev, 0] - t_far * k1)
    k2 = t_own * m1
    m2 = 1.0 / (ss[1] - t_own * k2)
    b1 = pvr[far_inner, 2] + k1 * pvr[far_outer, 2] - pvr[inner_dev, 0]
    b2 = pvr[inner_dev, 1] - pvr[outer_dev, 2]
    tile_k1 = jnp.where(left_rows, k1[0:8], k1[CX - 8:CX])
    for cond, cp in x_out + z_out + c_out + w_out + t_out + t_far_out + s_out + pv_out + e_out:
        pl.when(cond)(cp.wait_send)
    for cond, cp in e_in:
        pl.when(cond)(cp.wait_recv)

    def widen(tile):
        full = jnp.concatenate([tile, jnp.zeros((CX - 16, NY), F32), tile], axis=0)
        return jnp.where((row < 2) | (row >= CX - 2), full, 0.0)

    b1 = b1 + widen(er[far_inner, 2] + tile_k1 * er[far_outer, 2] - er[inner_dev, 0])
    b2 = b2 + widen(er[inner_dev, 1] - er[outer_dev, 2])
    r2 = (b2 + k2 * b1) * m2
    r1 = (b1 + t_own * r2) * m1
    below = jnp.where(g == 3, r2, jnp.where(g == 2, r1, jnp.where(g == 1, -r2, 0.0)))
    above = jnp.where(g == 0, -r2, jnp.where(g == 1, -r1, jnp.where(g == 2, r2, 0.0)))

    below_out[...] = below
    above_out[...] = above


def step(phase, old, solute, blocks, count):
    def buf(*shape):
        return pltpu.VMEM(shape + (NY,), F32)

    slab = buf(CZ, CX)
    dma = pltpu.SemaphoreType.DMA
    parts = pl.pallas_call(
        kernel,
        out_shape=[pltpu.VMEM((CZ, CX, NY), F32)] * 3 + [pltpu.VMEM((CX, NY), F32)] * 2,
        in_specs=[pl.BlockSpec(memory_space=pl.ANY)] * 5,
        out_specs=[pl.BlockSpec(memory_space=pltpu.VMEM)] * 5,
        scratch_shapes=[
            buf(CZ + 2, ROW), buf(CZ, ROW), slab, slab, buf(CZ, ROW), buf(CZ + 2, CX),
            slab, slab, slab, slab, slab, slab, slab, slab, slab,
            buf(2, 56), buf(2, 56), buf(2, 56), buf(2, 56),
            buf(2, 40), buf(2, 40), buf(2, 40), buf(2, 40), buf(2, 4, CZ),
            buf(2, 2, CZ), buf(6, 8),
            buf(2, 4, CZ), buf(2, 4, CZ),
            buf(2, 4, CX), buf(2, 4, CX),
            buf(4, 1), buf(4, 1),
            buf(CX), buf(NG, CX),
            buf(2, CX), buf(NG, 2, CX),
            buf(3, CX), buf(NG, 3, CX),
            buf(3, 8), buf(NG, 3, 8),
            pltpu.SMEM((1, 1, 6), jnp.int32),
            pltpu.SMEM((1, 1), jnp.int32),
            dma((5,)),
            dma((2,)), dma((2,)),
            dma((4,)), dma((4,)),
            dma((4,)), dma((4,)),
            dma((3,)), dma((NG,)),
            dma((3,)), dma((NG,)),
            dma((3,)), dma((NG,)),
            dma((3,)), dma((NG,)),
            pltpu.SemaphoreType.REGULAR,
        ],
        compiler_params=pltpu.CompilerParams(
            collective_id=0, has_side_effects=True, vmem_limit_bytes=65400000
        ),
    )(phase, old, solute, blocks, count)
    chunks = 4
    deep = CZ // chunks

    def close(ee, pp, qq, below, above, dst, stage, sems):
        lo, hi = below[...], above[...]
        cps = []
        for c in range(chunks):
            for z in range(c * deep, (c + 1) * deep):
                stage[z] = ee[z] + pp[z] * lo - qq[z] * hi
            at = pl.ds(c * deep, deep)
            cps.append(pltpu.make_async_copy(stage.at[at], dst.at[at], sems.at[c]))
            cps[-1].start()
        for cp in cps:
            cp.wait()

    return pl.pallas_call(
        close,
        out_shape=jax.ShapeDtypeStruct((CZ, CX, NY), F32),
        in_specs=[pl.BlockSpec(memory_space=pltpu.VMEM)] * 5,
        out_specs=pl.BlockSpec(memory_space=pl.ANY),
        scratch_shapes=[slab, dma((chunks,))],
        compiler_params=pltpu.CompilerParams(vmem_limit_bytes=4194304),
    )(*[pltpu.with_memory_space_constraint(a, pltpu.VMEM) for a in parts])


def solution(mesh):
    spec = P("growth", "lateral", None)
    return jax.shard_map(
        step,
        mesh=mesh,
        in_specs=(spec, spec, spec, spec, P("growth", "lateral")),
        out_specs=spec,
        check_vma=False,
    )
```
